32 devices in a mesh: layer: 2 (over x), row: 16 (over z, y, core).
Axes of the slice: x: 2, y: 2, z: 4, core: 2. Of those that a mesh axis runs over, the one named last changes fastest.
Arguments:
- left_factors: bfloat16 [2, 16384, 128], P('layer', 'row'), may hold values from -0.375 to 0.375
- right_factors: bfloat16 [2, 16384, 128], P('layer', 'row'), may hold values from -0.1875 to 0.1875
- sketch: bfloat16 [16384, 128], P('row'), may hold values from -0.1875 to 0.1875
- row_basis: bfloat16 [16384, 128], P('row'), may hold values from -0.4375 to 0.4375
- inverse_diag: bfloat16 [16384, 1024], P('row'), may hold values from -0.0625 to 1.44125, as said below
- right_side: bfloat16 [16384, 1024], P('row', 'layer'), may hold values from -6 to 6
- incoming: float32 [128, 1024], P(None, 'layer'), may hold values from -6 to 6
Outputs:
- solution: bfloat16 [16384, 1024], P('row', 'layer')
The draws below stay inside these ranges and needn't reach their ends.
Inputs may be any that keep to these rules, and one draw needn't show every extreme that they name: `inverse_diag`: each block of 1024 rows is the inverse of that row group's diagonal tile.
All inputs are finite; a program needn't handle non-finite values.
Results may differ from the reference program's by a relative error of at most 0.0095.
Values may be sent and summed in bfloat16 or wider, within the bound.
No kernel may reach another device: no remote copies, remote signals or barrier semaphores. Data moves between devices by JAX's collectives and lax.ppermute only.
A program may use at most 128 MiB of HBM per device.

```python
import math
import jax
import jax.numpy as jnp
from jax import lax

B = 1024
R = 128
LAYERS = 2
ROWS = 16384
COLS = 1024


def draw_inverse_diag(key, part):
    first, second = jax.random.split(jax.random.fold_in(key, 11))
    rows = lax.broadcasted_iota(jnp.int32, (ROWS, B), 0) % B
    cols = lax.broadcasted_iota(jnp.int32, (ROWS, B), 1)
    identity = (rows == cols).astype(jnp.float32)
    scale_diag = jax.random.uniform(first, (ROWS, 1), jnp.float32, 0.8, 1.2)
    spread = jnp.clip(jax.random.normal(second, (ROWS, B), jnp.float32), -4.0, 4.0) * (0.5 / math.sqrt(B))
    return (identity * scale_diag + spread).astype(jnp.bfloat16)


def steps_of(stream_key, extent, cuts, low, largest):
    factor_of = 1.0
    for axis_at, shards_of in cuts:
        steps = jax.random.uniform(jax.random.fold_in(jax.random.fold_in(stream_key, 6), axis_at), (shards_of,), jnp.float32, low / len(cuts), largest / len(cuts))
        factor_of = factor_of * jnp.repeat(jnp.exp(steps), extent[axis_at] // shards_of).reshape((-1,) + (1,) * (len(extent) - 1 - axis_at))
    return factor_of


def centred(rng, dims, scale, reach, shards=(), dtype=jnp.bfloat16):
    values = jax.random.normal(rng, dims, jnp.float32) * scale
    if len(shards) > 0:
        values = steps_of(rng, dims, shards, -0.22, 0.18) * values
    return jnp.clip(values, min=-reach, max=reach).astype(dtype)


def setup_inputs(seed: int = 0) -> dict:
    key_list = jax.random.split(jax.random.key(seed), 8)
    return {
        "left_factors": centred(key_list[0], (LAYERS, ROWS, R), (R * LAYERS) ** -0.5, 0.375, ((0, 2), (1, 16))),
        "right_factors": centred(key_list[1], (LAYERS, ROWS, R), B ** -0.5, 0.1875, ((0, 2), (1, 16))),
        "sketch": centred(key_list[2], (ROWS, R), B ** -0.5, 0.1875, ((0, 16),)),
        "row_basis": centred(key_list[3], (ROWS, R), (R + R // 3) ** -0.5, 0.4375, ((0, 16),)),
        "inverse_diag": draw_inverse_diag(jax.random.fold_in(key_list[7], 71), 0),
        "right_side": centred(key_list[5], (ROWS, COLS), 1.0, 6.0, ((0, 16), (1, 2))),
        "incoming": centred(key_list[6], (R, COLS), 1.0, 6.0, ((1, 2),), jnp.float32),
    }


def reference(left_factors, right_factors, sketch, row_basis, inverse_diag, right_side, incoming):
    groups = ROWS // B
    full = lax.Precision.HIGHEST
    coupled = incoming.astype(jnp.float32)
    pieces = []
    for group in range(groups):
        lo = group * B
        hi = lo + B
        total = jnp.zeros((B, R), jnp.float32)
        for layer in range(LAYERS):
            core = jnp.dot(right_factors[layer, lo:hi].T, sketch[lo:hi], preferred_element_type=jnp.float32).astype(jnp.bfloat16)
            total = total - jnp.dot(left_factors[layer, lo:hi], core, preferred_element_type=jnp.float32)
        tile_range = total.astype(jnp.bfloat16)
        applied = jnp.dot(inverse_diag[lo:hi], right_side[lo:hi], preferred_element_type=jnp.float32).astype(jnp.bfloat16)
        gain = jnp.dot(inverse_diag[lo:hi], tile_range, preferred_element_type=jnp.float32).astype(jnp.bfloat16)
        result = applied.astype(jnp.float32) - jnp.dot(gain.astype(jnp.float32), coupled, precision=full)
        pieces.append(result.astype(jnp.bfloat16))
        if group + 1 < groups:
            basis = row_basis[hi:hi + B]
            step_map = -jnp.dot(basis.T, gain, preferred_element_type=jnp.float32)
            step_shift = jnp.dot(basis.T, applied, preferred_element_type=jnp.float32)
            coupled = jnp.dot(step_map, coupled, precision=full) + step_shift
    return jnp.concatenate(pieces, axis=0)
```

```python
import jax
import jax.numpy as jnp
from jax import lax
from jax.sharding import PartitionSpec as P


def shifted(value, axis, steps):
    count = lax.axis_size(axis)
    leading, last = (max(0, -steps), min(count, count - steps))
    return lax.ppermute(value, axis, [(source, source + steps) for source in range(leading, last)])


def rotated(value, axis, steps):
    count = lax.axis_size(axis)
    return lax.ppermute(value, axis, [(source, (source + steps) % count) for source in range(count)])


def project(basis, vectors):
    return lax.dot_general(
        basis, vectors, (((0,), (0,)), ((), ())), preferred_element_type=jnp.float32
    )


def product(a, b):
    return jnp.dot(a, b, preferred_element_type=jnp.float32)


def body(left_factors, right_factors, sketch, row_basis, inverse_diag, right_side, incoming):
    half = jnp.bfloat16
    rank = sketch.shape[1]
    layers, groups = lax.axis_size("layer"), lax.axis_size("row")
    here = lax.axis_index("row")

    lefts = [left_factors[0]] + [rotated(left_factors[0], "layer", k) for k in range(1, layers)]
    next_rows = shifted(row_basis, "row", -1)
    core = project(right_factors[0], sketch).astype(half)
    cores = [core] + [rotated(core, "layer", k) for k in range(1, layers)]
    applied = product(inverse_diag, right_side).astype(half)
    tile_range = -sum(product(left, core) for left, core in zip(lefts, cores))
    gain = product(inverse_diag, tile_range.astype(half)).astype(half)
    step_map = -project(next_rows, gain)
    step_shift = project(next_rows, applied)

    step = jnp.concatenate([step_map, step_shift], axis=1).astype(half)
    begin = jnp.concatenate([jnp.zeros_like(step_map), incoming], axis=1).astype(half)

    def combine(later, earlier):
        moved = product(later[:, :rank], earlier)
        return moved + jnp.pad(later[:, rank:].astype(jnp.float32), ((0, 0), (rank, 0)))

    first = jnp.where(here == 0, begin, shifted(step, "row", 1))
    second = jnp.where(here == 1, begin, shifted(step, "row", 2))
    prefix = combine(first, second)
    span = 2
    while span < groups:
        sent = prefix.astype(half)
        if span * 2 >= groups:
            arrived = shifted(sent[:, rank:], "row", span)
            coupled = product(sent[:, :rank], arrived) + prefix[:, rank:]
        else:
            arrived = shifted(sent, "row", span)
            prefix = product(sent[:, :rank], arrived) + jnp.pad(prefix[:, rank:], ((0, 0), (rank, 0)))
        span *= 2
    result = applied.astype(jnp.float32) - product(gain, coupled.astype(half))
    return result.astype(half)


def solution(mesh):
    return jax.shard_map(
        body,
        mesh=mesh,
        in_specs=(
            P("layer", "row", None),
            P("layer", "row", None),
            P("row", None),
            P("row", None),
            P("row", None),
            P("row", "layer"),
            P(None, "layer"),
        ),
        out_specs=P("row", "layer"),
        check_vma=False,
    )
```

```python
import jax
import jax.numpy as jnp
from jax import lax
from jax.experimental import pallas as pl
from jax.experimental.pallas import tpu as pltpu
from jax.sharding import PartitionSpec as P


def shifted(value, axis, steps):
    count = lax.axis_size(axis)
    leading, last = (max(0, -steps), min(count, count - steps))
    return lax.ppermute(value, axis, [(source, source + steps) for source in range(leading, last)])


def rotated(value, axis, steps):
    count = lax.axis_size(axis)
    return lax.ppermute(value, axis, [(source, (source + steps) % count) for source in range(count)])


def project(basis, vectors):
    return lax.dot_general(
        basis, vectors, (((0,), (0,)), ((), ())), preferred_element_type=jnp.float32
    )


def product(a, b):
    return jnp.dot(a, b, preferred_element_type=jnp.float32)


def recurrence(maps_ref, shifts_ref, incoming_ref, coupled_ref):
    groups, width, _ = shifts_ref.shape
    state = incoming_ref[...]
    for group in range(groups):
        high = state.astype(jnp.bfloat16)
        coupled_ref[group] = high
        if group + 1 < groups:
            low = (state - high.astype(jnp.float32)).astype(jnp.bfloat16)
            both = product(jnp.concatenate([high, low], axis=0), maps_ref[group])
            state = both[:width] + both[width:] + shifts_ref[group].astype(jnp.float32)


def exchanged(blocks):
    return lax.all_to_all(blocks, "row", 0, 0, tiled=True)


def body(left_factors, right_factors, sketch, row_basis, inverse_diag, right_side, incoming):
    half = jnp.bfloat16
    rank = sketch.shape[1]
    width = right_side.shape[1]
    layers, groups = lax.axis_size("layer"), lax.axis_size("row")
    here = lax.axis_index("row")
    share = width // groups

    lefts = [left_factors[0]] + [rotated(left_factors[0], "layer", k) for k in range(1, layers)]
    next_rows = shifted(row_basis, "row", -1)
    core = project(right_factors[0], sketch).astype(half)
    cores = [core] + [rotated(core, "layer", k) for k in range(1, layers)]
    applied = product(inverse_diag, right_side).astype(half)

    shift_t = project(applied, next_rows).astype(half)
    shifts = exchanged(shift_t.reshape(groups, share, rank))
    begin = lax.dynamic_slice_in_dim(incoming, here * share, share, 1).T

    tile_range = -sum(product(left, core) for left, core in zip(lefts, cores))
    gain = product(inverse_diag, tile_range.astype(half)).astype(half)
    map_t = (-project(gain, next_rows)).astype(half)
    maps = exchanged(jnp.broadcast_to(map_t[None], (groups, rank, rank)))
    coupled = pl.pallas_call(
        recurrence,
        out_shape=jax.ShapeDtypeStruct((groups, share, rank), half),
        name="recurrence",
    )(maps, shifts, begin)
    coupled_t = exchanged(coupled).reshape(width, rank)
    moved = lax.dot_general(
        gain, coupled_t, (((1,), (1,)), ((), ())), preferred_element_type=jnp.float32
    )
    return (applied.astype(jnp.float32) - moved).astype(half)


def solution(mesh):
    return jax.shard_map(
        body,
        mesh=mesh,
        in_specs=(
            P("layer", "row", None),
            P("layer", "row", None),
            P("row", None),
            P("row", None),
            P("row", None),
            P("row", "layer"),
            P(None, "layer"),
        ),
        out_specs=P("row", "layer"),
        check_vma=False,
    )
```

```python
import jax
import jax.numpy as jnp
from jax import lax
from jax.experimental import pallas as pl
from jax.experimental.pallas import tpu as pltpu
from jax.sharding import PartitionSpec as P


def shifted(value, axis, steps):
    count = lax.axis_size(axis)
    leading, last = (max(0, -steps), min(count, count - steps))
    return lax.ppermute(value, axis, [(source, source + steps) for source in range(leading, last)])


def rotated(value, axis, steps):
    count = lax.axis_size(axis)
    return lax.ppermute(value, axis, [(source, (source + steps) % count) for source in range(count)])


def project(basis, vectors):
    return lax.dot_general(
        basis, vectors, (((0,), (0,)), ((), ())), preferred_element_type=jnp.float32
    )


def product(a, b):
    return jnp.dot(a, b, preferred_element_type=jnp.float32)


def compose(maps_ref, shifts_ref, begin_ref, total_ref, prefixes_ref):
    count = maps_ref.shape[0]
    rank = maps_ref.shape[1]
    state = begin_ref[...]
    for member in range(count):
        prefixes_ref[member] = state
        moved = product(state.astype(jnp.bfloat16), maps_ref[member])
        state = jnp.concatenate(
            [moved[:rank], moved[rank:] + shifts_ref[member].astype(jnp.float32)], axis=0
        )
    total = state.astype(jnp.bfloat16)
    for target in range(total_ref.shape[0]):
        total_ref[target] = total


def enter(upper_ref, totals_ref, prefixes_ref, coupled_ref):
    rank = totals_ref.shape[2]
    upper = upper_ref[0]
    state = jnp.zeros(coupled_ref.shape[1:], jnp.float32)
    for source in range(totals_ref.shape[0] - 1):
        moved = product(state.astype(jnp.bfloat16), totals_ref[source, :rank])
        moved = moved + totals_ref[source, rank:].astype(jnp.float32)
        state = jnp.where(source < upper, moved, state)
    state = state.astype(jnp.bfloat16)
    for member in range(coupled_ref.shape[0]):
        moved = product(state, prefixes_ref[member, :rank].astype(jnp.bfloat16))
        coupled_ref[member] = (moved + prefixes_ref[member, rank:]).astype(jnp.bfloat16)


def exchanged(blocks, members):
    return lax.all_to_all(blocks, "row", 0, 0, axis_index_groups=members, tiled=True)


def body(left_factors, right_factors, sketch, row_basis, inverse_diag, right_side, incoming):
    half = jnp.bfloat16
    rank = sketch.shape[1]
    width = right_side.shape[1]
    layers, groups = lax.axis_size("layer"), lax.axis_size("row")
    lowers = 1
    while lowers * lowers < groups:
        lowers *= 2
    uppers = groups // lowers
    here = lax.axis_index("row")
    upper, lower = here // lowers, here % lowers
    share = width // lowers
    near = [[u * lowers + l for l in range(lowers)] for u in range(uppers)]
    far = [[u * lowers + l for u in range(uppers)] for l in range(lowers)]

    lefts = [left_factors[0]] + [rotated(left_factors[0], "layer", k) for k in range(1, layers)]
    next_rows = shifted(row_basis, "row", -1)
    core = project(right_factors[0], sketch).astype(half)
    cores = [core] + [rotated(core, "layer", k) for k in range(1, layers)]
    applied = product(inverse_diag, right_side).astype(half)

    shift_t = project(applied, next_rows).astype(half)
    shifts = exchanged(shift_t.reshape(lowers, share, rank), near)
    entry = lax.dynamic_slice_in_dim(incoming, lower * share, share, 1).T
    begin = jnp.concatenate(
        [
            jnp.where(upper == 0, 0.0, jnp.eye(rank, dtype=jnp.float32)),
            jnp.where(upper == 0, entry, 0.0),
        ]
    )

    tile_range = -sum(product(left, core) for left, core in zip(lefts, cores))
    gain = product(inverse_diag, tile_range.astype(half)).astype(half)
    map_t = (-project(gain, next_rows)).astype(half)
    maps = exchanged(jnp.broadcast_to(map_t[None], (lowers, rank, rank)), near)
    total, prefixes = pl.pallas_call(
        compose,
        out_shape=(
            jax.ShapeDtypeStruct((uppers, rank + share, rank), half),
            jax.ShapeDtypeStruct((lowers, rank + share, rank), jnp.float32),
        ),
        name="compose",
    )(maps, shifts, begin)
    totals = exchanged(total, far)
    coupled = pl.pallas_call(
        enter,
        in_specs=[pl.BlockSpec(memory_space=pltpu.SMEM)] + [pl.BlockSpec(memory_space=pltpu.VMEM)] * 2,
        out_shape=jax.ShapeDtypeStruct((lowers, share, rank), half),
        name="enter",
    )(upper.reshape(1), totals, prefixes)
    coupled_t = exchanged(coupled, near).reshape(width, rank)
    moved = lax.dot_general(
        gain, coupled_t, (((1,), (1,)), ((), ())), preferred_element_type=jnp.float32
    )
    return (applied.astype(jnp.float32) - moved).astype(half)


def solution(mesh):
    return jax.shard_map(
        body,
        mesh=mesh,
        in_specs=(
            P("layer", "row", None),
            P("layer", "row", None),
            P("row", None),
            P("row", None),
            P("row", None),
            P("row", "layer"),
            P(None, "layer"),
        ),
        out_specs=P("row", "layer"),
        check_vma=False,
    )
```

```python
import jax
import jax.numpy as jnp
from jax import lax
from jax.experimental import pallas as pl
from jax.experimental.pallas import tpu as pltpu
from jax.sharding import PartitionSpec as P


def shifted(value, axis, steps):
    count = lax.axis_size(axis)
    leading, last = (max(0, -steps), min(count, count - steps))
    return lax.ppermute(value, axis, [(source, source + steps) for source in range(leading, last)])


def rotated(value, axis, steps):
    count = lax.axis_size(axis)
    return lax.ppermute(value, axis, [(source, (source + steps) % count) for source in range(count)])


def project(basis, vectors):
    return lax.dot_general(
        basis, vectors, (((0,), (0,)), ((), ())), preferred_element_type=jnp.float32
    )


def product(a, b):
    return jnp.dot(a, b, preferred_element_type=jnp.float32)


VMEM = pl.BlockSpec(memory_space=pltpu.VMEM)
SMEM = pl.BlockSpec(memory_space=pltpu.SMEM)
FLIPPED = (((1,), (1,)), ((), ()))


def make_maps(layers, *refs):
    lefts, cores = refs[:layers], refs[layers : 2 * layers]
    inverse_ref, next_ref, gain_ref, maps_ref = refs[2 * layers :]
    tile_range = product(lefts[0][...], cores[0][...])
    for left, core in zip(lefts[1:], cores[1:]):
        tile_range += product(left[...], core[...])
    gain = product(inverse_ref[...], (-tile_range).astype(jnp.bfloat16)).astype(jnp.bfloat16)
    gain_ref[...] = gain
    map_t = (-project(gain, next_ref[...])).astype(jnp.bfloat16)
    for target in range(maps_ref.shape[0]):
        maps_ref[target] = map_t


def compose(place_ref, maps_ref, shifts_ref, entry_ref, own_ref, sent_ref):
    count, rank, _ = maps_ref.shape
    share = entry_ref.shape[0]
    upper, lower = place_ref[0], place_ref[1]
    rows = lax.broadcasted_iota(jnp.int32, (rank, rank), 0)
    cols = lax.broadcasted_iota(jnp.int32, (rank, rank), 1)
    identity = jnp.where(rows == cols, 1.0, 0.0).astype(jnp.float32)
    before = jnp.where(upper == 0, entry_ref[...], 0.0)
    state = jnp.concatenate([identity, before], axis=0)
    own = identity
    for member in range(count):
        reached = (upper > 0) & (lower == member)
        own = jnp.where(reached, state[:rank], own)
        value = state[rank:].astype(jnp.bfloat16)
        sent_ref[member] = value
        sent_ref[count + member] = value
        moved = product(state.astype(jnp.bfloat16), maps_ref[member])
        state = jnp.concatenate(
            [moved[:rank], moved[rank:] + shifts_ref[member].astype(jnp.float32)], axis=0
        )
    own_ref[...] = own.astype(jnp.bfloat16)

    @pl.when(upper == 0)
    def _():
        value = state[rank:].astype(jnp.bfloat16)
        for member in range(count):
            sent_ref[count + member] = value


def solve(place_ref, parts_ref, own_ref, gain_ref, applied_ref, result_ref, coupled_ref):
    @pl.when(pl.program_id(0) == 0)
    def _():
        count = parts_ref.shape[0] // 2
        shape = coupled_ref.shape
        moved = product(parts_ref[:count].reshape(shape), own_ref[...])
        rest = parts_ref[count:].reshape(shape).astype(jnp.float32)
        coupled = moved + jnp.where(place_ref[0] == 0, 0.0, rest)
        coupled_ref[...] = coupled.astype(jnp.bfloat16)

    moved = lax.dot_general(
        gain_ref[...], coupled_ref[...], FLIPPED, preferred_element_type=jnp.float32
    )
    result_ref[...] = (applied_ref[...].astype(jnp.float32) - moved).astype(jnp.bfloat16)


def exchanged(blocks, members=None):
    return lax.all_to_all(blocks, "row", 0, 0, axis_index_groups=members, tiled=True)


def body(left_factors, right_factors, sketch, row_basis, inverse_diag, right_side, incoming):
    half = jnp.bfloat16
    order, rank = sketch.shape
    width = right_side.shape[1]
    layers, groups = lax.axis_size("layer"), lax.axis_size("row")
    lowers = groups // 2
    here = lax.axis_index("row")
    place = jnp.stack([here // lowers, here % lowers])
    share = width // lowers
    near = [list(range(lowers)), list(range(lowers, groups))]

    lefts = [left_factors[0]] + [rotated(left_factors[0], "layer", k) for k in range(1, layers)]
    next_rows = shifted(row_basis, "row", -1)
    applied = product(inverse_diag, right_side).astype(half)
    sketch, applied = lax.optimization_barrier((sketch, applied))
    core = project(right_factors[0], sketch).astype(half)
    cores = [core] + [rotated(core, "layer", k) for k in range(1, layers)]

    shift_t = project(applied, next_rows).astype(half)
    shifts = exchanged(shift_t.reshape(lowers, share, rank), near)
    entry = lax.dynamic_slice_in_dim(incoming, place[1] * share, share, 1).T
    lefts[-1], shifts, entry = lax.optimization_barrier((lefts[-1], shifts, entry))

    gain, maps = pl.pallas_call(
        lambda *refs: make_maps(layers, *refs),
        in_specs=[VMEM] * (2 * layers + 2),
        out_specs=[VMEM] * 2,
        out_shape=(
            jax.ShapeDtypeStruct((order, rank), half),
            jax.ShapeDtypeStruct((lowers, rank, rank), half),
        ),
        name="make_maps",
    )(*lefts, *cores, inverse_diag, next_rows)
    maps = exchanged(maps, near)
    own, sent = pl.pallas_call(
        compose,
        in_specs=[SMEM] + [VMEM] * 3,
        out_specs=[VMEM] * 2,
        out_shape=(
            jax.ShapeDtypeStruct((rank, rank), half),
            jax.ShapeDtypeStruct((groups, share, rank), half),
        ),
        name="compose",
    )(place, maps, shifts, entry)

    parts = exchanged(sent)
    tile = order // 4
    return pl.pallas_call(
        solve,
        grid=(4,),
        in_specs=[
            SMEM,
            pl.BlockSpec((groups, share, rank), lambda i: (0, 0, 0)),
            pl.BlockSpec((rank, rank), lambda i: (0, 0)),
            pl.BlockSpec((tile, rank), lambda i: (i, 0)),
            pl.BlockSpec((tile, width), lambda i: (i, 0)),
        ],
        out_specs=pl.BlockSpec((tile, width), lambda i: (i, 0)),
        out_shape=jax.ShapeDtypeStruct((order, width), half),
        scratch_shapes=[pltpu.VMEM((width, rank), half)],
        name="solve",
    )(place, parts, own, gain, applied)


def solution(mesh):
    return jax.shard_map(
        body,
        mesh=mesh,
        in_specs=(
            P("layer", "row", None),
            P("layer", "row", None),
            P("row", None),
            P("row", None),
            P("row", None),
            P("row", "layer"),
            P(None, "layer"),
        ),
        out_specs=P("row", "layer"),
        check_vma=False,
    )
```

```python
import jax
import jax.numpy as jnp
from jax import lax
from jax.experimental import pallas as pl
from jax.experimental.pallas import tpu as pltpu
from jax.sharding import PartitionSpec as P


def shifted(value, axis, steps):
    count = lax.axis_size(axis)
    leading, last = (max(0, -steps), min(count, count - steps))
    return lax.ppermute(value, axis, [(source, source + steps) for source in range(leading, last)])


def rotated(value, axis, steps):
    count = lax.axis_size(axis)
    return lax.ppermute(value, axis, [(source, (source + steps) % count) for source in range(count)])


def project(basis, vectors):
    return lax.dot_general(
        basis, vectors, (((0,), (0,)), ((), ())), preferred_element_type=jnp.float32
    )


def product(a, b):
    return jnp.dot(a, b, preferred_element_type=jnp.float32)


VMEM = pl.BlockSpec(memory_space=pltpu.VMEM)
SMEM = pl.BlockSpec(memory_space=pltpu.SMEM)
FLIPPED = (((1,), (1,)), ((), ()))


def make_maps(layers, *refs):
    lefts, cores = refs[:layers], refs[layers : 2 * layers]
    weights_ref, shift_ref, tile_range_ref, sent_ref = refs[2 * layers :]
    total = product(lefts[0][...], cores[0][...])
    for left, core in zip(lefts[1:], cores[1:]):
        total += product(left[...], core[...])
    tile_range = (-total).astype(jnp.bfloat16)
    tile_range_ref[...] = tile_range
    rank = tile_range.shape[1]
    parts = product(weights_ref[...], tile_range)
    map_t = (-(parts[:rank] + parts[rank:])).T.astype(jnp.bfloat16)
    for target in range(sent_ref.shape[0]):
        sent_ref[target, :rank] = map_t
        sent_ref[target, rank:] = shift_ref[target]


def compose(place_ref, steps_ref, entry_ref, own_ref, sent_ref):
    count, _, rank = steps_ref.shape
    share = entry_ref.shape[0]
    upper, lower = place_ref[0], place_ref[1]
    rows = lax.broadcasted_iota(jnp.int32, (rank, rank), 0)
    cols = lax.broadcasted_iota(jnp.int32, (rank, rank), 1)
    identity = jnp.where(rows == cols, 1.0, 0.0).astype(jnp.float32)
    before = jnp.where(upper == 0, entry_ref[...], 0.0)
    state = jnp.concatenate([identity, before], axis=0)
    own = identity
    for member in range(count):
        reached = (upper > 0) & (lower == member)
        own = jnp.where(reached, state[:rank], own)
        value = state[rank:].astype(jnp.bfloat16)
        sent_ref[member] = value
        sent_ref[count + member] = value
        moved = product(state.astype(jnp.bfloat16), steps_ref[member, :rank])
        state = jnp.concatenate(
            [moved[:rank], moved[rank:] + steps_ref[member, rank:].astype(jnp.float32)], axis=0
        )
    own_ref[...] = own.astype(jnp.bfloat16)

    @pl.when(upper == 0)
    def _():
        value = state[rank:].astype(jnp.bfloat16)
        for member in range(count):
            sent_ref[count + member] = value


def exchanged(blocks, members=None):
    return lax.all_to_all(blocks, "row", 0, 0, axis_index_groups=members, tiled=True)


def body(left_factors, right_factors, sketch, row_basis, inverse_diag, right_side, incoming):
    half = jnp.bfloat16
    order, rank = sketch.shape
    width = right_side.shape[1]
    layers, groups = lax.axis_size("layer"), lax.axis_size("row")
    lowers = groups // 2
    here = lax.axis_index("row")
    place = jnp.stack([lax.div(here, lowers), lax.rem(here, lowers)])
    share = width // lowers
    near = [list(range(lowers)), list(range(lowers, groups))]

    lefts = [left_factors[0]] + [rotated(left_factors[0], "layer", k) for k in range(1, layers)]
    next_rows = shifted(row_basis, "row", -1)
    applied = product(inverse_diag, right_side).astype(half)
    sketch, applied = lax.optimization_barrier((sketch, applied))
    core = project(right_factors[0], sketch).astype(half)
    cores = [core] + [rotated(core, "layer", k) for k in range(1, layers)]

    shift_t = project(applied, next_rows).astype(half).reshape(lowers, share, rank)
    entry = lax.dynamic_slice_in_dim(incoming, place[1] * share, share, 1).T
    weights = project(next_rows, inverse_diag)
    high = weights.astype(half)
    low = (weights - high.astype(jnp.float32)).astype(half)
    weights = jnp.concatenate([high, low])
    lefts[-1], shift_t, weights, entry, place = lax.optimization_barrier(
        (lefts[-1], shift_t, weights, entry, place)
    )

    tile_range, sent = pl.pallas_call(
        lambda *refs: make_maps(layers, *refs),
        in_specs=[VMEM] * (2 * layers + 2),
        out_specs=[VMEM] * 2,
        out_shape=(
            jax.ShapeDtypeStruct((order, rank), half),
            jax.ShapeDtypeStruct((lowers, rank + share, rank), half),
        ),
        name="make_maps",
    )(*lefts, *cores, weights, shift_t)
    steps = exchanged(sent, near)
    gain = product(inverse_diag, tile_range).astype(half)
    gain, steps = lax.optimization_barrier((gain, steps))
    own, sent = pl.pallas_call(
        compose,
        in_specs=[SMEM] + [VMEM] * 2,
        out_specs=[VMEM] * 2,
        out_shape=(
            jax.ShapeDtypeStruct((rank, rank), half),
            jax.ShapeDtypeStruct((groups, share, rank), half),
        ),
        name="compose",
    )(place, steps, entry)

    parts = exchanged(sent)
    rest = parts[lowers:].reshape(width, rank).astype(jnp.float32)
    coupled = product(parts[:lowers].reshape(width, rank), own)
    coupled = (coupled + jnp.where(place[0] == 0, 0.0, rest)).astype(half)
    moved = lax.dot_general(gain, coupled, FLIPPED, preferred_element_type=jnp.float32)
    return (applied.astype(jnp.float32) - moved).astype(half)


def solution(mesh):
    return jax.shard_map(
        body,
        mesh=mesh,
        in_specs=(
            P("layer", "row", None),
            P("layer", "row", None),
            P("row", None),
            P("row", None),
            P("row", None),
            P("row", "layer"),
            P(None, "layer"),
        ),
        out_specs=P("row", "layer"),
        check_vma=False,
    )
```

```python
import jax
import jax.numpy as jnp
from jax import lax
from jax.sharding import PartitionSpec as P


def shifted(value, axis, steps):
    count = lax.axis_size(axis)
    leading, last = (max(0, -steps), min(count, count - steps))
    return lax.ppermute(value, axis, [(source, source + steps) for source in range(leading, last)])


def rotated(value, axis, steps):
    count = lax.axis_size(axis)
    return lax.ppermute(value, axis, [(source, (source + steps) % count) for source in range(count)])


def project(basis, vectors):
    return lax.dot_general(
        basis, vectors, (((0,), (0,)), ((), ())), preferred_element_type=jnp.float32
    )


def product(a, b):
    return jnp.dot(a, b, preferred_element_type=jnp.float32)


FLIPPED = (((1,), (1,)), ((), ()))


def exchanged(blocks, members):
    return lax.all_to_all(blocks, "row", 0, 0, axis_index_groups=members, tiled=True)


def body(left_factors, right_factors, sketch, row_basis, inverse_diag, right_side, incoming):
    half = jnp.bfloat16
    rank = sketch.shape[1]
    width = right_side.shape[1]
    layers, groups = lax.axis_size("layer"), lax.axis_size("row")
    lowers = groups // 2
    here = lax.axis_index("row")
    upper, lower = lax.div(here, lowers), lax.rem(here, lowers)
    share = width // lowers
    near = [list(range(lowers)), list(range(lowers, groups))]

    lefts = [left_factors[0]] + [rotated(left_factors[0], "layer", k) for k in range(1, layers)]
    next_rows = shifted(row_basis, "row", -1)
    applied = product(inverse_diag, right_side).astype(half)
    sketch, applied = lax.optimization_barrier((sketch, applied))
    core = project(right_factors[0], sketch).astype(half)
    cores = [core] + [rotated(core, "layer", k) for k in range(1, layers)]

    shift_t = project(applied, next_rows).astype(half).reshape(lowers, share, rank)
    weights = project(next_rows, inverse_diag)
    high = weights.astype(half)
    low = (weights - high.astype(jnp.float32)).astype(half)
    partial_range = product(lefts[0], cores[0])
    lefts[-1], shift_t, high, low, partial_range = lax.optimization_barrier(
        (lefts[-1], shift_t, high, low, partial_range)
    )
    for left, core in zip(lefts[1:], cores[1:]):
        partial_range += product(left, core)
    tile_range = (-partial_range).astype(half)
    flip = (((0,), (1,)), ((), ()))
    map_t = lax.dot_general(tile_range, high, flip, preferred_element_type=jnp.float32)
    map_t += lax.dot_general(tile_range, low, flip, preferred_element_type=jnp.float32)
    map_t = (-map_t).astype(half)
    sent = jnp.concatenate([jnp.broadcast_to(map_t, (lowers, rank, rank)), shift_t], axis=1)
    steps = exchanged(sent, near)
    gain = product(inverse_diag, tile_range).astype(half)
    gain, steps = lax.optimization_barrier((gain, steps))

    entry = lax.dynamic_slice_in_dim(incoming, lower * share, share, 1).T
    entry = jnp.where(upper == 0, entry, 0.0).astype(half)
    state = jnp.concatenate([jnp.eye(rank, dtype=half), entry])
    is_shift = lax.broadcasted_iota(jnp.int32, state.shape, 0) >= rank
    states = []
    for member in range(lowers):
        states.append(state)
        moved = product(state, steps[member, :rank])
        state = (moved + jnp.where(is_shift, steps[member], 0).astype(jnp.float32)).astype(half)
    entered = shifted(state[rank:], "row", lowers)
    states = jnp.stack(states)
    coupled = lax.dot_general(
        jnp.broadcast_to(entered, (lowers, share, rank)),
        states[:, :rank],
        (((2,), (1,)), ((0,), (0,))),
        preferred_element_type=jnp.float32,
    )
    coupled = (coupled + states[:, rank:].astype(jnp.float32)).astype(half)
    coupled = exchanged(coupled, near).reshape(width, rank)
    moved = lax.dot_general(gain, coupled, FLIPPED, preferred_element_type=jnp.float32)
    return (applied.astype(jnp.float32) - moved).astype(half)


def solution(mesh):
    return jax.shard_map(
        body,
        mesh=mesh,
        in_specs=(
            P("layer", "row", None),
            P("layer", "row", None),
            P("row", None),
            P("row", None),
            P("row", None),
            P("row", "layer"),
            P(None, "layer"),
        ),
        out_specs=P("row", "layer"),
        check_vma=False,
    )
```

```python
import jax
import jax.numpy as jnp
from jax import lax
from jax.experimental import pallas as pl
from jax.experimental.pallas import tpu as pltpu
from jax.sharding import PartitionSpec as P


def shifted(value, axis, steps):
    count = lax.axis_size(axis)
    leading, last = (max(0, -steps), min(count, count - steps))
    return lax.ppermute(value, axis, [(source, source + steps) for source in range(leading, last)])


def rotated(value, axis, steps):
    count = lax.axis_size(axis)
    return lax.ppermute(value, axis, [(source, (source + steps) % count) for source in range(count)])


def project(basis, vectors):
    return lax.dot_general(
        basis, vectors, (((0,), (0,)), ((), ())), preferred_element_type=jnp.float32
    )


def product(a, b):
    return jnp.dot(a, b, preferred_element_type=jnp.float32)


VMEM = pl.BlockSpec(memory_space=pltpu.VMEM)
FLIPPED = (((1,), (1,)), ((), ()))


def split(value):
    high = value.astype(jnp.bfloat16)
    return high, (value - high.astype(jnp.float32)).astype(jnp.bfloat16)


def wide(value, matrix):
    both = product(jnp.concatenate(split(value)), matrix)
    return both[: value.shape[0]] + both[value.shape[0] :]


def make_maps(layers, *refs):
    lefts = jnp.concatenate([ref[...] for ref in refs[:layers]], axis=1)
    cores = jnp.concatenate([ref[...] for ref in refs[layers : 2 * layers]], axis=0)
    weights_ref, shift_ref, sent_ref = refs[2 * layers :]
    map_t = wide(wide(weights_ref[...], lefts), cores).T.astype(jnp.bfloat16)
    rank = map_t.shape[0]
    for target in range(sent_ref.shape[0]):
        sent_ref[target, :rank] = map_t
        sent_ref[target, rank:] = shift_ref[target]


def compose_values(steps_ref, entry_ref, values_ref, last_ref):
    count, _, rank = steps_ref.shape
    state = entry_ref[...]
    for member in range(count):
        values_ref[member] = state
        state = wide(state, steps_ref[member, :rank])
        state = state + steps_ref[member, rank:].astype(jnp.float32)
    last_ref[...] = state.astype(jnp.bfloat16)


def compose_maps(steps_ref, maps_ref):
    count, rank, _ = maps_ref.shape
    state = steps_ref[0, :rank]
    for member in range(1, count):
        maps_ref[member] = state
        if member + 1 < count:
            state = product(state, steps_ref[member, :rank]).astype(jnp.bfloat16)


def enter(entered_ref, maps_ref, values_ref, coupled_ref):
    entered = entered_ref[...]
    coupled_ref[0] = (entered.astype(jnp.float32) + values_ref[0]).astype(jnp.bfloat16)
    for member in range(1, coupled_ref.shape[0]):
        moved = product(entered, maps_ref[member])
        coupled_ref[member] = (moved + values_ref[member]).astype(jnp.bfloat16)


def local(kernel, inputs, *outputs):
    return pl.pallas_call(
        kernel,
        in_specs=[VMEM] * len(inputs),
        out_specs=[VMEM] * len(outputs),
        out_shape=[jax.ShapeDtypeStruct(*output) for output in outputs],
    )(*inputs)


def exchanged(blocks, members):
    return lax.all_to_all(blocks, "row", 0, 0, axis_index_groups=members, tiled=True)


def body(left_factors, right_factors, sketch, row_basis, inverse_diag, right_side, incoming):
    half = jnp.bfloat16
    rank = sketch.shape[1]
    width = right_side.shape[1]
    layers, groups = lax.axis_size("layer"), lax.axis_size("row")
    lowers = groups // 2
    here = lax.axis_index("row")
    upper, lower = lax.div(here, lowers), lax.rem(here, lowers)
    share = width // lowers
    near = [list(range(lowers)), list(range(lowers, groups))]

    lefts = [left_factors[0]] + [rotated(left_factors[0], "layer", k) for k in range(1, layers)]
    next_rows = shifted(row_basis, "row", -1)
    applied = product(inverse_diag, right_side).astype(half)
    sketch, applied = lax.optimization_barrier((sketch, applied))
    core = project(right_factors[0], sketch).astype(half)
    cores = [core] + [rotated(core, "layer", k) for k in range(1, layers)]

    shift_t = project(applied, next_rows).astype(half).reshape(lowers, share, rank)
    weights = project(next_rows, inverse_diag)
    lefts[-1], shift_t, weights = lax.optimization_barrier((lefts[-1], shift_t, weights))
    (sent,) = local(
        lambda *refs: make_maps(layers, *refs),
        (*lefts, *cores, weights, shift_t),
        ((lowers, rank + share, rank), half),
    )
    lefts, incoming, sent = lax.optimization_barrier((lefts, incoming, sent))
    steps = exchanged(sent, near)
    entry = lax.dynamic_slice_in_dim(incoming, lower * share, share, 1).T
    entry = jnp.where(upper == 0, entry, 0.0)
    tile_range = -sum(product(left, core) for left, core in zip(lefts, cores))
    gain = product(inverse_diag, tile_range.astype(half)).astype(half)
    gain, entry, steps = lax.optimization_barrier((gain, entry, steps))

    values, last = local(
        compose_values,
        (steps, entry),
        ((lowers, share, rank), jnp.float32),
        ((share, rank), half),
    )
    entered = shifted(last, "row", lowers)
    steps, _ = lax.optimization_barrier((steps, last))
    (maps,) = local(compose_maps, (steps,), ((lowers, rank, rank), half))
    (coupled,) = local(enter, (entered, maps, values), ((lowers, share, rank), half))
    coupled = exchanged(coupled, near).reshape(width, rank)
    moved = lax.dot_general(gain, coupled, FLIPPED, preferred_element_type=jnp.float32)
    return (applied.astype(jnp.float32) - moved).astype(half)


def solution(mesh):
    return jax.shard_map(
        body,
        mesh=mesh,
        in_specs=(
            P("layer", "row", None),
            P("layer", "row", None),
            P("row", None),
            P("row", None),
            P("row", None),
            P("row", "layer"),
            P(None, "layer"),
        ),
        out_specs=P("row", "layer"),
        check_vma=False,
    )
```

```python
import jax
import jax.numpy as jnp
from jax import lax
from jax.experimental import pallas as pl
from jax.experimental.pallas import tpu as pltpu
from jax.sharding import PartitionSpec as P


def shifted(value, axis, steps):
    count = lax.axis_size(axis)
    leading, last = (max(0, -steps), min(count, count - steps))
    return lax.ppermute(value, axis, [(source, source + steps) for source in range(leading, last)])


def rotated(value, axis, steps):
    count = lax.axis_size(axis)
    return lax.ppermute(value, axis, [(source, (source + steps) % count) for source in range(count)])


def project(basis, vectors):
    return lax.dot_general(
        basis, vectors, (((0,), (0,)), ((), ())), preferred_element_type=jnp.float32
    )


def product(a, b):
    return jnp.dot(a, b, preferred_element_type=jnp.float32)


VMEM = pl.BlockSpec(memory_space=pltpu.VMEM)
FLIPPED = (((1,), (1,)), ((), ()))


def split(value):
    high = value.astype(jnp.bfloat16)
    return high, (value - high.astype(jnp.float32)).astype(jnp.bfloat16)


def wide(value, matrix):
    both = product(jnp.concatenate(split(value)), matrix)
    return both[: value.shape[0]] + both[value.shape[0] :]


def make_maps(layers, *refs):
    lefts = jnp.concatenate([ref[...] for ref in refs[:layers]], axis=1)
    cores = jnp.concatenate([ref[...] for ref in refs[layers : 2 * layers]], axis=0)
    weights_ref, shift_ref, sent_ref = refs[2 * layers :]
    map_t = wide(wide(weights_ref[...], lefts), cores).T.astype(jnp.bfloat16)
    rank = map_t.shape[0]
    for target in range(sent_ref.shape[0]):
        sent_ref[target, :rank] = map_t
        sent_ref[target, rank:] = shift_ref[target]


def compose_values(steps_ref, entry_ref, values_ref, last_ref):
    count, _, rank = steps_ref.shape
    state = entry_ref[...].T
    for member in range(count):
        values_ref[member] = state
        state = wide(state, steps_ref[member, :rank])
        state = state + steps_ref[member, rank:].astype(jnp.float32)
    last_ref[...] = state.astype(jnp.bfloat16)


def compose_maps(steps_ref, maps_ref):
    count, rank, _ = maps_ref.shape
    state = steps_ref[0, :rank]
    for member in range(1, count):
        maps_ref[member] = state
        if member + 1 < count:
            state = product(state, steps_ref[member, :rank]).astype(jnp.bfloat16)


def enter(entered_ref, maps_ref, values_ref, coupled_ref):
    entered = entered_ref[...]
    coupled_ref[0] = (entered.astype(jnp.float32) + values_ref[0]).astype(jnp.bfloat16)
    for member in range(1, coupled_ref.shape[0]):
        moved = product(entered, maps_ref[member])
        coupled_ref[member] = (moved + values_ref[member]).astype(jnp.bfloat16)


def local(kernel, inputs, *outputs):
    return pl.pallas_call(
        kernel,
        in_specs=[VMEM] * len(inputs),
        out_specs=[VMEM] * len(outputs),
        out_shape=[jax.ShapeDtypeStruct(*output) for output in outputs],
        compiler_params=pltpu.CompilerParams(vmem_limit_bytes=16 * 2**20),
    )(*inputs)


def exchanged(blocks, members):
    return lax.all_to_all(blocks, "row", 0, 0, axis_index_groups=members, tiled=True)


def body(left_factors, right_factors, sketch, row_basis, inverse_diag, right_side, incoming):
    half = jnp.bfloat16
    rank = sketch.shape[1]
    width = right_side.shape[1]
    layers, groups = lax.axis_size("layer"), lax.axis_size("row")
    lowers = groups // 2
    here = lax.axis_index("row")
    upper, lower = lax.div(here, lowers), lax.rem(here, lowers)
    share = width // lowers
    near = [list(range(lowers)), list(range(lowers, groups))]

    lefts = [left_factors[0]] + [rotated(left_factors[0], "layer", k) for k in range(1, layers)]
    next_rows = shifted(row_basis, "row", -1)
    applied = product(inverse_diag, right_side).astype(half)
    sketch, applied = lax.optimization_barrier((sketch, applied))
    core = project(right_factors[0], sketch).astype(half)
    cores = [core] + [rotated(core, "layer", k) for k in range(1, layers)]

    shift_t = project(applied, next_rows).astype(half).reshape(lowers, share, rank)
    weights = project(next_rows, inverse_diag)
    lefts[-1], shift_t, weights = lax.optimization_barrier((lefts[-1], shift_t, weights))
    (sent,) = local(
        lambda *refs: make_maps(layers, *refs),
        (*lefts, *cores, weights, shift_t),
        ((lowers, rank + share, rank), half),
    )
    lefts, incoming, sent = lax.optimization_barrier((lefts, incoming, sent))
    steps = exchanged(sent, near)
    entry = lax.dynamic_slice_in_dim(incoming, lower * share, share, 1)
    entry = jnp.where(upper == 0, entry, 0.0)
    tile_range = -sum(product(left, core) for left, core in zip(lefts, cores))
    gain = product(inverse_diag, tile_range.astype(half)).astype(half)
    gain, entry, steps = lax.optimization_barrier((gain, entry, steps))

    values, last = local(
        compose_values,
        (steps, entry),
        ((lowers, share, rank), jnp.float32),
        ((share, rank), half),
    )
    entered = shifted(last, "row", lowers)
    steps, _ = lax.optimization_barrier((steps, last))
    (maps,) = local(compose_maps, (steps,), ((lowers, rank, rank), half))
    (coupled,) = local(enter, (entered, maps, values), ((lowers, share, rank), half))
    coupled = exchanged(coupled, near).reshape(width, rank)
    moved = lax.dot_general(gain, coupled, FLIPPED, preferred_element_type=jnp.float32)
    return (applied.astype(jnp.float32) - moved).astype(half)


def solution(mesh):
    return jax.shard_map(
        body,
        mesh=mesh,
        in_specs=(
            P("layer", "row", None),
            P("layer", "row", None),
            P("row", None),
            P("row", None),
            P("row", None),
            P("row", "layer"),
            P(None, "layer"),
        ),
        out_specs=P("row", "layer"),
        check_vma=False,
    )
```

```python
import jax
import jax.numpy as jnp
from jax import lax
from jax.experimental import pallas as pl
from jax.experimental.pallas import tpu as pltpu
from jax.sharding import PartitionSpec as P


def shifted(value, axis, steps):
    count = lax.axis_size(axis)
    leading, last = (max(0, -steps), min(count, count - steps))
    return lax.ppermute(value, axis, [(source, source + steps) for source in range(leading, last)])


def rotated(value, axis, steps):
    count = lax.axis_size(axis)
    return lax.ppermute(value, axis, [(source, (source + steps) % count) for source in range(count)])


def project(basis, vectors):
    return lax.dot_general(
        basis, vectors, (((0,), (0,)), ((), ())), preferred_element_type=jnp.float32
    )


def product(a, b):
    return jnp.dot(a, b, preferred_element_type=jnp.float32)


SMEM = pl.BlockSpec(memory_space=pltpu.SMEM)
VMEM = pl.BlockSpec(memory_space=pltpu.VMEM)
FLIPPED = (((1,), (1,)), ((), ()))


def split(value):
    high = value.astype(jnp.bfloat16)
    return high, (value - high.astype(jnp.float32)).astype(jnp.bfloat16)


def wide(value, matrix):
    both = product(jnp.concatenate(split(value)), matrix)
    return both[: value.shape[0]] + both[value.shape[0] :]


def make_maps(layers, *refs):
    lefts = jnp.concatenate([ref[...] for ref in refs[:layers]], axis=1)
    cores = jnp.concatenate([ref[...] for ref in refs[layers : 2 * layers]], axis=0)
    weights_ref, shift_ref, sent_ref = refs[2 * layers :]
    map_t = wide(wide(weights_ref[...], lefts), cores).T.astype(jnp.bfloat16)
    rank = map_t.shape[0]
    for target in range(sent_ref.shape[0]):
        sent_ref[target, :rank] = map_t
        sent_ref[target, rank:] = shift_ref[target]


def chain(steps_ref, state, values_ref):
    count, _, rank = steps_ref.shape
    for member in range(count):
        values_ref[member] = state
        state = wide(state, steps_ref[member, :rank])
        state = state + steps_ref[member, rank:].astype(jnp.float32)
    return state


def first_half(upper_ref, steps_ref, entry_ref, values_ref, last_ref):
    @pl.when(upper_ref[0] == 0)
    def _():
        last_ref[...] = chain(steps_ref, entry_ref[...].T, values_ref).astype(jnp.bfloat16)


def second_half(upper_ref, steps_ref, before_ref, values_ref, maps_ref):
    count, rank, _ = maps_ref.shape

    @pl.when(upper_ref[0] == 0)
    def _():
        maps_ref[...] = jnp.zeros(maps_ref.shape, jnp.bfloat16)

    @pl.when(upper_ref[0] > 0)
    def _():
        chain(steps_ref, jnp.zeros(values_ref.shape[1:], jnp.float32), values_ref)
        state = steps_ref[0, :rank]
        for member in range(1, count):
            maps_ref[member] = state
            if member + 1 < count:
                state = product(state, steps_ref[member, :rank]).astype(jnp.bfloat16)


def enter(entered_ref, maps_ref, values_ref, coupled_ref):
    entered = entered_ref[...]
    coupled_ref[0] = (entered.astype(jnp.float32) + values_ref[0]).astype(jnp.bfloat16)
    for member in range(1, coupled_ref.shape[0]):
        moved = product(entered, maps_ref[member])
        coupled_ref[member] = (moved + values_ref[member]).astype(jnp.bfloat16)


def local(kernel, inputs, *outputs, scalar=False, aliases={}):
    specs = [SMEM] * scalar + [VMEM] * (len(inputs) - scalar)
    return pl.pallas_call(
        kernel,
        in_specs=specs,
        out_specs=[VMEM] * len(outputs),
        out_shape=[jax.ShapeDtypeStruct(*output) for output in outputs],
        input_output_aliases=aliases,
        compiler_params=pltpu.CompilerParams(vmem_limit_bytes=16 * 2**20),
    )(*inputs)


def exchanged(blocks, members):
    return lax.all_to_all(blocks, "row", 0, 0, axis_index_groups=members, tiled=True)


def body(left_factors, right_factors, sketch, row_basis, inverse_diag, right_side, incoming):
    half = jnp.bfloat16
    rank = sketch.shape[1]
    width = right_side.shape[1]
    layers, groups = lax.axis_size("layer"), lax.axis_size("row")
    lowers = groups // 2
    here = lax.axis_index("row")
    upper, lower = lax.div(here, lowers), lax.rem(here, lowers)
    share = width // lowers
    near = [list(range(lowers)), list(range(lowers, groups))]

    lefts = [left_factors[0]] + [rotated(left_factors[0], "layer", k) for k in range(1, layers)]
    next_rows = shifted(row_basis, "row", -1)
    applied = product(inverse_diag, right_side).astype(half)
    sketch, applied = lax.optimization_barrier((sketch, applied))
    core = project(right_factors[0], sketch).astype(half)
    cores = [core] + [rotated(core, "layer", k) for k in range(1, layers)]

    shift_t = project(applied, next_rows).astype(half).reshape(lowers, share, rank)
    weights = project(next_rows, inverse_diag)
    lefts[-1], shift_t, weights = lax.optimization_barrier((lefts[-1], shift_t, weights))
    (sent,) = local(
        lambda *refs: make_maps(layers, *refs),
        (*lefts, *cores, weights, shift_t),
        ((lowers, rank + share, rank), half),
    )
    lefts, incoming, sent = lax.optimization_barrier((lefts, incoming, sent))
    steps = exchanged(sent, near)
    entry = lax.dynamic_slice_in_dim(incoming, lower * share, share, 1)
    tile_range = -sum(product(left, core) for left, core in zip(lefts, cores))
    gain = product(inverse_diag, tile_range.astype(half)).astype(half)
    gain, entry, steps = lax.optimization_barrier((gain, entry, steps))

    place = upper.reshape(1)
    values, last = local(
        first_half,
        (place, steps, entry),
        ((lowers, share, rank), jnp.float32),
        ((share, rank), half),
        scalar=True,
    )
    entered = shifted(last, "row", lowers)
    steps, _ = lax.optimization_barrier((steps, last))
    values, maps = local(
        second_half,
        (place, steps, values),
        ((lowers, share, rank), jnp.float32),
        ((lowers, rank, rank), half),
        scalar=True,
        aliases={2: 0},
    )
    (coupled,) = local(enter, (entered, maps, values), ((lowers, share, rank), half))
    coupled = exchanged(coupled, near).reshape(width, rank)
    moved = lax.dot_general(gain, coupled, FLIPPED, preferred_element_type=jnp.float32)
    return (applied.astype(jnp.float32) - moved).astype(half)


def solution(mesh):
    return jax.shard_map(
        body,
        mesh=mesh,
        in_specs=(
            P("layer", "row", None),
            P("layer", "row", None),
            P("row", None),
            P("row", None),
            P("row", None),
            P("row", "layer"),
            P(None, "layer"),
        ),
        out_specs=P("row", "layer"),
        check_vma=False,
    )
```

```python
import jax
import jax.numpy as jnp
from jax import lax
from jax.experimental import pallas as pl
from jax.experimental.pallas import tpu as pltpu
from jax.sharding import PartitionSpec as P


def shifted(value, axis, steps):
    count = lax.axis_size(axis)
    leading, last = (max(0, -steps), min(count, count - steps))
    return lax.ppermute(value, axis, [(source, source + steps) for source in range(leading, last)])


def rotated(value, axis, steps):
    count = lax.axis_size(axis)
    return lax.ppermute(value, axis, [(source, (source + steps) % count) for source in range(count)])


def project(basis, vectors):
    return lax.dot_general(
        basis, vectors, (((0,), (0,)), ((), ())), preferred_element_type=jnp.float32
    )


def product(a, b):
    return jnp.dot(a, b, preferred_element_type=jnp.float32)


SMEM = pl.BlockSpec(memory_space=pltpu.SMEM)
VMEM = pl.BlockSpec(memory_space=pltpu.VMEM)
FLIPPED = (((1,), (1,)), ((), ()))


def split(value):
    high = value.astype(jnp.bfloat16)
    return high, (value - high.astype(jnp.float32)).astype(jnp.bfloat16)


def wide(value, matrix):
    both = product(jnp.concatenate(split(value)), matrix)
    return both[: value.shape[0]] + both[value.shape[0] :]


def make_applied(inverse_ref, right_ref, applied_ref):
    rows = inverse_ref.shape[0] // 4

    def part(k, _):
        here = pl.ds(pl.multiple_of(k * rows, rows), rows)
        applied_ref[here, :] = product(inverse_ref[here, :], right_ref[...]).astype(jnp.bfloat16)
        return _

    lax.fori_loop(0, 4, part, 0)


def make_gain(layers, *refs):
    lefts = jnp.concatenate([ref[...] for ref in refs[:layers]], axis=1)
    cores = jnp.concatenate([ref[...] for ref in refs[layers : 2 * layers]], axis=0)
    inverse_ref, gain_ref = refs[2 * layers :]
    tile_range = (-product(lefts, cores)).astype(jnp.bfloat16)
    gain_ref[...] = product(inverse_ref[...], tile_range).astype(jnp.bfloat16)


def make_steps(gain_ref, applied_ref, next_ref, sent_ref):
    rank = gain_ref.shape[1]
    share = sent_ref.shape[1] - rank
    flipped = next_ref[...].T
    map_t = (-product(flipped, gain_ref[...])).T.astype(jnp.bfloat16)
    shift_t = product(flipped, applied_ref[...]).T.astype(jnp.bfloat16)
    for target in range(sent_ref.shape[0]):
        sent_ref[target, :rank] = map_t
        sent_ref[target, rank:] = shift_t[target * share : (target + 1) * share]


def chain(steps_ref, state, values_ref):
    count, _, rank = steps_ref.shape
    for member in range(count):
        values_ref[member] = state
        state = wide(state, steps_ref[member, :rank])
        state = state + steps_ref[member, rank:].astype(jnp.float32)
    return state


def first_half(upper_ref, steps_ref, entry_ref, values_ref, last_ref):
    @pl.when(upper_ref[0] == 0)
    def _():
        last_ref[...] = chain(steps_ref, entry_ref[...].T, values_ref).astype(jnp.bfloat16)


def second_half(upper_ref, steps_ref, before_ref, values_ref, maps_ref):
    count, rank, _ = maps_ref.shape

    @pl.when(upper_ref[0] == 0)
    def _():
        maps_ref[...] = jnp.zeros(maps_ref.shape, jnp.bfloat16)

    @pl.when(upper_ref[0] > 0)
    def _():
        chain(steps_ref, jnp.zeros(values_ref.shape[1:], jnp.float32), values_ref)
        state = steps_ref[0, :rank]
        for member in range(1, count):
            maps_ref[member] = state
            if member + 1 < count:
                state = product(state, steps_ref[member, :rank]).astype(jnp.bfloat16)


def enter(entered_ref, maps_ref, values_ref, coupled_ref):
    entered = entered_ref[...]
    coupled_ref[0] = (entered.astype(jnp.float32) + values_ref[0]).astype(jnp.bfloat16)
    for member in range(1, coupled_ref.shape[0]):
        moved = product(entered, maps_ref[member])
        coupled_ref[member] = (moved + values_ref[member]).astype(jnp.bfloat16)


def local(kernel, inputs, *outputs, scalar=False, aliases={}, cost=None):
    specs = [SMEM] * scalar + [VMEM] * (len(inputs) - scalar)
    return pl.pallas_call(
        kernel,
        in_specs=specs,
        out_specs=[VMEM] * len(outputs),
        out_shape=[jax.ShapeDtypeStruct(*output) for output in outputs],
        input_output_aliases=aliases,
        cost_estimate=cost,
        compiler_params=pltpu.CompilerParams(vmem_limit_bytes=16 * 2**20),
    )(*inputs)


def exchanged(blocks, members):
    return lax.all_to_all(blocks, "row", 0, 0, axis_index_groups=members, tiled=True)


def body(left_factors, right_factors, sketch, row_basis, inverse_diag, right_side, incoming):
    half = jnp.bfloat16
    order, rank = sketch.shape
    width = right_side.shape[1]
    layers, groups = lax.axis_size("layer"), lax.axis_size("row")
    lowers = groups // 2
    here = lax.axis_index("row")
    upper, lower = lax.div(here, lowers), lax.rem(here, lowers)
    share = width // lowers
    near = [list(range(lowers)), list(range(lowers, groups))]

    lefts = [left_factors[0]] + [rotated(left_factors[0], "layer", k) for k in range(1, layers)]
    next_rows = shifted(row_basis, "row", -1)
    core = project(right_factors[0], sketch).astype(half)
    right_side, core = lax.optimization_barrier((right_side, core))
    cores = [core] + [rotated(core, "layer", k) for k in range(1, layers)]
    (applied,) = local(
        make_applied,
        (inverse_diag, right_side),
        (right_side.shape, half),
        cost=pl.CostEstimate(flops=1, bytes_accessed=1, transcendentals=0),
    )
    lefts[-1], applied = lax.optimization_barrier((lefts[-1], applied))

    (gain,) = local(
        lambda *refs: make_gain(layers, *refs),
        (*lefts, *cores, inverse_diag),
        ((order, rank), half),
    )
    (sent,) = local(
        make_steps, (gain, applied, next_rows), ((lowers, rank + share, rank), half)
    )
    incoming, sent = lax.optimization_barrier((incoming, sent))
    steps = exchanged(sent, near)
    entry = lax.dynamic_slice_in_dim(incoming, lower * share, share, 1)

    place = upper.reshape(1)
    values, last = local(
        first_half,
        (place, steps, entry),
        ((lowers, share, rank), jnp.float32),
        ((share, rank), half),
        scalar=True,
    )
    entered = shifted(last, "row", lowers)
    steps, _ = lax.optimization_barrier((steps, last))
    values, maps = local(
        second_half,
        (place, steps, values),
        ((lowers, share, rank), jnp.float32),
        ((lowers, rank, rank), half),
        scalar=True,
        aliases={2: 0},
    )
    (coupled,) = local(enter, (entered, maps, values), ((lowers, share, rank), half))
    coupled = exchanged(coupled, near).reshape(width, rank)
    moved = lax.dot_general(gain, coupled, FLIPPED, preferred_element_type=jnp.float32)
    return (applied.astype(jnp.float32) - moved).astype(half)


def solution(mesh):
    return jax.shard_map(
        body,
        mesh=mesh,
        in_specs=(
            P("layer", "row", None),
            P("layer", "row", None),
            P("row", None),
            P("row", None),
            P("row", None),
            P("row", "layer"),
            P(None, "layer"),
        ),
        out_specs=P("row", "layer"),
        check_vma=False,
    )
```

```python
import jax
import jax.numpy as jnp
from jax import lax
from jax.experimental import pallas as pl
from jax.experimental.pallas import tpu as pltpu
from jax.sharding import PartitionSpec as P


def shifted(value, axis, steps):
    count = lax.axis_size(axis)
    leading, last = (max(0, -steps), min(count, count - steps))
    return lax.ppermute(value, axis, [(source, source + steps) for source in range(leading, last)])


def rotated(value, axis, steps):
    count = lax.axis_size(axis)
    return lax.ppermute(value, axis, [(source, (source + steps) % count) for source in range(count)])


def project(basis, vectors):
    return lax.dot_general(
        basis, vectors, (((0,), (0,)), ((), ())), preferred_element_type=jnp.float32
    )


def product(a, b):
    return jnp.dot(a, b, preferred_element_type=jnp.float32)


SMEM = pl.BlockSpec(memory_space=pltpu.SMEM)
HBM = pl.BlockSpec(memory_space=pltpu.HBM)
VMEM = pl.BlockSpec(memory_space=pltpu.VMEM)
PARTS = 4
FLIPPED = (((1,), (1,)), ((), ()))


def split(value):
    high = value.astype(jnp.bfloat16)
    return high, (value - high.astype(jnp.float32)).astype(jnp.bfloat16)


def wide(value, matrix):
    both = product(jnp.concatenate(split(value)), matrix)
    return both[: value.shape[0]] + both[value.shape[0] :]


def make_core(right_hbm, sketch_hbm, core_ref, right, sketch, arrived):
    copies = [
        pltpu.make_async_copy(right_hbm, right, arrived.at[0]),
        pltpu.make_async_copy(sketch_hbm, sketch, arrived.at[1]),
    ]
    for copy in copies:
        copy.start()
    for copy in copies:
        copy.wait()
    core_ref[...] = project(right[...], sketch[...]).astype(jnp.bfloat16)


def make_applied(inverse_hbm, right_hbm, applied_ref, flipped_ref, inverse, right, arrived):
    order = inverse.shape[0]
    rows = order // PARTS
    pieces = [pl.ds(part * rows, rows) for part in range(PARTS)]
    copies = [pltpu.make_async_copy(right_hbm, right, arrived.at[PARTS])]
    for part, piece in enumerate(pieces):
        copies.append(
            pltpu.make_async_copy(inverse_hbm.at[piece], inverse.at[piece], arrived.at[part])
        )
    for copy in copies:
        copy.start()
    copies[0].wait()
    for copy, piece in zip(copies[1:], pieces):
        copy.wait()
        applied = product(inverse[piece], right[...])
        applied_ref[piece] = applied.astype(jnp.bfloat16)
        flipped_ref[:, piece] = applied.T.astype(jnp.bfloat16)


def make_gain(layers, *refs):
    lefts = jnp.concatenate([ref[...] for ref in refs[:layers]], axis=1)
    cores = jnp.concatenate([ref[...] for ref in refs[layers : 2 * layers]], axis=0)
    inverse_ref, gain_ref, flipped_ref = refs[2 * layers :]
    tile_range = (-product(lefts, cores)).astype(jnp.bfloat16)
    gain = product(inverse_ref[...], tile_range)
    gain_ref[...] = gain.astype(jnp.bfloat16)
    flipped_ref[...] = gain.T.astype(jnp.bfloat16)


def make_steps(gain_ref, applied_ref, next_ref, sent_ref):
    rank = gain_ref.shape[0]
    share = sent_ref.shape[1] - rank
    basis = next_ref[...]
    map_t = (-product(gain_ref[...], basis)).astype(jnp.bfloat16)
    shift_t = product(applied_ref[...], basis).astype(jnp.bfloat16)
    for target in range(sent_ref.shape[0]):
        sent_ref[target, :rank] = map_t
        sent_ref[target, rank:] = shift_t[target * share : (target + 1) * share]


def chain(steps_ref, state, values_ref):
    count, _, rank = steps_ref.shape
    for member in range(count):
        values_ref[member] = state
        state = wide(state, steps_ref[member, :rank])
        state = state + steps_ref[member, rank:].astype(jnp.float32)
    return state


def first_half(upper_ref, steps_ref, entry_ref, values_ref, last_ref):
    @pl.when(upper_ref[0] == 0)
    def _():
        last_ref[...] = chain(steps_ref, entry_ref[...].T, values_ref).astype(jnp.bfloat16)


def second_half(upper_ref, steps_ref, before_ref, values_ref, maps_ref):
    count, rank, _ = maps_ref.shape

    @pl.when(upper_ref[0] == 0)
    def _():
        maps_ref[...] = jnp.zeros(maps_ref.shape, jnp.bfloat16)

    @pl.when(upper_ref[0] > 0)
    def _():
        chain(steps_ref, jnp.zeros(values_ref.shape[1:], jnp.float32), values_ref)
        state = steps_ref[0, :rank]
        for member in range(1, count):
            maps_ref[member] = state
            if member + 1 < count:
                state = product(state, steps_ref[member, :rank]).astype(jnp.bfloat16)


def enter(entered_ref, maps_ref, values_ref, coupled_ref):
    entered = entered_ref[...]
    coupled_ref[0] = (entered.astype(jnp.float32) + values_ref[0]).astype(jnp.bfloat16)
    for member in range(1, coupled_ref.shape[0]):
        moved = product(entered, maps_ref[member])
        coupled_ref[member] = (moved + values_ref[member]).astype(jnp.bfloat16)


def local(kernel, inputs, *outputs, scalar=False, aliases={}, cost=None, scratch=()):
    specs = [SMEM] * scalar + [HBM if scratch else VMEM] * (len(inputs) - scalar)
    return pl.pallas_call(
        kernel,
        in_specs=specs,
        out_specs=[VMEM] * len(outputs),
        out_shape=[jax.ShapeDtypeStruct(*output) for output in outputs],
        scratch_shapes=scratch,
        input_output_aliases=aliases,
        cost_estimate=cost,
        compiler_params=pltpu.CompilerParams(vmem_limit_bytes=(56 if scratch else 16) * 2**20),
    )(*inputs)


def exchanged(blocks, members):
    return lax.all_to_all(blocks, "row", 0, 0, axis_index_groups=members, tiled=True)


def body(left_factors, right_factors, sketch, row_basis, inverse_diag, right_side, incoming):
    half = jnp.bfloat16
    order, rank = sketch.shape
    width = right_side.shape[1]
    layers, groups = lax.axis_size("layer"), lax.axis_size("row")
    lowers = groups // 2
    here = lax.axis_index("row")
    upper, lower = lax.div(here, lowers), lax.rem(here, lowers)
    share = width // lowers
    near = [list(range(lowers)), list(range(lowers, groups))]

    lefts = [left_factors[0]] + [rotated(left_factors[0], "layer", k) for k in range(1, layers)]
    next_rows = shifted(row_basis, "row", -1)
    (core,) = local(
        make_core,
        (right_factors[0], sketch),
        ((rank, rank), half),
        scratch=(
            pltpu.VMEM(sketch.shape, half),
            pltpu.VMEM(sketch.shape, half),
            pltpu.SemaphoreType.DMA((2,)),
        ),
    )
    right_side, core = lax.optimization_barrier((right_side, core))
    cores = [core] + [rotated(core, "layer", k) for k in range(1, layers)]
    applied, applied_t = local(
        make_applied,
        (inverse_diag, right_side),
        ((order, width), half),
        ((width, order), half),
        cost=pl.CostEstimate(flops=1, bytes_accessed=1, transcendentals=0),
        scratch=(
            pltpu.VMEM((order, order), half),
            pltpu.VMEM((order, width), half),
            pltpu.SemaphoreType.DMA((PARTS + 1,)),
        ),
    )
    lefts[-1], applied_t = lax.optimization_barrier((lefts[-1], applied_t))

    gain, gain_t = local(
        lambda *refs: make_gain(layers, *refs),
        (*lefts, *cores, inverse_diag),
        ((order, rank), half),
        ((rank, order), half),
    )
    (sent,) = local(
        make_steps, (gain_t, applied_t, next_rows), ((lowers, rank + share, rank), half)
    )
    incoming, sent = lax.optimization_barrier((incoming, sent))
    steps = exchanged(sent, near)
    entry = lax.dynamic_slice_in_dim(incoming, lower * share, share, 1)

    place = upper.reshape(1)
    values, last = local(
        first_half,
        (place, steps, entry),
        ((lowers, share, rank), jnp.float32),
        ((share, rank), half),
        scalar=True,
    )
    entered = shifted(last, "row", lowers)
    steps, _ = lax.optimization_barrier((steps, last))
    values, maps = local(
        second_half,
        (place, steps, values),
        ((lowers, share, rank), jnp.float32),
        ((lowers, rank, rank), half),
        scalar=True,
        aliases={2: 0},
    )
    (coupled,) = local(enter, (entered, maps, values), ((lowers, share, rank), half))
    coupled = exchanged(coupled, near).reshape(width, rank)
    moved = lax.dot_general(gain, coupled, FLIPPED, preferred_element_type=jnp.float32)
    return (applied.astype(jnp.float32) - moved).astype(half)


def solution(mesh):
    return jax.shard_map(
        body,
        mesh=mesh,
        in_specs=(
            P("layer", "row", None),
            P("layer", "row", None),
            P("row", None),
            P("row", None),
            P("row", None),
            P("row", "layer"),
            P(None, "layer"),
        ),
        out_specs=P("row", "layer"),
        check_vma=False,
    )
```

```python
import jax
import jax.numpy as jnp
from jax import lax
from jax.experimental import pallas as pl
from jax.experimental.pallas import tpu as pltpu
from jax.sharding import PartitionSpec as P


def shifted(value, axis, steps):
    count = lax.axis_size(axis)
    leading, last = (max(0, -steps), min(count, count - steps))
    return lax.ppermute(value, axis, [(source, source + steps) for source in range(leading, last)])


def rotated(value, axis, steps):
    count = lax.axis_size(axis)
    return lax.ppermute(value, axis, [(source, (source + steps) % count) for source in range(count)])


def project(basis, vectors):
    return lax.dot_general(
        basis, vectors, (((0,), (0,)), ((), ())), preferred_element_type=jnp.float32
    )


def product(a, b):
    return jnp.dot(a, b, preferred_element_type=jnp.float32)


SMEM = pl.BlockSpec(memory_space=pltpu.SMEM)
HBM = pl.BlockSpec(memory_space=pltpu.HBM)
VMEM = pl.BlockSpec(memory_space=pltpu.VMEM)
FLIPPED = (((1,), (1,)), ((), ()))


def split(value):
    high = value.astype(jnp.bfloat16)
    return high, (value - high.astype(jnp.float32)).astype(jnp.bfloat16)


def wide(value, matrix):
    both = product(jnp.concatenate(split(value)), matrix)
    return both[: value.shape[0]] + both[value.shape[0] :]


def make_core(right_hbm, sketch_hbm, core_ref, right, sketch, arrived):
    copies = [
        pltpu.make_async_copy(right_hbm, right, arrived.at[0]),
        pltpu.make_async_copy(sketch_hbm, sketch, arrived.at[1]),
    ]
    for copy in copies:
        copy.start()
    for copy in copies:
        copy.wait()
    core_ref[...] = project(right[...], sketch[...]).astype(jnp.bfloat16)


def make_applied(inverse_ref, right_ref, applied_ref):
    rows = inverse_ref.shape[0] // 4

    def part(k, _):
        here = pl.ds(pl.multiple_of(k * rows, rows), rows)
        applied_ref[here, :] = product(inverse_ref[here, :], right_ref[...]).astype(jnp.bfloat16)
        return _

    lax.fori_loop(0, 4, part, 0)


def make_gain(layers, *refs):
    lefts = jnp.concatenate([ref[...] for ref in refs[:layers]], axis=1)
    cores = jnp.concatenate([ref[...] for ref in refs[layers : 2 * layers]], axis=0)
    inverse_ref, gain_ref = refs[2 * layers :]
    tile_range = (-product(lefts, cores)).astype(jnp.bfloat16)
    gain_ref[...] = product(inverse_ref[...], tile_range).astype(jnp.bfloat16)


def make_steps(gain_ref, applied_ref, next_ref, sent_ref):
    rank = gain_ref.shape[1]
    share = sent_ref.shape[1] - rank
    flipped = next_ref[...].T
    map_t = (-product(flipped, gain_ref[...])).T.astype(jnp.bfloat16)
    shift_t = product(flipped, applied_ref[...]).T.astype(jnp.bfloat16)
    for target in range(sent_ref.shape[0]):
        sent_ref[target, :rank] = map_t
        sent_ref[target, rank:] = shift_t[target * share : (target + 1) * share]


def chain(steps_ref, state, values_ref):
    count, _, rank = steps_ref.shape
    for member in range(count):
        values_ref[member] = state
        state = wide(state, steps_ref[member, :rank])
        state = state + steps_ref[member, rank:].astype(jnp.float32)
    return state


def first_half(upper_ref, steps_ref, entry_ref, values_ref, last_ref):
    @pl.when(upper_ref[0] == 0)
    def _():
        last_ref[...] = chain(steps_ref, entry_ref[...].T, values_ref).astype(jnp.bfloat16)


def second_half(upper_ref, steps_ref, before_ref, values_ref, maps_ref):
    count, rank, _ = maps_ref.shape

    @pl.when(upper_ref[0] == 0)
    def _():
        maps_ref[...] = jnp.zeros(maps_ref.shape, jnp.bfloat16)

    @pl.when(upper_ref[0] > 0)
    def _():
        chain(steps_ref, jnp.zeros(values_ref.shape[1:], jnp.float32), values_ref)
        state = steps_ref[0, :rank]
        for member in range(1, count):
            maps_ref[member] = state
            if member + 1 < count:
                state = product(state, steps_ref[member, :rank]).astype(jnp.bfloat16)


def enter(entered_ref, maps_ref, values_ref, coupled_ref):
    entered = entered_ref[...]
    coupled_ref[0] = (entered.astype(jnp.float32) + values_ref[0]).astype(jnp.bfloat16)
    for member in range(1, coupled_ref.shape[0]):
        moved = product(entered, maps_ref[member])
        coupled_ref[member] = (moved + values_ref[member]).astype(jnp.bfloat16)


def local(kernel, inputs, *outputs, scalar=False, aliases={}, cost=None, scratch=()):
    specs = [SMEM] * scalar + [HBM if scratch else VMEM] * (len(inputs) - scalar)
    return pl.pallas_call(
        kernel,
        in_specs=specs,
        out_specs=[VMEM] * len(outputs),
        out_shape=[jax.ShapeDtypeStruct(*output) for output in outputs],
        scratch_shapes=scratch,
        input_output_aliases=aliases,
        cost_estimate=cost,
        compiler_params=pltpu.CompilerParams(vmem_limit_bytes=(56 if scratch else 16) * 2**20),
    )(*inputs)


def exchanged(blocks, members):
    return lax.all_to_all(blocks, "row", 0, 0, axis_index_groups=members, tiled=True)


def body(left_factors, right_factors, sketch, row_basis, inverse_diag, right_side, incoming):
    half = jnp.bfloat16
    order, rank = sketch.shape
    width = right_side.shape[1]
    layers, groups = lax.axis_size("layer"), lax.axis_size("row")
    lowers = groups // 2
    here = lax.axis_index("row")
    upper, lower = lax.div(here, lowers), lax.rem(here, lowers)
    share = width // lowers
    near = [list(range(lowers)), list(range(lowers, groups))]

    lefts = [left_factors[0]] + [rotated(left_factors[0], "layer", k) for k in range(1, layers)]
    next_rows = shifted(row_basis, "row", -1)
    (core,) = local(
        make_core,
        (right_factors[0], sketch),
        ((rank, rank), half),
        scratch=(
            pltpu.VMEM(sketch.shape, half),
            pltpu.VMEM(sketch.shape, half),
            pltpu.SemaphoreType.DMA((2,)),
        ),
        cost=pl.CostEstimate(flops=10**10, bytes_accessed=1, transcendentals=0),
    )
    right_side, core = lax.optimization_barrier((right_side, core))
    cores = [core] + [rotated(core, "layer", k) for k in range(1, layers)]
    (applied,) = local(
        make_applied,
        (inverse_diag, right_side),
        (right_side.shape, half),
        cost=pl.CostEstimate(flops=1, bytes_accessed=1, transcendentals=0),
    )
    entry = lax.dynamic_slice_in_dim(incoming, lower * share, share, 1)
    lefts[-1], applied, entry = lax.optimization_barrier((lefts[-1], applied, entry))

    (gain,) = local(
        lambda *refs: make_gain(layers, *refs),
        (*lefts, *cores, inverse_diag),
        ((order, rank), half),
    )
    (sent,) = local(
        make_steps, (gain, applied, next_rows), ((lowers, rank + share, rank), half)
    )
    steps = exchanged(sent, near)

    place = upper.reshape(1)
    values, last = local(
        first_half,
        (place, steps, entry),
        ((lowers, share, rank), jnp.float32),
        ((share, rank), half),
        scalar=True,
    )
    entered = shifted(last, "row", lowers)
    steps, _ = lax.optimization_barrier((steps, last))
    values, maps = local(
        second_half,
        (place, steps, values),
        ((lowers, share, rank), jnp.float32),
        ((lowers, rank, rank), half),
        scalar=True,
        aliases={2: 0},
    )
    (coupled,) = local(enter, (entered, maps, values), ((lowers, share, rank), half))
    coupled = exchanged(coupled, near).reshape(width, rank)
    moved = lax.dot_general(gain, coupled, FLIPPED, preferred_element_type=jnp.float32)
    return (applied.astype(jnp.float32) - moved).astype(half)


def solution(mesh):
    return jax.shard_map(
        body,
        mesh=mesh,
        in_specs=(
            P("layer", "row", None),
            P("layer", "row", None),
            P("row", None),
            P("row", None),
            P("row", None),
            P("row", "layer"),
            P(None, "layer"),
        ),
        out_specs=P("row", "layer"),
        check_vma=False,
    )
```

```python
import jax
import jax.numpy as jnp
from jax import lax
from jax.experimental import pallas as pl
from jax.experimental.pallas import tpu as pltpu
from jax.sharding import PartitionSpec as P


def shifted(value, axis, steps):
    count = lax.axis_size(axis)
    leading, last = (max(0, -steps), min(count, count - steps))
    return lax.ppermute(value, axis, [(source, source + steps) for source in range(leading, last)])


def rotated(value, axis, steps):
    count = lax.axis_size(axis)
    return lax.ppermute(value, axis, [(source, (source + steps) % count) for source in range(count)])


def project(basis, vectors):
    return lax.dot_general(
        basis, vectors, (((0,), (0,)), ((), ())), preferred_element_type=jnp.float32
    )


def product(a, b):
    return jnp.dot(a, b, preferred_element_type=jnp.float32)


SMEM = pl.BlockSpec(memory_space=pltpu.SMEM)
HBM = pl.BlockSpec(memory_space=pltpu.HBM)
VMEM = pl.BlockSpec(memory_space=pltpu.VMEM)
PARTS = 4
FLIPPED = (((1,), (1,)), ((), ()))


def split(value):
    high = value.astype(jnp.bfloat16)
    return high, (value - high.astype(jnp.float32)).astype(jnp.bfloat16)


def wide(value, matrix, twice=False):
    parts = jnp.concatenate(split(value))
    both = product(jnp.concatenate([parts, parts], axis=1) if twice else parts, matrix)
    return both[: value.shape[0]] + both[value.shape[0] :]


def make_maps(layers, *refs):
    lefts = jnp.concatenate([ref[...] for ref in refs[:layers]], axis=1)
    cores = jnp.concatenate([ref[...] for ref in refs[layers : 2 * layers]], axis=0)
    weights_ref, shift_ref, sent_ref = refs[2 * layers :]
    map_t = wide(wide(weights_ref[...], lefts), cores).T.astype(jnp.bfloat16)
    rank = map_t.shape[0]
    for target in range(sent_ref.shape[0]):
        sent_ref[target, :rank] = map_t
        sent_ref[target, rank:] = shift_ref[target]


def chain(steps_ref, state, values_ref):
    count, _, rank = steps_ref.shape
    for member in range(count):
        values_ref[member] = state
        state = wide(state, steps_ref[member, :rank])
        state = state + steps_ref[member, rank:].astype(jnp.float32)
    return state


def leave(upper_ref, steps_ref, entry_ref, last_ref):
    count, _, rank = steps_ref.shape

    @pl.when(upper_ref[0] == 0)
    def _():
        pairs = [product(steps_ref[k], steps_ref[k + 1, :rank]) for k in range(0, count, 2)]
        state = entry_ref[...].T
        for index, pair in enumerate(pairs):
            moved = wide(state, jnp.concatenate(split(pair[:rank])), twice=True)
            shift = pair[rank:] + steps_ref[2 * index + 1, rank:].astype(jnp.float32)
            state = moved + shift
        last_ref[...] = state.astype(jnp.bfloat16)


def compose(upper_ref, steps_ref, entry_ref, values_ref, maps_ref):
    count, rank, _ = maps_ref.shape
    first = upper_ref[0] == 0
    chain(steps_ref, jnp.where(first, entry_ref[...].T, 0.0), values_ref)

    @pl.when(first)
    def _():
        maps_ref[...] = jnp.zeros(maps_ref.shape, jnp.bfloat16)

    @pl.when(jnp.logical_not(first))
    def _():
        state = steps_ref[0, :rank]
        for member in range(1, count):
            maps_ref[member] = state
            if member + 1 < count:
                state = product(state, steps_ref[member, :rank]).astype(jnp.bfloat16)


def enter(entered_ref, maps_ref, values_ref, coupled_ref):
    entered = entered_ref[...]
    coupled_ref[0] = (entered.astype(jnp.float32) + values_ref[0]).astype(jnp.bfloat16)
    for member in range(1, coupled_ref.shape[0]):
        moved = product(entered, maps_ref[member])
        coupled_ref[member] = (moved + values_ref[member]).astype(jnp.bfloat16)


def solve(gain_ref, coupled_ref, applied_ref, result_hbm, result, sent):
    rows = gain_ref.shape[0] // PARTS
    copies = []
    for part in range(PARTS):
        piece = pl.ds(part * rows, rows)
        moved = lax.dot_general(
            gain_ref[piece], coupled_ref[...], FLIPPED, preferred_element_type=jnp.float32
        )
        applied = applied_ref[piece].astype(jnp.float32)
        result[piece] = (applied - moved).astype(jnp.bfloat16)
        copies.append(pltpu.make_async_copy(result.at[piece], result_hbm.at[piece], sent.at[part]))
        copies[-1].start()
    for copy in copies:
        copy.wait()


def local(kernel, inputs, *outputs, scalar=False):
    specs = [SMEM] * scalar + [VMEM] * (len(inputs) - scalar)
    return pl.pallas_call(
        kernel,
        in_specs=specs,
        out_specs=[VMEM] * len(outputs),
        out_shape=[jax.ShapeDtypeStruct(*output) for output in outputs],
        compiler_params=pltpu.CompilerParams(vmem_limit_bytes=16 * 2**20),
    )(*inputs)


def exchanged(blocks, members):
    return lax.all_to_all(blocks, "row", 0, 0, axis_index_groups=members, tiled=True)


def body(left_factors, right_factors, sketch, row_basis, inverse_diag, right_side, incoming):
    half = jnp.bfloat16
    rank = sketch.shape[1]
    width = right_side.shape[1]
    layers, groups = lax.axis_size("layer"), lax.axis_size("row")
    lowers = groups // 2
    here = lax.axis_index("row")
    upper, lower = lax.div(here, lowers), lax.rem(here, lowers)
    share = width // lowers
    near = [list(range(lowers)), list(range(lowers, groups))]

    lefts = [left_factors[0]] + [rotated(left_factors[0], "layer", k) for k in range(1, layers)]
    next_rows = shifted(row_basis, "row", -1)
    applied = product(inverse_diag, right_side).astype(half)
    sketch, applied = lax.optimization_barrier((sketch, applied))
    core = project(right_factors[0], sketch).astype(half)
    cores = [core] + [rotated(core, "layer", k) for k in range(1, layers)]

    shift_t = project(applied, next_rows).astype(half).reshape(lowers, share, rank)
    weights = project(next_rows, inverse_diag)
    lefts[-1], shift_t, weights = lax.optimization_barrier((lefts[-1], shift_t, weights))
    (sent,) = local(
        lambda *refs: make_maps(layers, *refs),
        (*lefts, *cores, weights, shift_t),
        ((lowers, rank + share, rank), half),
    )
    lefts, incoming, sent = lax.optimization_barrier((lefts, incoming, sent))
    steps = exchanged(sent, near)
    entry = lax.dynamic_slice_in_dim(incoming, lower * share, share, 1)
    tile_range = -sum(product(left, core) for left, core in zip(lefts, cores))
    gain = product(inverse_diag, tile_range.astype(half)).astype(half)
    gain, entry, steps = lax.optimization_barrier((gain, entry, steps))

    place = upper.reshape(1)
    (last,) = local(leave, (place, steps, entry), ((share, rank), half), scalar=True)
    entered = shifted(last, "row", lowers)
    steps, _ = lax.optimization_barrier((steps, last))
    values, maps = local(
        compose,
        (place, steps, entry),
        ((lowers, share, rank), jnp.float32),
        ((lowers, rank, rank), half),
        scalar=True,
    )
    (coupled,) = local(enter, (entered, maps, values), ((lowers, share, rank), half))
    coupled = exchanged(coupled, near).reshape(width, rank)
    return pl.pallas_call(
        solve,
        in_specs=[VMEM] * 3,
        out_specs=HBM,
        out_shape=jax.ShapeDtypeStruct(applied.shape, half),
        scratch_shapes=[pltpu.VMEM(applied.shape, half), pltpu.SemaphoreType.DMA((PARTS,))],
        compiler_params=pltpu.CompilerParams(vmem_limit_bytes=16 * 2**20),
    )(gain, coupled, applied)


def solution(mesh):
    return jax.shard_map(
        body,
        mesh=mesh,
        in_specs=(
            P("layer", "row", None),
            P("layer", "row", None),
            P("row", None),
            P("row", None),
            P("row", None),
            P("row", "layer"),
            P(None, "layer"),
        ),
        out_specs=P("row", "layer"),
        check_vma=False,
    )
```

```python
import jax
import jax.numpy as jnp
from jax import lax
from jax.experimental import pallas as pl
from jax.experimental.pallas import tpu as pltpu
from jax.sharding import PartitionSpec as P


def shifted(value, axis, steps):
    count = lax.axis_size(axis)
    leading, last = (max(0, -steps), min(count, count - steps))
    return lax.ppermute(value, axis, [(source, source + steps) for source in range(leading, last)])


def rotated(value, axis, steps):
    count = lax.axis_size(axis)
    return lax.ppermute(value, axis, [(source, (source + steps) % count) for source in range(count)])


def project(basis, vectors):
    return lax.dot_general(
        basis, vectors, (((0,), (0,)), ((), ())), preferred_element_type=jnp.float32
    )


def product(a, b):
    return jnp.dot(a, b, preferred_element_type=jnp.float32)


SMEM = pl.BlockSpec(memory_space=pltpu.SMEM)
VMEM = pl.BlockSpec(memory_space=pltpu.VMEM)
FLIPPED = (((1,), (1,)), ((), ()))


def split(value):
    high = value.astype(jnp.bfloat16)
    return high, (value - high.astype(jnp.float32)).astype(jnp.bfloat16)


def wide(value, matrix, twice=False):
    parts = jnp.concatenate(split(value))
    both = product(jnp.concatenate([parts, parts], axis=1) if twice else parts, matrix)
    return both[: value.shape[0]] + both[value.shape[0] :]


def make_maps(layers, *refs):
    lefts = jnp.concatenate([ref[...] for ref in refs[:layers]], axis=1)
    cores = jnp.concatenate([ref[...] for ref in refs[layers : 2 * layers]], axis=0)
    weights_ref, shift_ref, sent_ref = refs[2 * layers :]
    map_t = wide(wide(weights_ref[...], lefts), cores).T.astype(jnp.bfloat16)
    rank = map_t.shape[0]
    for target in range(sent_ref.shape[0]):
        sent_ref[target, :rank] = map_t
        sent_ref[target, rank:] = shift_ref[target]


def make_gain(layers, *refs):
    lefts = jnp.concatenate([ref[...] for ref in refs[:layers]], axis=1)
    cores = jnp.concatenate([ref[...] for ref in refs[layers : 2 * layers]], axis=0)
    inverse_ref, gain_ref = refs[2 * layers :]
    tile_range = (-product(lefts, cores)).astype(jnp.bfloat16)
    gain_ref[...] = product(inverse_ref[...], tile_range).astype(jnp.bfloat16)


def chain(steps_ref, state, values_ref):
    count, _, rank = steps_ref.shape
    for member in range(count):
        values_ref[member] = state
        state = wide(state, steps_ref[member, :rank])
        state = state + steps_ref[member, rank:].astype(jnp.float32)
    return state


def leave(upper_ref, steps_ref, entry_ref, last_ref):
    count, _, rank = steps_ref.shape

    @pl.when(upper_ref[0] == 0)
    def _():
        pairs = [product(steps_ref[k], steps_ref[k + 1, :rank]) for k in range(0, count, 2)]
        state = entry_ref[...].T
        for index, pair in enumerate(pairs):
            moved = wide(state, jnp.concatenate(split(pair[:rank])), twice=True)
            shift = pair[rank:] + steps_ref[2 * index + 1, rank:].astype(jnp.float32)
            state = moved + shift
        last_ref[...] = state.astype(jnp.bfloat16)


def compose(upper_ref, steps_ref, entry_ref, values_ref, maps_ref):
    count, rank, _ = maps_ref.shape
    first = upper_ref[0] == 0
    chain(steps_ref, jnp.where(first, entry_ref[...].T, 0.0), values_ref)

    @pl.when(first)
    def _():
        maps_ref[...] = jnp.zeros(maps_ref.shape, jnp.bfloat16)

    @pl.when(jnp.logical_not(first))
    def _():
        state = steps_ref[0, :rank]
        for member in range(1, count):
            maps_ref[member] = state
            if member + 1 < count:
                state = product(state, steps_ref[member, :rank]).astype(jnp.bfloat16)


def enter(entered_ref, maps_ref, values_ref, coupled_ref):
    entered = entered_ref[...]
    coupled_ref[0] = (entered.astype(jnp.float32) + values_ref[0]).astype(jnp.bfloat16)
    for member in range(1, coupled_ref.shape[0]):
        moved = product(entered, maps_ref[member])
        coupled_ref[member] = (moved + values_ref[member]).astype(jnp.bfloat16)


def local(kernel, inputs, *outputs, scalar=False):
    specs = [SMEM] * scalar + [VMEM] * (len(inputs) - scalar)
    return pl.pallas_call(
        kernel,
        in_specs=specs,
        out_specs=[VMEM] * len(outputs),
        out_shape=[jax.ShapeDtypeStruct(*output) for output in outputs],
        compiler_params=pltpu.CompilerParams(vmem_limit_bytes=16 * 2**20),
    )(*inputs)


def exchanged(blocks, members):
    return lax.all_to_all(blocks, "row", 0, 0, axis_index_groups=members, tiled=True)


def body(left_factors, right_factors, sketch, row_basis, inverse_diag, right_side, incoming):
    half = jnp.bfloat16
    order, rank = sketch.shape
    width = right_side.shape[1]
    layers, groups = lax.axis_size("layer"), lax.axis_size("row")
    lowers = groups // 2
    here = lax.axis_index("row")
    upper, lower = lax.div(here, lowers), lax.rem(here, lowers)
    share = width // lowers
    near = [list(range(lowers)), list(range(lowers, groups))]

    lefts = [left_factors[0]] + [rotated(left_factors[0], "layer", k) for k in range(1, layers)]
    next_rows = shifted(row_basis, "row", -1)
    applied = product(inverse_diag, right_side).astype(half)
    sketch, applied = lax.optimization_barrier((sketch, applied))
    core = project(right_factors[0], sketch).astype(half)
    cores = [core] + [rotated(core, "layer", k) for k in range(1, layers)]

    shift_t = project(applied, next_rows).astype(half).reshape(lowers, share, rank)
    weights = project(next_rows, inverse_diag)
    entry = lax.dynamic_slice_in_dim(incoming, lower * share, share, 1)
    lefts[-1], shift_t, weights, entry = lax.optimization_barrier(
        (lefts[-1], shift_t, weights, entry)
    )
    (sent,) = local(
        lambda *refs: make_maps(layers, *refs),
        (*lefts, *cores, weights, shift_t),
        ((lowers, rank + share, rank), half),
    )
    steps = exchanged(sent, near)

    place = upper.reshape(1)
    (last,) = local(leave, (place, steps, entry), ((share, rank), half), scalar=True)
    entered = shifted(last, "row", lowers)
    steps, lefts, _ = lax.optimization_barrier((steps, lefts, last))
    values, maps = local(
        compose,
        (place, steps, entry),
        ((lowers, share, rank), jnp.float32),
        ((lowers, rank, rank), half),
        scalar=True,
    )
    (gain,) = local(
        lambda *refs: make_gain(layers, *refs),
        (*lefts, *cores, inverse_diag),
        ((order, rank), half),
    )
    gain, maps = lax.optimization_barrier((gain, maps))
    (coupled,) = local(enter, (entered, maps, values), ((lowers, share, rank), half))
    coupled = exchanged(coupled, near).reshape(width, rank)
    moved = lax.dot_general(gain, coupled, FLIPPED, preferred_element_type=jnp.float32)
    return (applied.astype(jnp.float32) - moved).astype(half)


def solution(mesh):
    return jax.shard_map(
        body,
        mesh=mesh,
        in_specs=(
            P("layer", "row", None),
            P("layer", "row", None),
            P("row", None),
            P("row", None),
            P("row", None),
            P("row", "layer"),
            P(None, "layer"),
        ),
        out_specs=P("row", "layer"),
        check_vma=False,
    )
```

```python
import jax
import jax.numpy as jnp
from jax import lax
from jax.experimental import pallas as pl
from jax.experimental.pallas import tpu as pltpu
from jax.sharding import PartitionSpec as P


def shifted(value, axis, steps):
    count = lax.axis_size(axis)
    leading, last = (max(0, -steps), min(count, count - steps))
    return lax.ppermute(value, axis, [(source, source + steps) for source in range(leading, last)])


def rotated(value, axis, steps):
    count = lax.axis_size(axis)
    return lax.ppermute(value, axis, [(source, (source + steps) % count) for source in range(count)])


def project(basis, vectors):
    return lax.dot_general(
        basis, vectors, (((0,), (0,)), ((), ())), preferred_element_type=jnp.float32
    )


def product(a, b):
    return jnp.dot(a, b, preferred_element_type=jnp.float32)


SMEM = pl.BlockSpec(memory_space=pltpu.SMEM)
VMEM = pl.BlockSpec(memory_space=pltpu.VMEM)
FLIPPED = (((1,), (1,)), ((), ()))


def split(value):
    high = value.astype(jnp.bfloat16)
    return high, (value - high.astype(jnp.float32)).astype(jnp.bfloat16)


def wide(value, matrix, twice=False):
    parts = jnp.concatenate(split(value))
    both = product(jnp.concatenate([parts, parts], axis=1) if twice else parts, matrix)
    return both[: value.shape[0]] + both[value.shape[0] :]


def make_maps(layers, *refs):
    lefts = jnp.concatenate([ref[...] for ref in refs[:layers]], axis=1)
    cores = jnp.concatenate([ref[...] for ref in refs[layers : 2 * layers]], axis=0)
    weights_ref, shift_ref, sent_ref = refs[2 * layers :]
    map_t = wide(wide(weights_ref[...], lefts), cores).T.astype(jnp.bfloat16)
    rank = map_t.shape[0]
    for target in range(sent_ref.shape[0]):
        sent_ref[target, :rank] = map_t
        sent_ref[target, rank:] = shift_ref[target]


def make_gain(layers, *refs):
    lefts = jnp.concatenate([ref[...] for ref in refs[:layers]], axis=1)
    cores = jnp.concatenate([ref[...] for ref in refs[layers : 2 * layers]], axis=0)
    inverse_ref, gain_ref = refs[2 * layers :]
    tile_range = (-product(lefts, cores)).astype(jnp.bfloat16)
    gain_ref[...] = product(inverse_ref[...], tile_range).astype(jnp.bfloat16)


def chain(steps_ref, state, values_ref):
    count, _, rank = steps_ref.shape
    for member in range(count):
        values_ref[member] = state
        state = wide(state, steps_ref[member, :rank])
        state = state + steps_ref[member, rank:].astype(jnp.float32)
    return state


def leave(upper_ref, steps_ref, entry_ref, last_ref):
    count, _, rank = steps_ref.shape

    @pl.when(upper_ref[0] == 0)
    def _():
        pairs = [product(steps_ref[k], steps_ref[k + 1, :rank]) for k in range(0, count, 2)]
        state = entry_ref[...].T
        for index, pair in enumerate(pairs):
            moved = wide(state, jnp.concatenate(split(pair[:rank])), twice=True)
            shift = pair[rank:] + steps_ref[2 * index + 1, rank:].astype(jnp.float32)
            state = moved + shift
        last_ref[...] = state.astype(jnp.bfloat16)


def compose(upper_ref, steps_ref, entry_ref, values_ref, maps_ref):
    count, rank, _ = maps_ref.shape
    first = upper_ref[0] == 0
    chain(steps_ref, jnp.where(first, entry_ref[...].T, 0.0), values_ref)

    @pl.when(first)
    def _():
        maps_ref[...] = jnp.zeros(maps_ref.shape, jnp.bfloat16)

    @pl.when(jnp.logical_not(first))
    def _():
        state = steps_ref[0, :rank]
        for member in range(1, count):
            maps_ref[member] = state
            if member + 1 < count:
                state = product(state, steps_ref[member, :rank]).astype(jnp.bfloat16)


def enter(entered_ref, maps_ref, values_ref, coupled_ref):
    entered = entered_ref[...]
    coupled_ref[0] = (entered.astype(jnp.float32) + values_ref[0]).astype(jnp.bfloat16)
    for member in range(1, coupled_ref.shape[0]):
        moved = product(entered, maps_ref[member])
        coupled_ref[member] = (moved + values_ref[member]).astype(jnp.bfloat16)


def local(kernel, inputs, *outputs, scalar=False):
    specs = [SMEM] * scalar + [VMEM] * (len(inputs) - scalar)
    return pl.pallas_call(
        kernel,
        in_specs=specs,
        out_specs=[VMEM] * len(outputs),
        out_shape=[jax.ShapeDtypeStruct(*output) for output in outputs],
        compiler_params=pltpu.CompilerParams(vmem_limit_bytes=16 * 2**20),
    )(*inputs)


def exchanged(blocks, members):
    return lax.all_to_all(blocks, "row", 0, 0, axis_index_groups=members, tiled=True)


def body(left_factors, right_factors, sketch, row_basis, inverse_diag, right_side, incoming):
    half = jnp.bfloat16
    order, rank = sketch.shape
    width = right_side.shape[1]
    layers, groups = lax.axis_size("layer"), lax.axis_size("row")
    lowers = groups // 2
    here = lax.axis_index("row")
    upper, lower = lax.div(here, lowers), lax.rem(here, lowers)
    share = width // lowers
    near = [list(range(lowers)), list(range(lowers, groups))]

    lefts = [left_factors[0]] + [rotated(left_factors[0], "layer", k) for k in range(1, layers)]
    next_rows = shifted(row_basis, "row", -1)
    applied = product(inverse_diag, right_side).astype(half)
    sketch, applied = lax.optimization_barrier((sketch, applied))
    core = project(right_factors[0], sketch).astype(half)
    cores = [core] + [rotated(core, "layer", k) for k in range(1, layers)]

    shift_t = project(applied, next_rows).astype(half).reshape(lowers, share, rank)
    weights = project(next_rows, inverse_diag)
    entry = lax.dynamic_slice_in_dim(incoming, lower * share, share, 1)
    place = upper.reshape(1)
    lefts[-1], shift_t, weights, entry, place = lax.optimization_barrier(
        (lefts[-1], shift_t, weights, entry, place)
    )
    (sent,) = local(
        lambda *refs: make_maps(layers, *refs),
        (*lefts, *cores, weights, shift_t),
        ((lowers, rank + share, rank), half),
    )
    sent, lefts, cores, entry, place, applied, inverse_diag = lax.optimization_barrier(
        (sent, lefts, cores, entry, place, applied, inverse_diag)
    )
    steps = exchanged(sent, near)
    steps, lefts, cores, entry, place, applied, inverse_diag = lax.optimization_barrier(
        (steps, lefts, cores, entry, place, applied, inverse_diag)
    )
    (last,) = local(leave, (place, steps, entry), ((share, rank), half), scalar=True)
    entered = shifted(last, "row", lowers)
    steps, lefts, _ = lax.optimization_barrier((steps, lefts, last))
    values, maps = local(
        compose,
        (place, steps, entry),
        ((lowers, share, rank), jnp.float32),
        ((lowers, rank, rank), half),
        scalar=True,
    )
    (gain,) = local(
        lambda *refs: make_gain(layers, *refs),
        (*lefts, *cores, inverse_diag),
        ((order, rank), half),
    )
    gain, maps = lax.optimization_barrier((gain, maps))
    (coupled,) = local(enter, (entered, maps, values), ((lowers, share, rank), half))
    coupled = exchanged(coupled, near).reshape(width, rank)
    moved = lax.dot_general(gain, coupled, FLIPPED, preferred_element_type=jnp.float32)
    return (applied.astype(jnp.float32) - moved).astype(half)


def solution(mesh):
    return jax.shard_map(
        body,
        mesh=mesh,
        in_specs=(
            P("layer", "row", None),
            P("layer", "row", None),
            P("row", None),
            P("row", None),
            P("row", None),
            P("row", "layer"),
            P(None, "layer"),
        ),
        out_specs=P("row", "layer"),
        check_vma=False,
    )
```

```python
import jax
import jax.numpy as jnp
from jax import lax
from jax.experimental import pallas as pl
from jax.experimental.pallas import tpu as pltpu
from jax.sharding import PartitionSpec as P


def shifted(value, axis, steps):
    count = lax.axis_size(axis)
    leading, last = (max(0, -steps), min(count, count - steps))
    return lax.ppermute(value, axis, [(source, source + steps) for source in range(leading, last)])


def rotated(value, axis, steps):
    count = lax.axis_size(axis)
    return lax.ppermute(value, axis, [(source, (source + steps) % count) for source in range(count)])


def project(basis, vectors):
    return lax.dot_general(
        basis, vectors, (((0,), (0,)), ((), ())), preferred_element_type=jnp.float32
    )


def product(a, b):
    return jnp.dot(a, b, preferred_element_type=jnp.float32)


SMEM = pl.BlockSpec(memory_space=pltpu.SMEM)
VMEM = pl.BlockSpec(memory_space=pltpu.VMEM)
FLIPPED = (((1,), (1,)), ((), ()))


def split(value):
    high = value.astype(jnp.bfloat16)
    return high, (value - high.astype(jnp.float32)).astype(jnp.bfloat16)


def wide(value, matrix, twice=False):
    parts = jnp.concatenate(split(value))
    both = product(jnp.concatenate([parts, parts], axis=1) if twice else parts, matrix)
    return both[: value.shape[0]] + both[value.shape[0] :]


def make_applied(inverse_ref, right_ref, applied_ref):
    rows = inverse_ref.shape[0] // 4

    def part(k, _):
        here = pl.ds(pl.multiple_of(k * rows, rows), rows)
        applied_ref[here, :] = product(inverse_ref[here, :], right_ref[...]).astype(jnp.bfloat16)
        return _

    lax.fori_loop(0, 4, part, 0)


def make_gain(layers, *refs):
    lefts = jnp.concatenate([ref[...] for ref in refs[:layers]], axis=1)
    cores = jnp.concatenate([ref[...] for ref in refs[layers : 2 * layers]], axis=0)
    inverse_ref, gain_ref = refs[2 * layers :]
    tile_range = (-product(lefts, cores)).astype(jnp.bfloat16)
    gain_ref[...] = product(inverse_ref[...], tile_range).astype(jnp.bfloat16)


def make_steps(gain_ref, applied_ref, next_ref, sent_ref):
    rank = gain_ref.shape[1]
    share = sent_ref.shape[1] - rank
    flipped = next_ref[...].T
    map_t = (-product(flipped, gain_ref[...])).T.astype(jnp.bfloat16)
    shift_t = product(flipped, applied_ref[...]).T.astype(jnp.bfloat16)
    for target in range(sent_ref.shape[0]):
        sent_ref[target, :rank] = map_t
        sent_ref[target, rank:] = shift_t[target * share : (target + 1) * share]


def chain(steps_ref, state, values_ref):
    count, _, rank = steps_ref.shape
    for member in range(count):
        values_ref[member] = state
        state = wide(state, steps_ref[member, :rank])
        state = state + steps_ref[member, rank:].astype(jnp.float32)
    return state


def leave(upper_ref, steps_ref, entry_ref, last_ref):
    count, _, rank = steps_ref.shape

    @pl.when(upper_ref[0] == 0)
    def _():
        pairs = [product(steps_ref[k], steps_ref[k + 1, :rank]) for k in range(0, count, 2)]
        state = entry_ref[...].T
        for index, pair in enumerate(pairs):
            moved = wide(state, jnp.concatenate(split(pair[:rank])), twice=True)
            shift = pair[rank:] + steps_ref[2 * index + 1, rank:].astype(jnp.float32)
            state = moved + shift
        last_ref[...] = state.astype(jnp.bfloat16)


def compose(upper_ref, steps_ref, entry_ref, values_ref, maps_ref):
    count, rank, _ = maps_ref.shape
    first = upper_ref[0] == 0
    chain(steps_ref, jnp.where(first, entry_ref[...].T, 0.0), values_ref)

    @pl.when(first)
    def _():
        maps_ref[...] = jnp.zeros(maps_ref.shape, jnp.bfloat16)

    @pl.when(jnp.logical_not(first))
    def _():
        state = steps_ref[0, :rank]
        for member in range(1, count):
            maps_ref[member] = state
            if member + 1 < count:
                state = product(state, steps_ref[member, :rank]).astype(jnp.bfloat16)


def enter(entered_ref, maps_ref, values_ref, coupled_ref):
    entered = entered_ref[...]
    coupled_ref[0] = (entered.astype(jnp.float32) + values_ref[0]).astype(jnp.bfloat16)
    for member in range(1, coupled_ref.shape[0]):
        moved = product(entered, maps_ref[member])
        coupled_ref[member] = (moved + values_ref[member]).astype(jnp.bfloat16)


def local(kernel, inputs, *outputs, scalar=False, cost=None):
    specs = [SMEM] * scalar + [VMEM] * (len(inputs) - scalar)
    return pl.pallas_call(
        kernel,
        in_specs=specs,
        out_specs=[VMEM] * len(outputs),
        out_shape=[jax.ShapeDtypeStruct(*output) for output in outputs],
        cost_estimate=cost,
        compiler_params=pltpu.CompilerParams(vmem_limit_bytes=16 * 2**20),
    )(*inputs)


def exchanged(blocks, members):
    return lax.all_to_all(blocks, "row", 0, 0, axis_index_groups=members, tiled=True)


def body(left_factors, right_factors, sketch, row_basis, inverse_diag, right_side, incoming):
    half = jnp.bfloat16
    order, rank = sketch.shape
    width = right_side.shape[1]
    layers, groups = lax.axis_size("layer"), lax.axis_size("row")
    lowers = groups // 2
    here = lax.axis_index("row")
    upper, lower = lax.div(here, lowers), lax.rem(here, lowers)
    share = width // lowers
    near = [list(range(lowers)), list(range(lowers, groups))]

    lefts = [left_factors[0]] + [rotated(left_factors[0], "layer", k) for k in range(1, layers)]
    next_rows = shifted(row_basis, "row", -1)
    core = project(right_factors[0], sketch).astype(half)
    right_side, core = lax.optimization_barrier((right_side, core))
    cores = [core] + [rotated(core, "layer", k) for k in range(1, layers)]
    (applied,) = local(
        make_applied,
        (inverse_diag, right_side),
        (right_side.shape, half),
        cost=pl.CostEstimate(flops=1, bytes_accessed=1, transcendentals=0),
    )
    entry = lax.dynamic_slice_in_dim(incoming, lower * share, share, 1)
    place = upper.reshape(1)
    lefts[-1], applied, entry, place = lax.optimization_barrier(
        (lefts[-1], applied, entry, place)
    )

    (gain,) = local(
        lambda *refs: make_gain(layers, *refs),
        (*lefts, *cores, inverse_diag),
        ((order, rank), half),
    )
    (sent,) = local(
        make_steps, (gain, applied, next_rows), ((lowers, rank + share, rank), half)
    )
    sent, entry, place = lax.optimization_barrier((sent, entry, place))
    steps = exchanged(sent, near)
    steps, entry, place = lax.optimization_barrier((steps, entry, place))
    (last,) = local(leave, (place, steps, entry), ((share, rank), half), scalar=True)
    entered = shifted(last, "row", lowers)
    steps, _ = lax.optimization_barrier((steps, last))
    values, maps = local(
        compose,
        (place, steps, entry),
        ((lowers, share, rank), jnp.float32),
        ((lowers, rank, rank), half),
        scalar=True,
    )
    (coupled,) = local(enter, (entered, maps, values), ((lowers, share, rank), half))
    coupled = exchanged(coupled, near).reshape(width, rank)
    moved = lax.dot_general(gain, coupled, FLIPPED, preferred_element_type=jnp.float32)
    return (applied.astype(jnp.float32) - moved).astype(half)


def solution(mesh):
    return jax.shard_map(
        body,
        mesh=mesh,
        in_specs=(
            P("layer", "row", None),
            P("layer", "row", None),
            P("row", None),
            P("row", None),
            P("row", None),
            P("row", "layer"),
            P(None, "layer"),
        ),
        out_specs=P("row", "layer"),
        check_vma=False,
    )
```

```python
import jax
import jax.numpy as jnp
from jax import lax
from jax.experimental import pallas as pl
from jax.experimental.pallas import tpu as pltpu
from jax.sharding import PartitionSpec as P


def shifted(value, axis, steps):
    count = lax.axis_size(axis)
    leading, last = (max(0, -steps), min(count, count - steps))
    return lax.ppermute(value, axis, [(source, source + steps) for source in range(leading, last)])


def rotated(value, axis, steps):
    count = lax.axis_size(axis)
    return lax.ppermute(value, axis, [(source, (source + steps) % count) for source in range(count)])


def project(basis, vectors):
    return lax.dot_general(
        basis, vectors, (((0,), (0,)), ((), ())), preferred_element_type=jnp.float32
    )


def product(a, b):
    return jnp.dot(a, b, preferred_element_type=jnp.float32)


SMEM = pl.BlockSpec(memory_space=pltpu.SMEM)
VMEM = pl.BlockSpec(memory_space=pltpu.VMEM)
FLIPPED = (((1,), (1,)), ((), ()))


def split(value):
    high = value.astype(jnp.bfloat16)
    return high, (value - high.astype(jnp.float32)).astype(jnp.bfloat16)


def wide(value, matrix):
    both = product(jnp.concatenate(split(value)), matrix)
    return both[: value.shape[0]] + both[value.shape[0] :]


def make_maps(layers, *refs):
    lefts = jnp.concatenate([ref[...] for ref in refs[:layers]], axis=1)
    cores = jnp.concatenate([ref[...] for ref in refs[layers : 2 * layers]], axis=0)
    weights_ref, shift_ref, range_ref, sent_ref = refs[2 * layers :]
    range_ref[...] = (-product(lefts, cores)).astype(jnp.bfloat16)
    map_t = wide(wide(weights_ref[...], lefts), cores).T.astype(jnp.bfloat16)
    rank = map_t.shape[0]
    for target in range(sent_ref.shape[0]):
        sent_ref[target, :rank] = map_t
        sent_ref[target, rank:] = shift_ref[target]


def chain(steps_ref, state, values_ref):
    count, _, rank = steps_ref.shape
    for member in range(count):
        values_ref[member] = state
        state = wide(state, steps_ref[member, :rank])
        state = state + steps_ref[member, rank:].astype(jnp.float32)
    return state


def first_half(upper_ref, steps_ref, entry_ref, values_ref, last_ref):
    @pl.when(upper_ref[0] == 0)
    def _():
        last_ref[...] = chain(steps_ref, entry_ref[...].T, values_ref).astype(jnp.bfloat16)


def second_half(upper_ref, steps_ref, before_ref, values_ref, maps_ref):
    count, rank, _ = maps_ref.shape

    @pl.when(upper_ref[0] == 0)
    def _():
        maps_ref[...] = jnp.zeros(maps_ref.shape, jnp.bfloat16)

    @pl.when(upper_ref[0] > 0)
    def _():
        chain(steps_ref, jnp.zeros(values_ref.shape[1:], jnp.float32), values_ref)
        state = steps_ref[0, :rank]
        for member in range(1, count):
            maps_ref[member] = state
            if member + 1 < count:
                state = product(state, steps_ref[member, :rank]).astype(jnp.bfloat16)


def enter(entered_ref, maps_ref, values_ref, coupled_ref):
    entered = entered_ref[...]
    coupled_ref[0] = (entered.astype(jnp.float32) + values_ref[0]).astype(jnp.bfloat16)
    for member in range(1, coupled_ref.shape[0]):
        moved = product(entered, maps_ref[member])
        coupled_ref[member] = (moved + values_ref[member]).astype(jnp.bfloat16)


def local(kernel, inputs, *outputs, scalar=False, aliases={}):
    specs = [SMEM] * scalar + [VMEM] * (len(inputs) - scalar)
    return pl.pallas_call(
        kernel,
        in_specs=specs,
        out_specs=[VMEM] * len(outputs),
        out_shape=[jax.ShapeDtypeStruct(*output) for output in outputs],
        input_output_aliases=aliases,
        compiler_params=pltpu.CompilerParams(vmem_limit_bytes=16 * 2**20),
    )(*inputs)


def exchanged(blocks, members):
    return lax.all_to_all(blocks, "row", 0, 0, axis_index_groups=members, tiled=True)


def body(left_factors, right_factors, sketch, row_basis, inverse_diag, right_side, incoming):
    half = jnp.bfloat16
    order, rank = sketch.shape
    width = right_side.shape[1]
    layers, groups = lax.axis_size("layer"), lax.axis_size("row")
    lowers = groups // 2
    here = lax.axis_index("row")
    upper, lower = lax.div(here, lowers), lax.rem(here, lowers)
    share = width // lowers
    near = [list(range(lowers)), list(range(lowers, groups))]

    lefts = [left_factors[0]] + [rotated(left_factors[0], "layer", k) for k in range(1, layers)]
    next_rows = shifted(row_basis, "row", -1)
    applied = product(inverse_diag, right_side).astype(half)
    sketch, applied = lax.optimization_barrier((sketch, applied))
    core = project(right_factors[0], sketch).astype(half)
    cores = [core] + [rotated(core, "layer", k) for k in range(1, layers)]

    shift_t = project(applied, next_rows).astype(half).reshape(lowers, share, rank)
    weights = project(next_rows, inverse_diag)
    entry = lax.dynamic_slice_in_dim(incoming, lower * share, share, 1)
    place = upper.reshape(1)
    lefts[-1], shift_t, weights, entry, place = lax.optimization_barrier(
        (lefts[-1], shift_t, weights, entry, place)
    )
    tile_range, sent = local(
        lambda *refs: make_maps(layers, *refs),
        (*lefts, *cores, weights, shift_t),
        ((order, rank), half),
        ((lowers, rank + share, rank), half),
    )
    sent, tile_range, entry, place = lax.optimization_barrier((sent, tile_range, entry, place))
    steps = exchanged(sent, near)
    steps, tile_range, entry, place = lax.optimization_barrier((steps, tile_range, entry, place))
    values, last = local(
        first_half,
        (place, steps, entry),
        ((lowers, share, rank), jnp.float32),
        ((share, rank), half),
        scalar=True,
    )
    entered = shifted(last, "row", lowers)
    steps, tile_range, _ = lax.optimization_barrier((steps, tile_range, last))
    gain = product(inverse_diag, tile_range).astype(half)
    values, maps = local(
        second_half,
        (place, steps, values),
        ((lowers, share, rank), jnp.float32),
        ((lowers, rank, rank), half),
        scalar=True,
        aliases={2: 0},
    )
    gain, maps = lax.optimization_barrier((gain, maps))
    (coupled,) = local(enter, (entered, maps, values), ((lowers, share, rank), half))
    coupled = exchanged(coupled, near).reshape(width, rank)
    moved = lax.dot_general(gain, coupled, FLIPPED, preferred_element_type=jnp.float32)
    return (applied.astype(jnp.float32) - moved).astype(half)


def solution(mesh):
    return jax.shard_map(
        body,
        mesh=mesh,
        in_specs=(
            P("layer", "row", None),
            P("layer", "row", None),
            P("row", None),
            P("row", None),
            P("row", None),
            P("row", "layer"),
            P(None, "layer"),
        ),
        out_specs=P("row", "layer"),
        check_vma=False,
    )
```

```python
import jax
import jax.numpy as jnp
from jax import lax
from jax.experimental import pallas as pl
from jax.experimental.pallas import tpu as pltpu
from jax.sharding import PartitionSpec as P


def shifted(value, axis, steps):
    count = lax.axis_size(axis)
    leading, last = (max(0, -steps), min(count, count - steps))
    return lax.ppermute(value, axis, [(source, source + steps) for source in range(leading, last)])


def rotated(value, axis, steps):
    count = lax.axis_size(axis)
    return lax.ppermute(value, axis, [(source, (source + steps) % count) for source in range(count)])


def project(basis, vectors):
    return lax.dot_general(
        basis, vectors, (((0,), (0,)), ((), ())), preferred_element_type=jnp.float32
    )


def product(a, b):
    return jnp.dot(a, b, preferred_element_type=jnp.float32)


SMEM = pl.BlockSpec(memory_space=pltpu.SMEM)
VMEM = pl.BlockSpec(memory_space=pltpu.VMEM)
FLIPPED = (((1,), (1,)), ((), ()))


def split(value):
    high = value.astype(jnp.bfloat16)
    return high, (value - high.astype(jnp.float32)).astype(jnp.bfloat16)


def wide(value, matrix):
    both = product(jnp.concatenate(split(value)), matrix)
    return both[: value.shape[0]] + both[value.shape[0] :]


def use_basis(next_ref, inverse_ref, applied_ref, high_ref, low_ref, shift_ref):
    flipped = next_ref[...].T
    high_ref[...], low_ref[...] = split(product(flipped, inverse_ref[...]))
    shift_ref[...] = product(flipped, applied_ref[...]).T.astype(jnp.bfloat16)


def make_maps(layers, *refs):
    lefts = jnp.concatenate([ref[...] for ref in refs[:layers]], axis=1)
    cores = jnp.concatenate([ref[...] for ref in refs[layers : 2 * layers]], axis=0)
    high_ref, low_ref, shift_ref, range_ref, sent_ref = refs[2 * layers :]
    range_ref[...] = (-product(lefts, cores)).astype(jnp.bfloat16)
    parts = product(jnp.concatenate([high_ref[...], low_ref[...]]), lefts)
    rank = parts.shape[0] // 2
    map_t = wide(parts[:rank] + parts[rank:], cores).T.astype(jnp.bfloat16)
    share = sent_ref.shape[1] - rank
    for target in range(sent_ref.shape[0]):
        sent_ref[target, :rank] = map_t
        sent_ref[target, rank:] = shift_ref[target * share : (target + 1) * share]


def chain(steps_ref, state, values_ref):
    count, _, rank = steps_ref.shape
    for member in range(count):
        values_ref[member] = state
        state = wide(state, steps_ref[member, :rank])
        state = state + steps_ref[member, rank:].astype(jnp.float32)
    return state


def first_half(upper_ref, steps_ref, entry_ref, values_ref, last_ref):
    @pl.when(upper_ref[0] == 0)
    def _():
        last_ref[...] = chain(steps_ref, entry_ref[...].T, values_ref).astype(jnp.bfloat16)


def second_half(upper_ref, steps_ref, before_ref, values_ref, maps_ref):
    count, rank, _ = maps_ref.shape

    @pl.when(upper_ref[0] == 0)
    def _():
        maps_ref[...] = jnp.zeros(maps_ref.shape, jnp.bfloat16)

    @pl.when(upper_ref[0] > 0)
    def _():
        chain(steps_ref, jnp.zeros(values_ref.shape[1:], jnp.float32), values_ref)
        state = steps_ref[0, :rank]
        for member in range(1, count):
            maps_ref[member] = state
            if member + 1 < count:
                state = product(state, steps_ref[member, :rank]).astype(jnp.bfloat16)


def enter(entered_ref, maps_ref, values_ref, coupled_ref):
    entered = entered_ref[...]
    coupled_ref[0] = (entered.astype(jnp.float32) + values_ref[0]).astype(jnp.bfloat16)
    for member in range(1, coupled_ref.shape[0]):
        moved = product(entered, maps_ref[member])
        coupled_ref[member] = (moved + values_ref[member]).astype(jnp.bfloat16)


def local(kernel, inputs, *outputs, scalar=False, aliases={}):
    specs = [SMEM] * scalar + [VMEM] * (len(inputs) - scalar)
    return pl.pallas_call(
        kernel,
        in_specs=specs,
        out_specs=[VMEM] * len(outputs),
        out_shape=[jax.ShapeDtypeStruct(*output) for output in outputs],
        input_output_aliases=aliases,
        compiler_params=pltpu.CompilerParams(vmem_limit_bytes=16 * 2**20),
    )(*inputs)


def exchanged(blocks, members):
    return lax.all_to_all(blocks, "row", 0, 0, axis_index_groups=members, tiled=True)


def body(left_factors, right_factors, sketch, row_basis, inverse_diag, right_side, incoming):
    half = jnp.bfloat16
    order, rank = sketch.shape
    width = right_side.shape[1]
    layers, groups = lax.axis_size("layer"), lax.axis_size("row")
    lowers = groups // 2
    here = lax.axis_index("row")
    upper, lower = lax.div(here, lowers), lax.rem(here, lowers)
    share = width // lowers
    near = [list(range(lowers)), list(range(lowers, groups))]

    lefts = [left_factors[0]] + [rotated(left_factors[0], "layer", k) for k in range(1, layers)]
    next_rows = shifted(row_basis, "row", -1)
    applied = product(inverse_diag, right_side).astype(half)
    sketch, applied = lax.optimization_barrier((sketch, applied))
    core = project(right_factors[0], sketch).astype(half)
    cores = [core] + [rotated(core, "layer", k) for k in range(1, layers)]

    high, low, shift_t = local(
        use_basis,
        (next_rows, inverse_diag, applied),
        ((rank, order), half),
        ((rank, order), half),
        ((width, rank), half),
    )
    entry = lax.dynamic_slice_in_dim(incoming, lower * share, share, 1)
    place = upper.reshape(1)
    lefts[-1], shift_t, entry, place = lax.optimization_barrier(
        (lefts[-1], shift_t, entry, place)
    )
    tile_range, sent = local(
        lambda *refs: make_maps(layers, *refs),
        (*lefts, *cores, high, low, shift_t),
        ((order, rank), half),
        ((lowers, rank + share, rank), half),
    )
    sent, tile_range, entry, place = lax.optimization_barrier((sent, tile_range, entry, place))
    steps = exchanged(sent, near)
    steps, tile_range, entry, place = lax.optimization_barrier((steps, tile_range, entry, place))
    values, last = local(
        first_half,
        (place, steps, entry),
        ((lowers, share, rank), jnp.float32),
        ((share, rank), half),
        scalar=True,
    )
    entered = shifted(last, "row", lowers)
    steps, tile_range, _ = lax.optimization_barrier((steps, tile_range, last))
    gain = product(inverse_diag, tile_range).astype(half)
    values, maps = local(
        second_half,
        (place, steps, values),
        ((lowers, share, rank), jnp.float32),
        ((lowers, rank, rank), half),
        scalar=True,
        aliases={2: 0},
    )
    gain, maps = lax.optimization_barrier((gain, maps))
    (coupled,) = local(enter, (entered, maps, values), ((lowers, share, rank), half))
    coupled = exchanged(coupled, near).reshape(width, rank)
    moved = lax.dot_general(gain, coupled, FLIPPED, preferred_element_type=jnp.float32)
    return (applied.astype(jnp.float32) - moved).astype(half)


def solution(mesh):
    return jax.shard_map(
        body,
        mesh=mesh,
        in_specs=(
            P("layer", "row", None),
            P("layer", "row", None),
            P("row", None),
            P("row", None),
            P("row", None),
            P("row", "layer"),
            P(None, "layer"),
        ),
        out_specs=P("row", "layer"),
        check_vma=False,
    )
```

```python
import jax
import jax.numpy as jnp
from jax import lax
from jax.experimental import pallas as pl
from jax.experimental.pallas import tpu as pltpu
from jax.sharding import PartitionSpec as P


def shifted(value, axis, steps):
    count = lax.axis_size(axis)
    leading, last = (max(0, -steps), min(count, count - steps))
    return lax.ppermute(value, axis, [(source, source + steps) for source in range(leading, last)])


def rotated(value, axis, steps):
    count = lax.axis_size(axis)
    return lax.ppermute(value, axis, [(source, (source + steps) % count) for source in range(count)])


def project(basis, vectors):
    return lax.dot_general(
        basis, vectors, (((0,), (0,)), ((), ())), preferred_element_type=jnp.float32
    )


def product(a, b):
    return jnp.dot(a, b, preferred_element_type=jnp.float32)


SMEM = pl.BlockSpec(memory_space=pltpu.SMEM)
VMEM = pl.BlockSpec(memory_space=pltpu.VMEM)
FLIPPED = (((1,), (1,)), ((), ()))


def split(value):
    high = value.astype(jnp.bfloat16)
    return high, (value - high.astype(jnp.float32)).astype(jnp.bfloat16)


def wide(value, matrix):
    both = product(jnp.concatenate(split(value)), matrix)
    return both[: value.shape[0]] + both[value.shape[0] :]


def make_shift(next_ref, applied_ref, shift_ref):
    shift_ref[...] = project(next_ref[...], applied_ref[...]).T.astype(jnp.bfloat16)


def make_maps(layers, *refs):
    lefts = jnp.concatenate([ref[...] for ref in refs[:layers]], axis=1)
    cores = jnp.concatenate([ref[...] for ref in refs[layers : 2 * layers]], axis=0)
    weights_ref, shift_ref, range_ref, sent_ref = refs[2 * layers :]
    range_ref[...] = (-product(lefts, cores)).astype(jnp.bfloat16)
    map_t = wide(wide(weights_ref[...], lefts), cores).T.astype(jnp.bfloat16)
    rank = map_t.shape[0]
    share = sent_ref.shape[1] - rank
    for target in range(sent_ref.shape[0]):
        sent_ref[target, :rank] = map_t
        sent_ref[target, rank:] = shift_ref[target * share : (target + 1) * share]


def chain(steps_ref, state, values_ref):
    count, _, rank = steps_ref.shape
    for member in range(count):
        values_ref[member] = state
        state = wide(state, steps_ref[member, :rank])
        state = state + steps_ref[member, rank:].astype(jnp.float32)
    return state


def first_half(upper_ref, steps_ref, entry_ref, values_ref, last_ref):
    @pl.when(upper_ref[0] == 0)
    def _():
        last_ref[...] = chain(steps_ref, entry_ref[...].T, values_ref).astype(jnp.bfloat16)


def second_half(upper_ref, steps_ref, before_ref, values_ref, maps_ref):
    count, rank, _ = maps_ref.shape

    @pl.when(upper_ref[0] == 0)
    def _():
        maps_ref[...] = jnp.zeros(maps_ref.shape, jnp.bfloat16)

    @pl.when(upper_ref[0] > 0)
    def _():
        chain(steps_ref, jnp.zeros(values_ref.shape[1:], jnp.float32), values_ref)
        state = steps_ref[0, :rank]
        for member in range(1, count):
            maps_ref[member] = state
            if member + 1 < count:
                state = product(state, steps_ref[member, :rank]).astype(jnp.bfloat16)


def enter(entered_ref, maps_ref, values_ref, coupled_ref):
    entered = entered_ref[...]
    coupled_ref[0] = (entered.astype(jnp.float32) + values_ref[0]).astype(jnp.bfloat16)
    for member in range(1, coupled_ref.shape[0]):
        moved = product(entered, maps_ref[member])
        coupled_ref[member] = (moved + values_ref[member]).astype(jnp.bfloat16)


def local(kernel, inputs, *outputs, scalar=False, aliases={}):
    specs = [SMEM] * scalar + [VMEM] * (len(inputs) - scalar)
    return pl.pallas_call(
        kernel,
        in_specs=specs,
        out_specs=[VMEM] * len(outputs),
        out_shape=[jax.ShapeDtypeStruct(*output) for output in outputs],
        input_output_aliases=aliases,
        compiler_params=pltpu.CompilerParams(vmem_limit_bytes=16 * 2**20),
    )(*inputs)


def exchanged(blocks, members):
    return lax.all_to_all(blocks, "row", 0, 0, axis_index_groups=members, tiled=True)


def body(left_factors, right_factors, sketch, row_basis, inverse_diag, right_side, incoming):
    half = jnp.bfloat16
    order, rank = sketch.shape
    width = right_side.shape[1]
    layers, groups = lax.axis_size("layer"), lax.axis_size("row")
    lowers = groups // 2
    here = lax.axis_index("row")
    upper, lower = lax.div(here, lowers), lax.rem(here, lowers)
    share = width // lowers
    near = [list(range(lowers)), list(range(lowers, groups))]

    lefts = [left_factors[0]] + [rotated(left_factors[0], "layer", k) for k in range(1, layers)]
    next_rows = shifted(row_basis, "row", -1)
    applied = product(inverse_diag, right_side).astype(half)
    sketch, applied = lax.optimization_barrier((sketch, applied))
    core = project(right_factors[0], sketch).astype(half)
    cores = [core] + [rotated(core, "layer", k) for k in range(1, layers)]

    (shift_t,) = local(make_shift, (next_rows, applied), ((width, rank), half))
    weights = project(next_rows, inverse_diag)
    entry = lax.dynamic_slice_in_dim(incoming, lower * share, share, 1)
    place = upper.reshape(1)
    lefts[-1], shift_t, weights, entry, place = lax.optimization_barrier(
        (lefts[-1], shift_t, weights, entry, place)
    )
    tile_range, sent = local(
        lambda *refs: make_maps(layers, *refs),
        (*lefts, *cores, weights, shift_t),
        ((order, rank), half),
        ((lowers, rank + share, rank), half),
    )
    sent, tile_range, entry, place = lax.optimization_barrier((sent, tile_range, entry, place))
    steps = exchanged(sent, near)
    steps, tile_range, entry, place = lax.optimization_barrier((steps, tile_range, entry, place))
    values, last = local(
        first_half,
        (place, steps, entry),
        ((lowers, share, rank), jnp.float32),
        ((share, rank), half),
        scalar=True,
    )
    entered = shifted(last, "row", lowers)
    steps, tile_range, _ = lax.optimization_barrier((steps, tile_range, last))
    gain = product(inverse_diag, tile_range).astype(half)
    values, maps = local(
        second_half,
        (place, steps, values),
        ((lowers, share, rank), jnp.float32),
        ((lowers, rank, rank), half),
        scalar=True,
        aliases={2: 0},
    )
    gain, maps = lax.optimization_barrier((gain, maps))
    (coupled,) = local(enter, (entered, maps, values), ((lowers, share, rank), half))
    coupled = exchanged(coupled, near).reshape(width, rank)
    moved = lax.dot_general(gain, coupled, FLIPPED, preferred_element_type=jnp.float32)
    return (applied.astype(jnp.float32) - moved).astype(half)


def solution(mesh):
    return jax.shard_map(
        body,
        mesh=mesh,
        in_specs=(
            P("layer", "row", None),
            P("layer", "row", None),
            P("row", None),
            P("row", None),
            P("row", None),
            P("row", "layer"),
            P(None, "layer"),
        ),
        out_specs=P("row", "layer"),
        check_vma=False,
    )
```

```python
import jax
import jax.numpy as jnp
from jax import lax
from jax.experimental import pallas as pl
from jax.experimental.pallas import tpu as pltpu
from jax.sharding import PartitionSpec as P


def shifted(value, axis, steps):
    count = lax.axis_size(axis)
    leading, last = (max(0, -steps), min(count, count - steps))
    return lax.ppermute(value, axis, [(source, source + steps) for source in range(leading, last)])


def rotated(value, axis, steps):
    count = lax.axis_size(axis)
    return lax.ppermute(value, axis, [(source, (source + steps) % count) for source in range(count)])


def project(basis, vectors):
    return lax.dot_general(
        basis, vectors, (((0,), (0,)), ((), ())), preferred_element_type=jnp.float32
    )


def product(a, b):
    return jnp.dot(a, b, preferred_element_type=jnp.float32)


SMEM = pl.BlockSpec(memory_space=pltpu.SMEM)
VMEM = pl.BlockSpec(memory_space=pltpu.VMEM)
FLIPPED = (((1,), (1,)), ((), ()))


def split(value):
    high = value.astype(jnp.bfloat16)
    return high, (value - high.astype(jnp.float32)).astype(jnp.bfloat16)


def wide(value, matrix):
    both = product(jnp.concatenate(split(value)), matrix)
    return both[: value.shape[0]] + both[value.shape[0] :]


def make_shift(next_ref, applied_ref, shift_ref):
    shift_ref[...] = project(next_ref[...], applied_ref[...]).T.astype(jnp.bfloat16)


def make_maps(layers, *refs):
    lefts = jnp.concatenate([ref[...] for ref in refs[:layers]], axis=1)
    cores = jnp.concatenate([ref[...] for ref in refs[layers : 2 * layers]], axis=0)
    weights_ref, shift_ref, range_ref, sent_ref = refs[2 * layers :]
    range_ref[...] = (-product(lefts, cores)).astype(jnp.bfloat16)
    map_t = wide(wide(weights_ref[...], lefts), cores).T.astype(jnp.bfloat16)
    rank = map_t.shape[0]
    share = sent_ref.shape[1] - rank
    for target in range(sent_ref.shape[0]):
        sent_ref[target, :rank] = map_t
        sent_ref[target, rank:] = shift_ref[target * share : (target + 1) * share]


def chain(steps_ref, state, values_ref):
    count, _, rank = steps_ref.shape
    for member in range(count):
        values_ref[member] = state
        state = wide(state, steps_ref[member, :rank])
        state = state + steps_ref[member, rank:].astype(jnp.float32)
    return state


def first_half(upper_ref, steps_ref, entry_ref, values_ref, last_ref):
    @pl.when(upper_ref[0] == 0)
    def _():
        last_ref[...] = chain(steps_ref, entry_ref[...].T, values_ref).astype(jnp.bfloat16)


def second_half(upper_ref, steps_ref, before_ref, values_ref, maps_ref):
    count, rank, _ = maps_ref.shape

    @pl.when(upper_ref[0] == 0)
    def _():
        maps_ref[...] = jnp.zeros(maps_ref.shape, jnp.bfloat16)

    @pl.when(upper_ref[0] > 0)
    def _():
        chain(steps_ref, jnp.zeros(values_ref.shape[1:], jnp.float32), values_ref)
        state = steps_ref[0, :rank]
        for member in range(1, count):
            maps_ref[member] = state
            if member + 1 < count:
                state = product(state, steps_ref[member, :rank]).astype(jnp.bfloat16)


def enter(entered_ref, maps_ref, values_ref, coupled_ref):
    entered = entered_ref[...]
    coupled_ref[0] = (entered.astype(jnp.float32) + values_ref[0]).astype(jnp.bfloat16)
    for member in range(1, coupled_ref.shape[0]):
        moved = product(entered, maps_ref[member])
        coupled_ref[member] = (moved + values_ref[member]).astype(jnp.bfloat16)


def local(kernel, inputs, *outputs, scalar=False, aliases={}):
    specs = [SMEM] * scalar + [VMEM] * (len(inputs) - scalar)
    return pl.pallas_call(
        kernel,
        in_specs=specs,
        out_specs=[VMEM] * len(outputs),
        out_shape=[jax.ShapeDtypeStruct(*output) for output in outputs],
        input_output_aliases=aliases,
        compiler_params=pltpu.CompilerParams(vmem_limit_bytes=6 * 2**20),
    )(*inputs)


def exchanged(blocks, members):
    return lax.all_to_all(blocks, "row", 0, 0, axis_index_groups=members, tiled=True)


def body(left_factors, right_factors, sketch, row_basis, inverse_diag, right_side, incoming):
    half = jnp.bfloat16
    order, rank = sketch.shape
    width = right_side.shape[1]
    layers, groups = lax.axis_size("layer"), lax.axis_size("row")
    lowers = groups // 2
    here = lax.axis_index("row")
    upper, lower = lax.div(here, lowers), lax.rem(here, lowers)
    share = width // lowers
    near = [list(range(lowers)), list(range(lowers, groups))]

    lefts = [left_factors[0]] + [rotated(left_factors[0], "layer", k) for k in range(1, layers)]
    next_rows = shifted(row_basis, "row", -1)
    applied = product(inverse_diag, right_side).astype(half)
    sketch, applied = lax.optimization_barrier((sketch, applied))
    core = project(right_factors[0], sketch).astype(half)
    cores = [core] + [rotated(core, "layer", k) for k in range(1, layers)]

    (shift_t,) = local(make_shift, (next_rows, applied), ((width, rank), half))
    weights = project(next_rows, inverse_diag)
    entry = lax.dynamic_slice_in_dim(incoming, lower * share, share, 1)
    place = upper.reshape(1)
    lefts[-1], shift_t, weights, entry, place = lax.optimization_barrier(
        (lefts[-1], shift_t, weights, entry, place)
    )
    tile_range, sent = local(
        lambda *refs: make_maps(layers, *refs),
        (*lefts, *cores, weights, shift_t),
        ((order, rank), half),
        ((lowers, rank + share, rank), half),
    )
    sent, tile_range, entry, place = lax.optimization_barrier((sent, tile_range, entry, place))
    steps = exchanged(sent, near)
    steps, tile_range, entry, place = lax.optimization_barrier((steps, tile_range, entry, place))
    values, last = local(
        first_half,
        (place, steps, entry),
        ((lowers, share, rank), jnp.float32),
        ((share, rank), half),
        scalar=True,
    )
    entered = shifted(last, "row", lowers)
    steps, tile_range, _ = lax.optimization_barrier((steps, tile_range, last))
    gain = product(inverse_diag, tile_range).astype(half)
    values, maps = local(
        second_half,
        (place, steps, values),
        ((lowers, share, rank), jnp.float32),
        ((lowers, rank, rank), half),
        scalar=True,
        aliases={2: 0},
    )
    gain, maps = lax.optimization_barrier((gain, maps))
    (coupled,) = local(enter, (entered, maps, values), ((lowers, share, rank), half))
    coupled = exchanged(coupled, near).reshape(width, rank)
    moved = lax.dot_general(gain, coupled, FLIPPED, preferred_element_type=jnp.float32)
    return (applied.astype(jnp.float32) - moved).astype(half)


def solution(mesh):
    return jax.shard_map(
        body,
        mesh=mesh,
        in_specs=(
            P("layer", "row", None),
            P("layer", "row", None),
            P("row", None),
            P("row", None),
            P("row", None),
            P("row", "layer"),
            P(None, "layer"),
        ),
        out_specs=P("row", "layer"),
        check_vma=False,
    )
```

```python
import jax
import jax.numpy as jnp
from jax import lax
from jax.experimental import pallas as pl
from jax.experimental.pallas import tpu as pltpu
from jax.sharding import PartitionSpec as P


def shifted(value, axis, steps):
    count = lax.axis_size(axis)
    leading, last = (max(0, -steps), min(count, count - steps))
    return lax.ppermute(value, axis, [(source, source + steps) for source in range(leading, last)])


def rotated(value, axis, steps):
    count = lax.axis_size(axis)
    return lax.ppermute(value, axis, [(source, (source + steps) % count) for source in range(count)])


def project(basis, vectors):
    return lax.dot_general(
        basis, vectors, (((0,), (0,)), ((), ())), preferred_element_type=jnp.float32
    )


def product(a, b):
    return jnp.dot(a, b, preferred_element_type=jnp.float32)


SMEM = pl.BlockSpec(memory_space=pltpu.SMEM)
VMEM = pl.BlockSpec(memory_space=pltpu.VMEM)
FLIPPED = (((1,), (1,)), ((), ()))


def split(value):
    high = value.astype(jnp.bfloat16)
    return high, (value - high.astype(jnp.float32)).astype(jnp.bfloat16)


def wide(value, matrix):
    both = product(jnp.concatenate(split(value)), matrix)
    return both[: value.shape[0]] + both[value.shape[0] :]


def make_shift(next_ref, applied_ref, shift_ref):
    shift_ref[...] = project(next_ref[...], applied_ref[...]).T.astype(jnp.bfloat16)


def lay(*refs):
    rank = refs[0].shape[1]
    for layer, ref in enumerate(refs[:-1]):
        refs[-1][:, layer * rank : (layer + 1) * rank] = ref[...]


def make_maps(layers, *refs):
    cores = jnp.concatenate([ref[...] for ref in refs[:layers]], axis=0)
    lefts_ref, weights_ref, shift_ref, range_ref, sent_ref = refs[layers:]
    lefts = lefts_ref[...]
    range_ref[...] = (-product(lefts, cores)).astype(jnp.bfloat16)
    map_t = wide(wide(weights_ref[...], lefts), cores).T.astype(jnp.bfloat16)
    rank = map_t.shape[0]
    share = sent_ref.shape[1] - rank
    for target in range(sent_ref.shape[0]):
        sent_ref[target, :rank] = map_t
        sent_ref[target, rank:] = shift_ref[target * share : (target + 1) * share]


def chain(steps_ref, state, values_ref):
    count, _, rank = steps_ref.shape
    for member in range(count):
        values_ref[member] = state
        state = wide(state, steps_ref[member, :rank])
        state = state + steps_ref[member, rank:].astype(jnp.float32)
    return state


def first_half(upper_ref, steps_ref, entry_ref, values_ref, last_ref):
    @pl.when(upper_ref[0] == 0)
    def _():
        last_ref[...] = chain(steps_ref, entry_ref[...].T, values_ref).astype(jnp.bfloat16)


def second_half(upper_ref, steps_ref, before_ref, values_ref, maps_ref):
    count, rank, _ = maps_ref.shape

    @pl.when(upper_ref[0] == 0)
    def _():
        maps_ref[...] = jnp.zeros(maps_ref.shape, jnp.bfloat16)

    @pl.when(upper_ref[0] > 0)
    def _():
        chain(steps_ref, jnp.zeros(values_ref.shape[1:], jnp.float32), values_ref)
        state = steps_ref[0, :rank]
        for member in range(1, count):
            maps_ref[member] = state
            if member + 1 < count:
                state = product(state, steps_ref[member, :rank]).astype(jnp.bfloat16)


def enter(entered_ref, maps_ref, values_ref, coupled_ref):
    entered = entered_ref[...]
    coupled_ref[0] = (entered.astype(jnp.float32) + values_ref[0]).astype(jnp.bfloat16)
    for member in range(1, coupled_ref.shape[0]):
        moved = product(entered, maps_ref[member])
        coupled_ref[member] = (moved + values_ref[member]).astype(jnp.bfloat16)


def local(kernel, inputs, *outputs, scalar=False, aliases={}):
    specs = [SMEM] * scalar + [VMEM] * (len(inputs) - scalar)
    return pl.pallas_call(
        kernel,
        in_specs=specs,
        out_specs=[VMEM] * len(outputs),
        out_shape=[jax.ShapeDtypeStruct(*output) for output in outputs],
        input_output_aliases=aliases,
        compiler_params=pltpu.CompilerParams(vmem_limit_bytes=16 * 2**20),
    )(*inputs)


def exchanged(blocks, members):
    return lax.all_to_all(blocks, "row", 0, 0, axis_index_groups=members, tiled=True)


def body(left_factors, right_factors, sketch, row_basis, inverse_diag, right_side, incoming):
    half = jnp.bfloat16
    order, rank = sketch.shape
    width = right_side.shape[1]
    layers, groups = lax.axis_size("layer"), lax.axis_size("row")
    lowers = groups // 2
    here = lax.axis_index("row")
    upper, lower = lax.div(here, lowers), lax.rem(here, lowers)
    share = width // lowers
    near = [list(range(lowers)), list(range(lowers, groups))]

    lefts = [left_factors[0]] + [rotated(left_factors[0], "layer", k) for k in range(1, layers)]
    next_rows = shifted(row_basis, "row", -1)
    applied = product(inverse_diag, right_side).astype(half)
    sketch, applied = lax.optimization_barrier((sketch, applied))
    core = project(right_factors[0], sketch).astype(half)
    cores = [core] + [rotated(core, "layer", k) for k in range(1, layers)]

    (side,) = local(lay, lefts, ((order, layers * rank), half))
    next_rows, side = lax.optimization_barrier((next_rows, side))
    (shift_t,) = local(make_shift, (next_rows, applied), ((width, rank), half))
    weights = project(next_rows, inverse_diag)
    entry = lax.dynamic_slice_in_dim(incoming, lower * share, share, 1)
    place = upper.reshape(1)
    side, shift_t, weights, entry, place = lax.optimization_barrier(
        (side, shift_t, weights, entry, place)
    )
    tile_range, sent = local(
        lambda *refs: make_maps(layers, *refs),
        (*cores, side, weights, shift_t),
        ((order, rank), half),
        ((lowers, rank + share, rank), half),
    )
    sent, tile_range, entry, place = lax.optimization_barrier((sent, tile_range, entry, place))
    steps = exchanged(sent, near)
    steps, tile_range, entry, place = lax.optimization_barrier((steps, tile_range, entry, place))
    values, last = local(
        first_half,
        (place, steps, entry),
        ((lowers, share, rank), jnp.float32),
        ((share, rank), half),
        scalar=True,
    )
    entered = shifted(last, "row", lowers)
    steps, tile_range, _ = lax.optimization_barrier((steps, tile_range, last))
    gain = product(inverse_diag, tile_range).astype(half)
    values, maps = local(
        second_half,
        (place, steps, values),
        ((lowers, share, rank), jnp.float32),
        ((lowers, rank, rank), half),
        scalar=True,
        aliases={2: 0},
    )
    gain, maps = lax.optimization_barrier((gain, maps))
    (coupled,) = local(enter, (entered, maps, values), ((lowers, share, rank), half))
    coupled = exchanged(coupled, near).reshape(width, rank)
    moved = lax.dot_general(gain, coupled, FLIPPED, preferred_element_type=jnp.float32)
    return (applied.astype(jnp.float32) - moved).astype(half)


def solution(mesh):
    return jax.shard_map(
        body,
        mesh=mesh,
        in_specs=(
            P("layer", "row", None),
            P("layer", "row", None),
            P("row", None),
            P("row", None),
            P("row", None),
            P("row", "layer"),
            P(None, "layer"),
        ),
        out_specs=P("row", "layer"),
        check_vma=False,
    )
```

```python
import jax
import jax.numpy as jnp
from jax import lax
from jax.experimental import pallas as pl
from jax.experimental.pallas import tpu as pltpu
from jax.sharding import PartitionSpec as P


def shifted(value, axis, steps):
    count = lax.axis_size(axis)
    leading, last = (max(0, -steps), min(count, count - steps))
    return lax.ppermute(value, axis, [(source, source + steps) for source in range(leading, last)])


def rotated(value, axis, steps):
    count = lax.axis_size(axis)
    return lax.ppermute(value, axis, [(source, (source + steps) % count) for source in range(count)])


def project(basis, vectors):
    return lax.dot_general(
        basis, vectors, (((0,), (0,)), ((), ())), preferred_element_type=jnp.float32
    )


def product(a, b):
    return jnp.dot(a, b, preferred_element_type=jnp.float32)


SMEM = pl.BlockSpec(memory_space=pltpu.SMEM)
VMEM = pl.BlockSpec(memory_space=pltpu.VMEM)
FLIPPED = (((1,), (1,)), ((), ()))


def split(value):
    high = value.astype(jnp.bfloat16)
    return high, (value - high.astype(jnp.float32)).astype(jnp.bfloat16)


def wide(value, matrix):
    both = product(jnp.concatenate(split(value)), matrix)
    return both[: value.shape[0]] + both[value.shape[0] :]


def make_shift(next_ref, applied_ref, shift_ref):
    shift_ref[...] = project(next_ref[...], applied_ref[...]).T.astype(jnp.bfloat16)


def lay(*refs):
    rank = refs[0].shape[1]
    for layer, ref in enumerate(refs[:-1]):
        refs[-1][:, layer * rank : (layer + 1) * rank] = ref[...]


def make_maps(layers, *refs):
    cores = jnp.concatenate([ref[...] for ref in refs[:layers]], axis=0)
    left_ref, others_ref, weights_ref, shift_ref, range_ref, sent_ref = refs[layers:]
    lefts = jnp.concatenate([left_ref[...], others_ref[...]], axis=1)
    range_ref[...] = (-product(lefts, cores)).astype(jnp.bfloat16)
    map_t = wide(wide(weights_ref[...], lefts), cores).T.astype(jnp.bfloat16)
    rank = map_t.shape[0]
    share = sent_ref.shape[1] - rank
    for target in range(sent_ref.shape[0]):
        sent_ref[target, :rank] = map_t
        sent_ref[target, rank:] = shift_ref[target * share : (target + 1) * share]


def chain(steps_ref, state, values_ref):
    count, _, rank = steps_ref.shape
    for member in range(count):
        values_ref[member] = state
        state = wide(state, steps_ref[member, :rank])
        state = state + steps_ref[member, rank:].astype(jnp.float32)
    return state


def first_half(upper_ref, steps_ref, entry_ref, values_ref, last_ref):
    @pl.when(upper_ref[0] == 0)
    def _():
        last_ref[...] = chain(steps_ref, entry_ref[...].T, values_ref).astype(jnp.bfloat16)


def second_half(upper_ref, steps_ref, before_ref, values_ref, maps_ref):
    count, rank, _ = maps_ref.shape

    @pl.when(upper_ref[0] == 0)
    def _():
        maps_ref[...] = jnp.zeros(maps_ref.shape, jnp.bfloat16)

    @pl.when(upper_ref[0] > 0)
    def _():
        chain(steps_ref, jnp.zeros(values_ref.shape[1:], jnp.float32), values_ref)
        state = steps_ref[0, :rank]
        for member in range(1, count):
            maps_ref[member] = state
            if member + 1 < count:
                state = product(state, steps_ref[member, :rank]).astype(jnp.bfloat16)


def enter(entered_ref, maps_ref, values_ref, coupled_ref):
    entered = entered_ref[...]
    coupled_ref[0] = (entered.astype(jnp.float32) + values_ref[0]).astype(jnp.bfloat16)
    for member in range(1, coupled_ref.shape[0]):
        moved = product(entered, maps_ref[member])
        coupled_ref[member] = (moved + values_ref[member]).astype(jnp.bfloat16)


def local(kernel, inputs, *outputs, scalar=False, aliases={}):
    specs = [SMEM] * scalar + [VMEM] * (len(inputs) - scalar)
    return pl.pallas_call(
        kernel,
        in_specs=specs,
        out_specs=[VMEM] * len(outputs),
        out_shape=[jax.ShapeDtypeStruct(*output) for output in outputs],
        input_output_aliases=aliases,
        compiler_params=pltpu.CompilerParams(vmem_limit_bytes=16 * 2**20),
    )(*inputs)


def exchanged(blocks, members):
    return lax.all_to_all(blocks, "row", 0, 0, axis_index_groups=members, tiled=True)


def body(left_factors, right_factors, sketch, row_basis, inverse_diag, right_side, incoming):
    half = jnp.bfloat16
    order, rank = sketch.shape
    width = right_side.shape[1]
    layers, groups = lax.axis_size("layer"), lax.axis_size("row")
    lowers = groups // 2
    here = lax.axis_index("row")
    upper, lower = lax.div(here, lowers), lax.rem(here, lowers)
    share = width // lowers
    near = [list(range(lowers)), list(range(lowers, groups))]

    lefts = [left_factors[0]] + [rotated(left_factors[0], "layer", k) for k in range(1, layers)]
    next_rows = shifted(row_basis, "row", -1)
    applied = product(inverse_diag, right_side).astype(half)
    sketch, applied = lax.optimization_barrier((sketch, applied))
    core = project(right_factors[0], sketch).astype(half)
    cores = [core] + [rotated(core, "layer", k) for k in range(1, layers)]

    (others,) = local(lay, lefts[1:], ((order, (layers - 1) * rank), half))
    next_rows, others = lax.optimization_barrier((next_rows, others))
    (shift_t,) = local(make_shift, (next_rows, applied), ((width, rank), half))
    weights = project(next_rows, inverse_diag)
    entry = lax.dynamic_slice_in_dim(incoming, lower * share, share, 1)
    place = upper.reshape(1)
    others, shift_t, weights, entry, place = lax.optimization_barrier(
        (others, shift_t, weights, entry, place)
    )
    tile_range, sent = local(
        lambda *refs: make_maps(layers, *refs),
        (*cores, lefts[0], others, weights, shift_t),
        ((order, rank), half),
        ((lowers, rank + share, rank), half),
    )
    sent, tile_range, entry, place = lax.optimization_barrier((sent, tile_range, entry, place))
    steps = exchanged(sent, near)
    steps, tile_range, entry, place = lax.optimization_barrier((steps, tile_range, entry, place))
    values, last = local(
        first_half,
        (place, steps, entry),
        ((lowers, share, rank), jnp.float32),
        ((share, rank), half),
        scalar=True,
    )
    entered = shifted(last, "row", lowers)
    steps, tile_range, _ = lax.optimization_barrier((steps, tile_range, last))
    gain = product(inverse_diag, tile_range).astype(half)
    values, maps = local(
        second_half,
        (place, steps, values),
        ((lowers, share, rank), jnp.float32),
        ((lowers, rank, rank), half),
        scalar=True,
        aliases={2: 0},
    )
    gain, maps = lax.optimization_barrier((gain, maps))
    (coupled,) = local(enter, (entered, maps, values), ((lowers, share, rank), half))
    coupled = exchanged(coupled, near).reshape(width, rank)
    moved = lax.dot_general(gain, coupled, FLIPPED, preferred_element_type=jnp.float32)
    return (applied.astype(jnp.float32) - moved).astype(half)


def solution(mesh):
    return jax.shard_map(
        body,
        mesh=mesh,
        in_specs=(
            P("layer", "row", None),
            P("layer", "row", None),
            P("row", None),
            P("row", None),
            P("row", None),
            P("row", "layer"),
            P(None, "layer"),
        ),
        out_specs=P("row", "layer"),
        check_vma=False,
    )
```

```python
import jax
import jax.numpy as jnp
from jax import lax
from jax.experimental import pallas as pl
from jax.experimental.pallas import tpu as pltpu
from jax.sharding import PartitionSpec as P


def shifted(value, axis, steps):
    count = lax.axis_size(axis)
    leading, last = (max(0, -steps), min(count, count - steps))
    return lax.ppermute(value, axis, [(source, source + steps) for source in range(leading, last)])


def rotated(value, axis, steps):
    count = lax.axis_size(axis)
    return lax.ppermute(value, axis, [(source, (source + steps) % count) for source in range(count)])


def project(basis, vectors):
    return lax.dot_general(
        basis, vectors, (((0,), (0,)), ((), ())), preferred_element_type=jnp.float32
    )


def product(a, b):
    return jnp.dot(a, b, preferred_element_type=jnp.float32)


SMEM = pl.BlockSpec(memory_space=pltpu.SMEM)
VMEM = pl.BlockSpec(memory_space=pltpu.VMEM)
FLIPPED = (((1,), (1,)), ((), ()))


def split(value):
    high = value.astype(jnp.bfloat16)
    return high, (value - high.astype(jnp.float32)).astype(jnp.bfloat16)


def wide(value, matrix):
    both = product(jnp.concatenate(split(value)), matrix)
    return both[: value.shape[0]] + both[value.shape[0] :]


def make_maps(layers, *refs):
    lefts = jnp.concatenate([ref[...] for ref in refs[:layers]], axis=1)
    cores = jnp.concatenate([ref[...] for ref in refs[layers : 2 * layers]], axis=0)
    weights_ref, shift_ref, range_ref, sent_ref = refs[2 * layers :]
    range_ref[...] = (-product(lefts, cores)).astype(jnp.bfloat16)
    map_t = wide(wide(weights_ref[...], lefts), cores).T.astype(jnp.bfloat16)
    rank = map_t.shape[0]
    for target in range(sent_ref.shape[0]):
        sent_ref[target, :rank] = map_t
        sent_ref[target, rank:] = shift_ref[target]


def chain(steps_ref, state, values_ref):
    count, _, rank = steps_ref.shape
    for member in range(count):
        values_ref[member] = state
        state = wide(state, steps_ref[member, :rank])
        state = state + steps_ref[member, rank:].astype(jnp.float32)
    return state


def first_half(place_ref, steps_ref, incoming_ref, values_ref, last_ref, flipped):
    share = last_ref.shape[0]

    @pl.when(place_ref[0] == 0)
    def _():
        flipped[...] = incoming_ref[...].T
        entry = flipped[pl.ds(pl.multiple_of(place_ref[1] * share, share), share), :]
        last_ref[...] = chain(steps_ref, entry, values_ref).astype(jnp.bfloat16)


def second_half(upper_ref, steps_ref, before_ref, values_ref, maps_ref):
    count, rank, _ = maps_ref.shape

    @pl.when(upper_ref[0] == 0)
    def _():
        maps_ref[...] = jnp.zeros(maps_ref.shape, jnp.bfloat16)

    @pl.when(upper_ref[0] > 0)
    def _():
        chain(steps_ref, jnp.zeros(values_ref.shape[1:], jnp.float32), values_ref)
        state = steps_ref[0, :rank]
        for member in range(1, count):
            maps_ref[member] = state
            if member + 1 < count:
                state = product(state, steps_ref[member, :rank]).astype(jnp.bfloat16)


def enter(entered_ref, maps_ref, values_ref, coupled_ref):
    entered = entered_ref[...]
    coupled_ref[0] = (entered.astype(jnp.float32) + values_ref[0]).astype(jnp.bfloat16)
    for member in range(1, coupled_ref.shape[0]):
        moved = product(entered, maps_ref[member])
        coupled_ref[member] = (moved + values_ref[member]).astype(jnp.bfloat16)


def local(kernel, inputs, *outputs, scalar=False, aliases={}, scratch=()):
    specs = [SMEM] * scalar + [VMEM] * (len(inputs) - scalar)
    return pl.pallas_call(
        kernel,
        in_specs=specs,
        out_specs=[VMEM] * len(outputs),
        out_shape=[jax.ShapeDtypeStruct(*output) for output in outputs],
        input_output_aliases=aliases,
        scratch_shapes=scratch,
        compiler_params=pltpu.CompilerParams(vmem_limit_bytes=16 * 2**20),
    )(*inputs)


def exchanged(blocks, members):
    return lax.all_to_all(blocks, "row", 0, 0, axis_index_groups=members, tiled=True)


def body(left_factors, right_factors, sketch, row_basis, inverse_diag, right_side, incoming):
    half = jnp.bfloat16
    order, rank = sketch.shape
    width = right_side.shape[1]
    layers, groups = lax.axis_size("layer"), lax.axis_size("row")
    lowers = groups // 2
    here = lax.axis_index("row")
    upper, lower = lax.div(here, lowers), lax.rem(here, lowers)
    share = width // lowers
    near = [list(range(lowers)), list(range(lowers, groups))]

    lefts = [left_factors[0]] + [rotated(left_factors[0], "layer", k) for k in range(1, layers)]
    next_rows = shifted(row_basis, "row", -1)
    applied = product(inverse_diag, right_side).astype(half)
    sketch, applied = lax.optimization_barrier((sketch, applied))
    core = project(right_factors[0], sketch).astype(half)
    cores = [core] + [rotated(core, "layer", k) for k in range(1, layers)]

    shift_t = project(applied, next_rows).astype(half).reshape(lowers, share, rank)
    weights = project(next_rows, inverse_diag)
    place = jnp.stack([upper, lower])
    lefts[-1], shift_t, weights, place = lax.optimization_barrier(
        (lefts[-1], shift_t, weights, place)
    )
    tile_range, sent = local(
        lambda *refs: make_maps(layers, *refs),
        (*lefts, *cores, weights, shift_t),
        ((order, rank), half),
        ((lowers, rank + share, rank), half),
    )
    sent, tile_range, place = lax.optimization_barrier((sent, tile_range, place))
    steps = exchanged(sent, near)
    steps, tile_range, place = lax.optimization_barrier((steps, tile_range, place))
    values, last = local(
        first_half,
        (place, steps, incoming),
        ((lowers, share, rank), jnp.float32),
        ((share, rank), half),
        scalar=True,
        scratch=[pltpu.VMEM((width, rank), jnp.float32)],
    )
    entered = shifted(last, "row", lowers)
    steps, tile_range, _ = lax.optimization_barrier((steps, tile_range, last))
    gain = product(inverse_diag, tile_range).astype(half)
    values, maps = local(
        second_half,
        (place, steps, values),
        ((lowers, share, rank), jnp.float32),
        ((lowers, rank, rank), half),
        scalar=True,
        aliases={2: 0},
    )
    gain, maps = lax.optimization_barrier((gain, maps))
    (coupled,) = local(enter, (entered, maps, values), ((lowers, share, rank), half))
    coupled = exchanged(coupled, near).reshape(width, rank)
    moved = lax.dot_general(gain, coupled, FLIPPED, preferred_element_type=jnp.float32)
    return (applied.astype(jnp.float32) - moved).astype(half)


def solution(mesh):
    return jax.shard_map(
        body,
        mesh=mesh,
        in_specs=(
            P("layer", "row", None),
            P("layer", "row", None),
            P("row", None),
            P("row", None),
            P("row", None),
            P("row", "layer"),
            P(None, "layer"),
        ),
        out_specs=P("row", "layer"),
        check_vma=False,
    )
```

```python
import jax
import jax.numpy as jnp
from jax import lax
from jax.experimental import pallas as pl
from jax.experimental.pallas import tpu as pltpu
from jax.sharding import PartitionSpec as P


def shifted(value, axis, steps):
    count = lax.axis_size(axis)
    leading, last = (max(0, -steps), min(count, count - steps))
    return lax.ppermute(value, axis, [(source, source + steps) for source in range(leading, last)])


def rotated(value, axis, steps):
    count = lax.axis_size(axis)
    return lax.ppermute(value, axis, [(source, (source + steps) % count) for source in range(count)])


def project(basis, vectors):
    return lax.dot_general(
        basis, vectors, (((0,), (0,)), ((), ())), preferred_element_type=jnp.float32
    )


def product(a, b):
    return jnp.dot(a, b, preferred_element_type=jnp.float32)


SMEM = pl.BlockSpec(memory_space=pltpu.SMEM)
VMEM = pl.BlockSpec(memory_space=pltpu.VMEM)
FLIPPED = (((1,), (1,)), ((), ()))


def split(value):
    high = value.astype(jnp.bfloat16)
    return high, (value - high.astype(jnp.float32)).astype(jnp.bfloat16)


def wide(value, matrix):
    both = product(jnp.concatenate(split(value)), matrix)
    return both[: value.shape[0]] + both[value.shape[0] :]


def make_shift(next_ref, applied_ref, shift_ref):
    shift_ref[...] = project(next_ref[...], applied_ref[...]).T.astype(jnp.bfloat16)


def lay(*refs):
    arrived, target, sources = refs[-1], refs[-2], refs[:-2]
    rank = sources[0].shape[1]
    copies = [
        pltpu.make_async_copy(source, target.at[:, pl.ds(k * rank, rank)], arrived.at[k])
        for k, source in enumerate(sources)
    ]
    for copy in copies:
        copy.start()
    for copy in copies:
        copy.wait()


def make_maps(layers, *refs):
    cores = jnp.concatenate([ref[...] for ref in refs[:layers]], axis=0)
    left_ref, others_ref, weights_ref, shift_ref, range_ref, sent_ref = refs[layers:]
    lefts = jnp.concatenate([left_ref[...], others_ref[...]], axis=1)
    range_ref[...] = (-product(lefts, cores)).astype(jnp.bfloat16)
    map_t = wide(wide(weights_ref[...], lefts), cores).T.astype(jnp.bfloat16)
    rank = map_t.shape[0]
    share = sent_ref.shape[1] - rank
    for target in range(sent_ref.shape[0]):
        sent_ref[target, :rank] = map_t
        sent_ref[target, rank:] = shift_ref[target * share : (target + 1) * share]


def chain(steps_ref, state, values_ref):
    count, _, rank = steps_ref.shape
    for member in range(count):
        values_ref[member] = state
        state = wide(state, steps_ref[member, :rank])
        state = state + steps_ref[member, rank:].astype(jnp.float32)
    return state


def first_half(upper_ref, steps_ref, entry_ref, values_ref, last_ref):
    @pl.when(upper_ref[0] == 0)
    def _():
        last_ref[...] = chain(steps_ref, entry_ref[...].T, values_ref).astype(jnp.bfloat16)


def second_half(upper_ref, steps_ref, before_ref, values_ref, maps_ref):
    count, rank, _ = maps_ref.shape

    @pl.when(upper_ref[0] == 0)
    def _():
        maps_ref[...] = jnp.zeros(maps_ref.shape, jnp.bfloat16)

    @pl.when(upper_ref[0] > 0)
    def _():
        chain(steps_ref, jnp.zeros(values_ref.shape[1:], jnp.float32), values_ref)
        state = steps_ref[0, :rank]
        for member in range(1, count):
            maps_ref[member] = state
            if member + 1 < count:
                state = product(state, steps_ref[member, :rank]).astype(jnp.bfloat16)


def enter(entered_ref, maps_ref, values_ref, coupled_ref):
    entered = entered_ref[...]
    coupled_ref[0] = (entered.astype(jnp.float32) + values_ref[0]).astype(jnp.bfloat16)
    for member in range(1, coupled_ref.shape[0]):
        moved = product(entered, maps_ref[member])
        coupled_ref[member] = (moved + values_ref[member]).astype(jnp.bfloat16)


def local(kernel, inputs, *outputs, scalar=False, aliases={}):
    specs = [SMEM] * scalar + [VMEM] * (len(inputs) - scalar)
    return pl.pallas_call(
        kernel,
        in_specs=specs,
        out_specs=[VMEM] * len(outputs),
        out_shape=[jax.ShapeDtypeStruct(*output) for output in outputs],
        input_output_aliases=aliases,
        compiler_params=pltpu.CompilerParams(vmem_limit_bytes=16 * 2**20),
    )(*inputs)


def exchanged(blocks, members):
    return lax.all_to_all(blocks, "row", 0, 0, axis_index_groups=members, tiled=True)


def body(left_factors, right_factors, sketch, row_basis, inverse_diag, right_side, incoming):
    half = jnp.bfloat16
    order, rank = sketch.shape
    width = right_side.shape[1]
    layers, groups = lax.axis_size("layer"), lax.axis_size("row")
    lowers = groups // 2
    here = lax.axis_index("row")
    upper, lower = lax.div(here, lowers), lax.rem(here, lowers)
    share = width // lowers
    near = [list(range(lowers)), list(range(lowers, groups))]

    lefts = [left_factors[0]] + [rotated(left_factors[0], "layer", k) for k in range(1, layers)]
    next_rows = shifted(row_basis, "row", -1)
    applied = product(inverse_diag, right_side).astype(half)
    sketch, applied = lax.optimization_barrier((sketch, applied))
    core = project(right_factors[0], sketch).astype(half)
    cores = [core] + [rotated(core, "layer", k) for k in range(1, layers)]

    others = pl.pallas_call(
        lay,
        in_specs=[pl.BlockSpec(memory_space=pl.ANY)] * (layers - 1),
        out_specs=VMEM,
        out_shape=jax.ShapeDtypeStruct((order, (layers - 1) * rank), half),
        scratch_shapes=[pltpu.SemaphoreType.DMA((layers - 1,))],
        compiler_params=pltpu.CompilerParams(vmem_limit_bytes=16 * 2**20),
    )(*lefts[1:])
    next_rows, others = lax.optimization_barrier((next_rows, others))
    (shift_t,) = local(make_shift, (next_rows, applied), ((width, rank), half))
    weights = project(next_rows, inverse_diag)
    entry = lax.dynamic_slice_in_dim(incoming, lower * share, share, 1)
    place = upper.reshape(1)
    others, shift_t, weights, entry, place = lax.optimization_barrier(
        (others, shift_t, weights, entry, place)
    )
    tile_range, sent = local(
        lambda *refs: make_maps(layers, *refs),
        (*cores, lefts[0], others, weights, shift_t),
        ((order, rank), half),
        ((lowers, rank + share, rank), half),
    )
    sent, tile_range, entry, place = lax.optimization_barrier((sent, tile_range, entry, place))
    steps = exchanged(sent, near)
    steps, tile_range, entry, place = lax.optimization_barrier((steps, tile_range, entry, place))
    values, last = local(
        first_half,
        (place, steps, entry),
        ((lowers, share, rank), jnp.float32),
        ((share, rank), half),
        scalar=True,
    )
    entered = shifted(last, "row", lowers)
    steps, tile_range, _ = lax.optimization_barrier((steps, tile_range, last))
    gain = product(inverse_diag, tile_range).astype(half)
    values, maps = local(
        second_half,
        (place, steps, values),
        ((lowers, share, rank), jnp.float32),
        ((lowers, rank, rank), half),
        scalar=True,
        aliases={2: 0},
    )
    gain, maps = lax.optimization_barrier((gain, maps))
    (coupled,) = local(enter, (entered, maps, values), ((lowers, share, rank), half))
    coupled = exchanged(coupled, near).reshape(width, rank)
    moved = lax.dot_general(gain, coupled, FLIPPED, preferred_element_type=jnp.float32)
    return (applied.astype(jnp.float32) - moved).astype(half)


def solution(mesh):
    return jax.shard_map(
        body,
        mesh=mesh,
        in_specs=(
            P("layer", "row", None),
            P("layer", "row", None),
            P("row", None),
            P("row", None),
            P("row", None),
            P("row", "layer"),
            P(None, "layer"),
        ),
        out_specs=P("row", "layer"),
        check_vma=False,
    )
```

```python
import jax
import jax.numpy as jnp
from jax import lax
from jax.experimental import pallas as pl
from jax.experimental.pallas import tpu as pltpu
from jax.sharding import PartitionSpec as P


def shifted(value, axis, steps):
    count = lax.axis_size(axis)
    leading, last = (max(0, -steps), min(count, count - steps))
    return lax.ppermute(value, axis, [(source, source + steps) for source in range(leading, last)])


def rotated(value, axis, steps):
    count = lax.axis_size(axis)
    return lax.ppermute(value, axis, [(source, (source + steps) % count) for source in range(count)])


def project(basis, vectors):
    return lax.dot_general(
        basis, vectors, (((0,), (0,)), ((), ())), preferred_element_type=jnp.float32
    )


def product(a, b):
    return jnp.dot(a, b, preferred_element_type=jnp.float32)


SMEM = pl.BlockSpec(memory_space=pltpu.SMEM)
VMEM = pl.BlockSpec(memory_space=pltpu.VMEM)
FLIPPED = (((1,), (1,)), ((), ()))


def split(value):
    high = value.astype(jnp.bfloat16)
    return high, (value - high.astype(jnp.float32)).astype(jnp.bfloat16)


def wide(value, matrix):
    both = product(jnp.concatenate(split(value)), matrix)
    return both[: value.shape[0]] + both[value.shape[0] :]


def make_maps(layers, *refs):
    cores = jnp.concatenate([ref[...] for ref in refs[:layers]], axis=0)
    lefts = jnp.concatenate([ref[...] for ref in refs[layers : 2 * layers]], axis=1)
    weights_ref, next_ref, applied_ref, range_ref, sent_ref = refs[2 * layers :]
    shift_t = project(next_ref[...], applied_ref[...]).T.astype(jnp.bfloat16)
    range_ref[...] = (-product(lefts, cores)).astype(jnp.bfloat16)
    map_t = wide(wide(weights_ref[...], lefts), cores).T.astype(jnp.bfloat16)
    rank = map_t.shape[0]
    share = sent_ref.shape[1] - rank
    for target in range(sent_ref.shape[0]):
        sent_ref[target, :rank] = map_t
        sent_ref[target, rank:] = shift_t[target * share : (target + 1) * share]


def chain(steps_ref, state, values_ref):
    count, _, rank = steps_ref.shape
    for member in range(count):
        values_ref[member] = state
        state = wide(state, steps_ref[member, :rank])
        state = state + steps_ref[member, rank:].astype(jnp.float32)
    return state


def first_half(upper_ref, steps_ref, entry_ref, values_ref, last_ref):
    @pl.when(upper_ref[0] == 0)
    def _():
        last_ref[...] = chain(steps_ref, entry_ref[...].T, values_ref).astype(jnp.bfloat16)


def second_half(upper_ref, steps_ref, before_ref, values_ref, maps_ref):
    count, rank, _ = maps_ref.shape

    @pl.when(upper_ref[0] == 0)
    def _():
        maps_ref[...] = jnp.zeros(maps_ref.shape, jnp.bfloat16)

    @pl.when(upper_ref[0] > 0)
    def _():
        chain(steps_ref, jnp.zeros(values_ref.shape[1:], jnp.float32), values_ref)
        state = steps_ref[0, :rank]
        for member in range(1, count):
            maps_ref[member] = state
            if member + 1 < count:
                state = product(state, steps_ref[member, :rank]).astype(jnp.bfloat16)


def enter(entered_ref, maps_ref, values_ref, coupled_ref):
    entered = entered_ref[...]
    coupled_ref[0] = (entered.astype(jnp.float32) + values_ref[0]).astype(jnp.bfloat16)
    for member in range(1, coupled_ref.shape[0]):
        moved = product(entered, maps_ref[member])
        coupled_ref[member] = (moved + values_ref[member]).astype(jnp.bfloat16)


def local(kernel, inputs, *outputs, scalar=False, aliases={}):
    specs = [SMEM] * scalar + [VMEM] * (len(inputs) - scalar)
    return pl.pallas_call(
        kernel,
        in_specs=specs,
        out_specs=[VMEM] * len(outputs),
        out_shape=[jax.ShapeDtypeStruct(*output) for output in outputs],
        input_output_aliases=aliases,
        compiler_params=pltpu.CompilerParams(vmem_limit_bytes=16 * 2**20),
    )(*inputs)


def exchanged(blocks, members):
    return lax.all_to_all(blocks, "row", 0, 0, axis_index_groups=members, tiled=True)


def body(left_factors, right_factors, sketch, row_basis, inverse_diag, right_side, incoming):
    half = jnp.bfloat16
    order, rank = sketch.shape
    width = right_side.shape[1]
    layers, groups = lax.axis_size("layer"), lax.axis_size("row")
    lowers = groups // 2
    here = lax.axis_index("row")
    upper, lower = lax.div(here, lowers), lax.rem(here, lowers)
    share = width // lowers
    near = [list(range(lowers)), list(range(lowers, groups))]

    lefts = [left_factors[0]] + [rotated(left_factors[0], "layer", k) for k in range(1, layers)]
    next_rows = shifted(row_basis, "row", -1)
    applied = product(inverse_diag, right_side).astype(half)
    sketch, applied = lax.optimization_barrier((sketch, applied))
    core = project(right_factors[0], sketch).astype(half)
    cores = [core] + [rotated(core, "layer", k) for k in range(1, layers)]

    next_rows, *others = lax.optimization_barrier((next_rows, *lefts[1:]))
    weights = project(next_rows, inverse_diag)
    entry = lax.dynamic_slice_in_dim(incoming, lower * share, share, 1)
    place = upper.reshape(1)
    weights, entry, place = lax.optimization_barrier((weights, entry, place))
    tile_range, sent = local(
        lambda *refs: make_maps(layers, *refs),
        (*cores, lefts[0], *others, weights, next_rows, applied),
        ((order, rank), half),
        ((lowers, rank + share, rank), half),
    )
    sent, tile_range, entry, place = lax.optimization_barrier((sent, tile_range, entry, place))
    steps = exchanged(sent, near)
    steps, tile_range, entry, place = lax.optimization_barrier((steps, tile_range, entry, place))
    values, last = local(
        first_half,
        (place, steps, entry),
        ((lowers, share, rank), jnp.float32),
        ((share, rank), half),
        scalar=True,
    )
    entered = shifted(last, "row", lowers)
    steps, tile_range, _ = lax.optimization_barrier((steps, tile_range, last))
    gain = product(inverse_diag, tile_range).astype(half)
    values, maps = local(
        second_half,
        (place, steps, values),
        ((lowers, share, rank), jnp.float32),
        ((lowers, rank, rank), half),
        scalar=True,
        aliases={2: 0},
    )
    gain, maps = lax.optimization_barrier((gain, maps))
    (coupled,) = local(enter, (entered, maps, values), ((lowers, share, rank), half))
    coupled = exchanged(coupled, near).reshape(width, rank)
    moved = lax.dot_general(gain, coupled, FLIPPED, preferred_element_type=jnp.float32)
    return (applied.astype(jnp.float32) - moved).astype(half)


def solution(mesh):
    return jax.shard_map(
        body,
        mesh=mesh,
        in_specs=(
            P("layer", "row", None),
            P("layer", "row", None),
            P("row", None),
            P("row", None),
            P("row", None),
            P("row", "layer"),
            P(None, "layer"),
        ),
        out_specs=P("row", "layer"),
        check_vma=False,
    )
```

```python
import jax
import jax.numpy as jnp
from jax import lax
from jax.experimental import pallas as pl
from jax.experimental.pallas import tpu as pltpu
from jax.sharding import PartitionSpec as P


def shifted(value, axis, steps):
    count = lax.axis_size(axis)
    leading, last = (max(0, -steps), min(count, count - steps))
    return lax.ppermute(value, axis, [(source, source + steps) for source in range(leading, last)])


def rotated(value, axis, steps):
    count = lax.axis_size(axis)
    return lax.ppermute(value, axis, [(source, (source + steps) % count) for source in range(count)])


def project(basis, vectors):
    return lax.dot_general(
        basis, vectors, (((0,), (0,)), ((), ())), preferred_element_type=jnp.float32
    )


def product(a, b):
    return jnp.dot(a, b, preferred_element_type=jnp.float32)


SMEM = pl.BlockSpec(memory_space=pltpu.SMEM)
VMEM = pl.BlockSpec(memory_space=pltpu.VMEM)
FLIPPED = (((1,), (1,)), ((), ()))


def split(value):
    high = value.astype(jnp.bfloat16)
    return high, (value - high.astype(jnp.float32)).astype(jnp.bfloat16)


def wide(value, matrix):
    both = product(jnp.concatenate(split(value)), matrix)
    return both[: value.shape[0]] + both[value.shape[0] :]


def lay(*refs):
    rank = refs[0].shape[1]
    for layer, ref in enumerate(refs[:-1]):
        refs[-1][:, layer * rank : (layer + 1) * rank] = ref[...]


def make_maps(layers, *refs):
    cores = jnp.concatenate([ref[...] for ref in refs[:layers]], axis=0)
    left_ref, others_ref, weights_ref, next_ref, applied_ref, range_ref, sent_ref = refs[layers:]
    lefts = jnp.concatenate([left_ref[...], others_ref[...]], axis=1)
    shift_t = project(next_ref[...], applied_ref[...]).T.astype(jnp.bfloat16)
    range_ref[...] = (-product(lefts, cores)).astype(jnp.bfloat16)
    map_t = wide(wide(weights_ref[...], lefts), cores).T.astype(jnp.bfloat16)
    rank = map_t.shape[0]
    share = sent_ref.shape[1] - rank
    for target in range(sent_ref.shape[0]):
        sent_ref[target, :rank] = map_t
        sent_ref[target, rank:] = shift_t[target * share : (target + 1) * share]


def chain(steps_ref, state, values_ref):
    count, _, rank = steps_ref.shape
    for member in range(count):
        values_ref[member] = state
        state = wide(state, steps_ref[member, :rank])
        state = state + steps_ref[member, rank:].astype(jnp.float32)
    return state


def first_half(upper_ref, steps_ref, entry_ref, values_ref, last_ref):
    @pl.when(upper_ref[0] == 0)
    def _():
        last_ref[...] = chain(steps_ref, entry_ref[...].T, values_ref).astype(jnp.bfloat16)


def second_half(upper_ref, steps_ref, before_ref, values_ref, maps_ref):
    count, rank, _ = maps_ref.shape

    @pl.when(upper_ref[0] == 0)
    def _():
        maps_ref[...] = jnp.zeros(maps_ref.shape, jnp.bfloat16)

    @pl.when(upper_ref[0] > 0)
    def _():
        chain(steps_ref, jnp.zeros(values_ref.shape[1:], jnp.float32), values_ref)
        state = steps_ref[0, :rank]
        for member in range(1, count):
            maps_ref[member] = state
            if member + 1 < count:
                state = product(state, steps_ref[member, :rank]).astype(jnp.bfloat16)


def enter(entered_ref, maps_ref, values_ref, coupled_ref):
    entered = entered_ref[...]
    coupled_ref[0] = (entered.astype(jnp.float32) + values_ref[0]).astype(jnp.bfloat16)
    for member in range(1, coupled_ref.shape[0]):
        moved = product(entered, maps_ref[member])
        coupled_ref[member] = (moved + values_ref[member]).astype(jnp.bfloat16)


def local(kernel, inputs, *outputs, scalar=False, aliases={}):
    specs = [SMEM] * scalar + [VMEM] * (len(inputs) - scalar)
    return pl.pallas_call(
        kernel,
        in_specs=specs,
        out_specs=[VMEM] * len(outputs),
        out_shape=[jax.ShapeDtypeStruct(*output) for output in outputs],
        input_output_aliases=aliases,
        compiler_params=pltpu.CompilerParams(vmem_limit_bytes=16 * 2**20),
    )(*inputs)


def exchanged(blocks, members):
    return lax.all_to_all(blocks, "row", 0, 0, axis_index_groups=members, tiled=True)


def body(left_factors, right_factors, sketch, row_basis, inverse_diag, right_side, incoming):
    half = jnp.bfloat16
    order, rank = sketch.shape
    width = right_side.shape[1]
    layers, groups = lax.axis_size("layer"), lax.axis_size("row")
    lowers = groups // 2
    here = lax.axis_index("row")
    upper, lower = lax.div(here, lowers), lax.rem(here, lowers)
    share = width // lowers
    near = [list(range(lowers)), list(range(lowers, groups))]

    lefts = [left_factors[0]] + [rotated(left_factors[0], "layer", k) for k in range(1, layers)]
    next_rows = shifted(row_basis, "row", -1)
    applied = product(inverse_diag, right_side).astype(half)
    sketch, applied = lax.optimization_barrier((sketch, applied))
    core = project(right_factors[0], sketch).astype(half)
    cores = [core] + [rotated(core, "layer", k) for k in range(1, layers)]

    (others,) = local(lay, lefts[1:], ((order, (layers - 1) * rank), half))
    next_rows, others = lax.optimization_barrier((next_rows, others))
    weights = project(next_rows, inverse_diag)
    entry = lax.dynamic_slice_in_dim(incoming, lower * share, share, 1)
    place = upper.reshape(1)
    weights, entry, place = lax.optimization_barrier((weights, entry, place))
    tile_range, sent = local(
        lambda *refs: make_maps(layers, *refs),
        (*cores, lefts[0], others, weights, next_rows, applied),
        ((order, rank), half),
        ((lowers, rank + share, rank), half),
    )
    sent, tile_range, entry, place = lax.optimization_barrier((sent, tile_range, entry, place))
    steps = exchanged(sent, near)
    steps, tile_range, entry, place = lax.optimization_barrier((steps, tile_range, entry, place))
    values, last = local(
        first_half,
        (place, steps, entry),
        ((lowers, share, rank), jnp.float32),
        ((share, rank), half),
        scalar=True,
    )
    entered = shifted(last, "row", lowers)
    steps, tile_range, _ = lax.optimization_barrier((steps, tile_range, last))
    gain = product(inverse_diag, tile_range).astype(half)
    values, maps = local(
        second_half,
        (place, steps, values),
        ((lowers, share, rank), jnp.float32),
        ((lowers, rank, rank), half),
        scalar=True,
        aliases={2: 0},
    )
    gain, maps = lax.optimization_barrier((gain, maps))
    (coupled,) = local(enter, (entered, maps, values), ((lowers, share, rank), half))
    coupled = exchanged(coupled, near).reshape(width, rank)
    moved = lax.dot_general(gain, coupled, FLIPPED, preferred_element_type=jnp.float32)
    return (applied.astype(jnp.float32) - moved).astype(half)


def solution(mesh):
    return jax.shard_map(
        body,
        mesh=mesh,
        in_specs=(
            P("layer", "row", None),
            P("layer", "row", None),
            P("row", None),
            P("row", None),
            P("row", None),
            P("row", "layer"),
            P(None, "layer"),
        ),
        out_specs=P("row", "layer"),
        check_vma=False,
    )
```

```python
import jax
import jax.numpy as jnp
from jax import lax
from jax.experimental import pallas as pl
from jax.experimental.pallas import tpu as pltpu
from jax.sharding import PartitionSpec as P


def shifted(value, axis, steps):
    count = lax.axis_size(axis)
    leading, last = (max(0, -steps), min(count, count - steps))
    return lax.ppermute(value, axis, [(source, source + steps) for source in range(leading, last)])


def rotated(value, axis, steps):
    count = lax.axis_size(axis)
    return lax.ppermute(value, axis, [(source, (source + steps) % count) for source in range(count)])


def project(basis, vectors):
    return lax.dot_general(
        basis, vectors, (((0,), (0,)), ((), ())), preferred_element_type=jnp.float32
    )


def product(a, b):
    return jnp.dot(a, b, preferred_element_type=jnp.float32)


SMEM = pl.BlockSpec(memory_space=pltpu.SMEM)
VMEM = pl.BlockSpec(memory_space=pltpu.VMEM)
FLIPPED = (((1,), (1,)), ((), ()))


def split(value):
    high = value.astype(jnp.bfloat16)
    return high, (value - high.astype(jnp.float32)).astype(jnp.bfloat16)


def wide(value, matrix):
    both = product(jnp.concatenate(split(value)), matrix)
    return both[: value.shape[0]] + both[value.shape[0] :]


def make_shift(next_ref, applied_ref, shift_ref):
    shift_ref[...] = project(next_ref[...], applied_ref[...]).T.astype(jnp.bfloat16)


def lay(*refs):
    rank = refs[0].shape[1]
    for layer, ref in enumerate(refs[:-1]):
        refs[-1][:, layer * rank : (layer + 1) * rank] = ref[...]


def make_maps(layers, *refs):
    cores = jnp.concatenate([ref[...] for ref in refs[:layers]], axis=0)
    left_ref, others_ref, weights_ref, shift_ref, range_ref, sent_ref = refs[layers:]
    lefts = jnp.concatenate([left_ref[...], others_ref[...]], axis=1)
    range_ref[...] = (-product(lefts, cores)).astype(jnp.bfloat16)
    map_t = wide(wide(weights_ref[...], lefts), cores).T.astype(jnp.bfloat16)
    rank = map_t.shape[0]
    share = sent_ref.shape[1] - rank
    for target in range(sent_ref.shape[0]):
        sent_ref[target, :rank] = map_t
        sent_ref[target, rank:] = shift_ref[target * share : (target + 1) * share]


def chain(steps_ref, state, values_ref, swap):
    count, _, rank = steps_ref.shape
    for member in range(count):
        values_ref[member ^ swap] = state
        state = wide(state, steps_ref[member ^ swap, :rank])
        state = state + steps_ref[member ^ swap, rank:].astype(jnp.float32)
    return state


def first_half(upper_ref, steps_ref, entry_ref, values_ref, last_ref):
    @pl.when(upper_ref[0] == 0)
    def _():
        last_ref[...] = chain(steps_ref, entry_ref[...].T, values_ref, 0).astype(jnp.bfloat16)


def second_half(upper_ref, steps_ref, before_ref, values_ref, maps_ref):
    count, rank, _ = maps_ref.shape

    @pl.when(upper_ref[0] == 0)
    def _():
        maps_ref[...] = jnp.zeros(maps_ref.shape, jnp.bfloat16)

    @pl.when(upper_ref[0] > 0)
    def _():
        chain(steps_ref, jnp.zeros(values_ref.shape[1:], jnp.float32), values_ref, 1)
        rows = lax.broadcasted_iota(jnp.int32, (rank, rank), 0)
        cols = lax.broadcasted_iota(jnp.int32, (rank, rank), 1)
        maps_ref[1] = jnp.where(rows == cols, 1.0, 0.0).astype(jnp.bfloat16)
        state = steps_ref[1, :rank]
        for member in range(1, count):
            maps_ref[member ^ 1] = state
            if member + 1 < count:
                state = product(state, steps_ref[member ^ 1, :rank]).astype(jnp.bfloat16)


def enter(entered_ref, maps_ref, values_ref, coupled_ref):
    entered = entered_ref[...]
    for member in range(coupled_ref.shape[0]):
        moved = product(entered, maps_ref[member])
        coupled_ref[member] = (moved + values_ref[member]).astype(jnp.bfloat16)


def local(kernel, inputs, *outputs, scalar=False, aliases={}):
    specs = [SMEM] * scalar + [VMEM] * (len(inputs) - scalar)
    return pl.pallas_call(
        kernel,
        in_specs=specs,
        out_specs=[VMEM] * len(outputs),
        out_shape=[jax.ShapeDtypeStruct(*output) for output in outputs],
        input_output_aliases=aliases,
        compiler_params=pltpu.CompilerParams(vmem_limit_bytes=16 * 2**20),
    )(*inputs)


def exchanged(blocks, members):
    return lax.all_to_all(blocks, "row", 0, 0, axis_index_groups=members, tiled=True)


def body(left_factors, right_factors, sketch, row_basis, inverse_diag, right_side, incoming):
    half = jnp.bfloat16
    order, rank = sketch.shape
    width = right_side.shape[1]
    layers, groups = lax.axis_size("layer"), lax.axis_size("row")
    lowers = groups // 2
    here = lax.axis_index("row")
    upper, lower = lax.div(here, lowers), lax.rem(here, lowers)
    share = width // lowers
    across = [lowers + (place ^ 1) for place in range(lowers)]
    near = [list(range(lowers)), across]

    lefts = [left_factors[0]] + [rotated(left_factors[0], "layer", k) for k in range(1, layers)]
    next_rows = shifted(row_basis, "row", -1)
    applied = product(inverse_diag, right_side).astype(half)
    sketch, applied = lax.optimization_barrier((sketch, applied))
    core = project(right_factors[0], sketch).astype(half)
    cores = [core] + [rotated(core, "layer", k) for k in range(1, layers)]

    (others,) = local(lay, lefts[1:], ((order, (layers - 1) * rank), half))
    next_rows, others = lax.optimization_barrier((next_rows, others))
    (shift_t,) = local(make_shift, (next_rows, applied), ((width, rank), half))
    weights = project(next_rows, inverse_diag)
    entry = lax.dynamic_slice_in_dim(incoming, lower * share, share, 1)
    place = upper.reshape(1)
    others, shift_t, weights, entry, place = lax.optimization_barrier(
        (others, shift_t, weights, entry, place)
    )
    tile_range, sent = local(
        lambda *refs: make_maps(layers, *refs),
        (*cores, lefts[0], others, weights, shift_t),
        ((order, rank), half),
        ((lowers, rank + share, rank), half),
    )
    sent, tile_range, entry, place = lax.optimization_barrier((sent, tile_range, entry, place))
    steps = exchanged(sent, near)
    steps, tile_range, entry, place = lax.optimization_barrier((steps, tile_range, entry, place))
    values, last = local(
        first_half,
        (place, steps, entry),
        ((lowers, share, rank), jnp.float32),
        ((share, rank), half),
        scalar=True,
    )
    entered = lax.ppermute(last, "row", list(enumerate(across)))
    steps, tile_range, _ = lax.optimization_barrier((steps, tile_range, last))
    gain = product(inverse_diag, tile_range).astype(half)
    values, maps = local(
        second_half,
        (place, steps, values),
        ((lowers, share, rank), jnp.float32),
        ((lowers, rank, rank), half),
        scalar=True,
        aliases={2: 0},
    )
    gain, maps = lax.optimization_barrier((gain, maps))
    (coupled,) = local(enter, (entered, maps, values), ((lowers, share, rank), half))
    coupled = exchanged(coupled, near).reshape(width, rank)
    moved = lax.dot_general(gain, coupled, FLIPPED, preferred_element_type=jnp.float32)
    return (applied.astype(jnp.float32) - moved).astype(half)


def solution(mesh):
    return jax.shard_map(
        body,
        mesh=mesh,
        in_specs=(
            P("layer", "row", None),
            P("layer", "row", None),
            P("row", None),
            P("row", None),
            P("row", None),
            P("row", "layer"),
            P(None, "layer"),
        ),
        out_specs=P("row", "layer"),
        check_vma=False,
    )
```

```python
import jax
import jax.numpy as jnp
from jax import lax
from jax.experimental import pallas as pl
from jax.experimental.pallas import tpu as pltpu
from jax.sharding import PartitionSpec as P


def shifted(value, axis, steps):
    count = lax.axis_size(axis)
    leading, last = (max(0, -steps), min(count, count - steps))
    return lax.ppermute(value, axis, [(source, source + steps) for source in range(leading, last)])


def rotated(value, axis, steps):
    count = lax.axis_size(axis)
    return lax.ppermute(value, axis, [(source, (source + steps) % count) for source in range(count)])


def project(basis, vectors):
    return lax.dot_general(
        basis, vectors, (((0,), (0,)), ((), ())), preferred_element_type=jnp.float32
    )


def product(a, b):
    return jnp.dot(a, b, preferred_element_type=jnp.float32)


SMEM = pl.BlockSpec(memory_space=pltpu.SMEM)
VMEM = pl.BlockSpec(memory_space=pltpu.VMEM)
PARTS = 4


def split(value):
    high = value.astype(jnp.bfloat16)
    return high, (value - high.astype(jnp.float32)).astype(jnp.bfloat16)


def wide(value, matrix):
    both = product(jnp.concatenate(split(value)), matrix)
    return both[: value.shape[0]] + both[value.shape[0] :]


def make_shift(next_ref, applied_ref, shift_ref):
    shift_ref[...] = project(next_ref[...], applied_ref[...]).T.astype(jnp.bfloat16)


def lay(*refs):
    rank = refs[0].shape[1]
    for layer, ref in enumerate(refs[:-1]):
        refs[-1][:, layer * rank : (layer + 1) * rank] = ref[...]


def make_maps(layers, *refs):
    cores = jnp.concatenate([ref[...] for ref in refs[:layers]], axis=0)
    left_ref, others_ref, weights_ref, shift_ref, range_ref, sent_ref = refs[layers:]
    lefts = jnp.concatenate([left_ref[...], others_ref[...]], axis=1)
    range_ref[...] = (-product(lefts, cores)).astype(jnp.bfloat16)
    map_t = wide(wide(weights_ref[...], lefts), cores).T.astype(jnp.bfloat16)
    rank = map_t.shape[0]
    share = sent_ref.shape[1] - rank
    for target in range(sent_ref.shape[0]):
        sent_ref[target, :rank] = map_t
        sent_ref[target, rank:] = shift_ref[target * share : (target + 1) * share]


def chain(steps_ref, state, values_ref, swap):
    count, _, rank = steps_ref.shape
    for member in range(count):
        values_ref[member ^ swap] = state
        state = wide(state, steps_ref[member ^ swap, :rank])
        state = state + steps_ref[member ^ swap, rank:].astype(jnp.float32)
    return state


def first_half(upper_ref, steps_ref, entry_ref, values_ref, last_ref):
    @pl.when(upper_ref[0] == 0)
    def _():
        last_ref[...] = chain(steps_ref, entry_ref[...].T, values_ref, 0).astype(jnp.bfloat16)


def second_half(upper_ref, steps_ref, before_ref, values_ref, maps_ref):
    count, rank, _ = maps_ref.shape

    @pl.when(upper_ref[0] == 0)
    def _():
        maps_ref[...] = jnp.zeros(maps_ref.shape, jnp.bfloat16)

    @pl.when(upper_ref[0] > 0)
    def _():
        chain(steps_ref, jnp.zeros(values_ref.shape[1:], jnp.float32), values_ref, 1)
        rows = lax.broadcasted_iota(jnp.int32, (rank, rank), 0)
        cols = lax.broadcasted_iota(jnp.int32, (rank, rank), 1)
        maps_ref[1] = jnp.where(rows == cols, 1.0, 0.0).astype(jnp.bfloat16)
        state = steps_ref[1, :rank]
        for member in range(1, count):
            maps_ref[member ^ 1] = state
            if member + 1 < count:
                state = product(state, steps_ref[member ^ 1, :rank]).astype(jnp.bfloat16)


def enter(entered_ref, maps_ref, values_ref, coupled_ref):
    entered = entered_ref[...]
    for member in range(coupled_ref.shape[0]):
        moved = product(entered, maps_ref[member])
        coupled_ref[member] = (moved + values_ref[member]).astype(jnp.bfloat16)


def solve(gain_ref, coupled_ref, applied_ref, result_hbm, result, sent):
    rows = gain_ref.shape[0] // PARTS
    coupled = coupled_ref[...].T
    copies = []
    for part in range(PARTS):
        piece = pl.ds(part * rows, rows)
        moved = product(gain_ref[piece], coupled)
        applied = applied_ref[piece].astype(jnp.float32)
        result[piece] = (applied - moved).astype(jnp.bfloat16)
        copies.append(pltpu.make_async_copy(result.at[piece], result_hbm.at[piece], sent.at[part]))
        copies[-1].start()
    for copy in copies:
        copy.wait()


def local(kernel, inputs, *outputs, scalar=False, aliases={}):
    specs = [SMEM] * scalar + [VMEM] * (len(inputs) - scalar)
    return pl.pallas_call(
        kernel,
        in_specs=specs,
        out_specs=[VMEM] * len(outputs),
        out_shape=[jax.ShapeDtypeStruct(*output) for output in outputs],
        input_output_aliases=aliases,
        compiler_params=pltpu.CompilerParams(vmem_limit_bytes=16 * 2**20),
    )(*inputs)


def exchanged(blocks, members):
    return lax.all_to_all(blocks, "row", 0, 0, axis_index_groups=members, tiled=True)


def body(left_factors, right_factors, sketch, row_basis, inverse_diag, right_side, incoming):
    half = jnp.bfloat16
    order, rank = sketch.shape
    width = right_side.shape[1]
    layers, groups = lax.axis_size("layer"), lax.axis_size("row")
    lowers = groups // 2
    here = lax.axis_index("row")
    upper, lower = lax.div(here, lowers), lax.rem(here, lowers)
    share = width // lowers
    across = [lowers + (place ^ 1) for place in range(lowers)]
    near = [list(range(lowers)), across]

    lefts = [left_factors[0]] + [rotated(left_factors[0], "layer", k) for k in range(1, layers)]
    next_rows = shifted(row_basis, "row", -1)
    applied = product(inverse_diag, right_side).astype(half)
    sketch, applied = lax.optimization_barrier((sketch, applied))
    core = project(right_factors[0], sketch).astype(half)
    cores = [core] + [rotated(core, "layer", k) for k in range(1, layers)]

    (others,) = local(lay, lefts[1:], ((order, (layers - 1) * rank), half))
    next_rows, others = lax.optimization_barrier((next_rows, others))
    (shift_t,) = local(make_shift, (next_rows, applied), ((width, rank), half))
    weights = project(next_rows, inverse_diag)
    entry = lax.dynamic_slice_in_dim(incoming, lower * share, share, 1)
    place = upper.reshape(1)
    others, shift_t, weights, entry, place = lax.optimization_barrier(
        (others, shift_t, weights, entry, place)
    )
    tile_range, sent = local(
        lambda *refs: make_maps(layers, *refs),
        (*cores, lefts[0], others, weights, shift_t),
        ((order, rank), half),
        ((lowers, rank + share, rank), half),
    )
    sent, tile_range, entry, place = lax.optimization_barrier((sent, tile_range, entry, place))
    steps = exchanged(sent, near)
    steps, tile_range, entry, place = lax.optimization_barrier((steps, tile_range, entry, place))
    values, last = local(
        first_half,
        (place, steps, entry),
        ((lowers, share, rank), jnp.float32),
        ((share, rank), half),
        scalar=True,
    )
    entered = lax.ppermute(last, "row", list(enumerate(across)))
    steps, tile_range, _ = lax.optimization_barrier((steps, tile_range, last))
    gain = product(inverse_diag, tile_range).astype(half)
    values, maps = local(
        second_half,
        (place, steps, values),
        ((lowers, share, rank), jnp.float32),
        ((lowers, rank, rank), half),
        scalar=True,
        aliases={2: 0},
    )
    gain, maps = lax.optimization_barrier((gain, maps))
    (coupled,) = local(enter, (entered, maps, values), ((lowers, share, rank), half))
    coupled = exchanged(coupled, near).reshape(width, rank)
    return pl.pallas_call(
        solve,
        in_specs=[VMEM] * 3,
        out_specs=pl.BlockSpec(memory_space=pl.ANY),
        out_shape=jax.ShapeDtypeStruct(applied.shape, half),
        scratch_shapes=[pltpu.VMEM(applied.shape, half), pltpu.SemaphoreType.DMA((PARTS,))],
        compiler_params=pltpu.CompilerParams(vmem_limit_bytes=16 * 2**20),
    )(gain, coupled, applied)


def solution(mesh):
    return jax.shard_map(
        body,
        mesh=mesh,
        in_specs=(
            P("layer", "row", None),
            P("layer", "row", None),
            P("row", None),
            P("row", None),
            P("row", None),
            P("row", "layer"),
            P(None, "layer"),
        ),
        out_specs=P("row", "layer"),
        check_vma=False,
    )
```

```python
import jax
import jax.numpy as jnp
from jax import lax
from jax.experimental import pallas as pl
from jax.experimental.pallas import tpu as pltpu
from jax.sharding import PartitionSpec as P


def shifted(value, axis, steps):
    count = lax.axis_size(axis)
    leading, last = (max(0, -steps), min(count, count - steps))
    return lax.ppermute(value, axis, [(source, source + steps) for source in range(leading, last)])


def rotated(value, axis, steps):
    count = lax.axis_size(axis)
    return lax.ppermute(value, axis, [(source, (source + steps) % count) for source in range(count)])


def project(basis, vectors):
    return lax.dot_general(
        basis, vectors, (((0,), (0,)), ((), ())), preferred_element_type=jnp.float32
    )


def product(a, b):
    return jnp.dot(a, b, preferred_element_type=jnp.float32)


SMEM = pl.BlockSpec(memory_space=pltpu.SMEM)
VMEM = pl.BlockSpec(memory_space=pltpu.VMEM)
PARTS = 8


def split(value):
    high = value.astype(jnp.bfloat16)
    return high, (value - high.astype(jnp.float32)).astype(jnp.bfloat16)


def wide(value, matrix):
    both = product(jnp.concatenate(split(value)), matrix)
    return both[: value.shape[0]] + both[value.shape[0] :]


def weigh(left_ref, others_ref, weights_ref, next_ref, applied_ref, high_ref, low_ref, shift_ref):
    lefts = jnp.concatenate([left_ref[...], others_ref[...]], axis=1)
    high_ref[...], low_ref[...] = split(wide(weights_ref[...], lefts))
    shift_ref[...] = project(next_ref[...], applied_ref[...]).T.astype(jnp.bfloat16)


def lay(*refs):
    rank = refs[0].shape[1]
    for layer, ref in enumerate(refs[:-1]):
        refs[-1][:, layer * rank : (layer + 1) * rank] = ref[...]


def make_maps(layers, *refs):
    cores = jnp.concatenate([ref[...] for ref in refs[:layers]], axis=0)
    left_ref, others_ref, high_ref, low_ref, shift_ref, range_ref, sent_ref = refs[layers:]
    both = product(jnp.concatenate([high_ref[...], low_ref[...]]), cores)
    rank = both.shape[1]
    map_t = (both[:rank] + both[rank:]).T.astype(jnp.bfloat16)
    share = sent_ref.shape[1] - rank
    for target in range(sent_ref.shape[0]):
        sent_ref[target, :rank] = map_t
        sent_ref[target, rank:] = shift_ref[target * share : (target + 1) * share]
    lefts = jnp.concatenate([left_ref[...], others_ref[...]], axis=1)
    range_ref[...] = (-product(lefts, cores)).astype(jnp.bfloat16)


def chain(steps_ref, state, values_ref, swap):
    count, _, rank = steps_ref.shape
    for member in range(count):
        values_ref[member ^ swap] = state
        state = wide(state, steps_ref[member ^ swap, :rank])
        state = state + steps_ref[member ^ swap, rank:].astype(jnp.float32)
    return state


def first_half(upper_ref, steps_ref, entry_ref, values_ref, last_ref):
    @pl.when(upper_ref[0] == 0)
    def _():
        last_ref[...] = chain(steps_ref, entry_ref[...].T, values_ref, 0).astype(jnp.bfloat16)


def second_half(upper_ref, steps_ref, before_ref, values_ref, maps_ref):
    count, rank, _ = maps_ref.shape

    @pl.when(upper_ref[0] == 0)
    def _():
        maps_ref[...] = jnp.zeros(maps_ref.shape, jnp.bfloat16)

    @pl.when(upper_ref[0] > 0)
    def _():
        chain(steps_ref, jnp.zeros(values_ref.shape[1:], jnp.float32), values_ref, 1)
        rows = lax.broadcasted_iota(jnp.int32, (rank, rank), 0)
        cols = lax.broadcasted_iota(jnp.int32, (rank, rank), 1)
        maps_ref[1] = jnp.where(rows == cols, 1.0, 0.0).astype(jnp.bfloat16)
        state = steps_ref[1, :rank]
        for member in range(1, count):
            maps_ref[member ^ 1] = state
            if member + 1 < count:
                state = product(state, steps_ref[member ^ 1, :rank]).astype(jnp.bfloat16)


def enter(entered_ref, maps_ref, values_ref, coupled_ref):
    entered = entered_ref[...]
    for member in range(coupled_ref.shape[0]):
        moved = product(entered, maps_ref[member])
        coupled_ref[member] = (moved + values_ref[member]).astype(jnp.bfloat16)


def solve(gain_ref, coupled_ref, applied_ref, result_hbm, result, sent):
    rows = gain_ref.shape[0] // PARTS
    coupled = coupled_ref[...].T
    copies = []
    for part in range(PARTS):
        piece = pl.ds(part * rows, rows)
        moved = product(gain_ref[piece], coupled)
        applied = applied_ref[piece].astype(jnp.float32)
        result[piece] = (applied - moved).astype(jnp.bfloat16)
        copies.append(pltpu.make_async_copy(result.at[piece], result_hbm.at[piece], sent.at[part]))
        copies[-1].start()
    for copy in copies:
        copy.wait()


def local(kernel, inputs, *outputs, scalar=False, aliases={}):
    specs = [SMEM] * scalar + [VMEM] * (len(inputs) - scalar)
    return pl.pallas_call(
        kernel,
        in_specs=specs,
        out_specs=[VMEM] * len(outputs),
        out_shape=[jax.ShapeDtypeStruct(*output) for output in outputs],
        input_output_aliases=aliases,
        compiler_params=pltpu.CompilerParams(vmem_limit_bytes=16 * 2**20),
    )(*inputs)


def exchanged(blocks, members):
    return lax.all_to_all(blocks, "row", 0, 0, axis_index_groups=members, tiled=True)


def body(left_factors, right_factors, sketch, row_basis, inverse_diag, right_side, incoming):
    half = jnp.bfloat16
    order, rank = sketch.shape
    width = right_side.shape[1]
    layers, groups = lax.axis_size("layer"), lax.axis_size("row")
    lowers = groups // 2
    here = lax.axis_index("row")
    upper, lower = lax.div(here, lowers), lax.rem(here, lowers)
    share = width // lowers
    across = [lowers + (place ^ 1) for place in range(lowers)]
    near = [list(range(lowers)), across]

    lefts = [left_factors[0]] + [rotated(left_factors[0], "layer", k) for k in range(1, layers)]
    next_rows = shifted(row_basis, "row", -1)
    applied = product(inverse_diag, right_side).astype(half)
    sketch, applied = lax.optimization_barrier((sketch, applied))
    core = project(right_factors[0], sketch).astype(half)
    cores = [core] + [rotated(core, "layer", k) for k in range(1, layers)]

    (others,) = local(lay, lefts[1:], ((order, (layers - 1) * rank), half))
    next_rows, others = lax.optimization_barrier((next_rows, others))
    weights = project(next_rows, inverse_diag)
    high, low, shift_t = local(
        weigh,
        (lefts[0], others, weights, next_rows, applied),
        ((rank, layers * rank), half),
        ((rank, layers * rank), half),
        ((width, rank), half),
    )
    entry = lax.dynamic_slice_in_dim(incoming, lower * share, share, 1)
    place = upper.reshape(1)
    high, entry, place = lax.optimization_barrier((high, entry, place))
    tile_range, sent = local(
        lambda *refs: make_maps(layers, *refs),
        (*cores, lefts[0], others, high, low, shift_t),
        ((order, rank), half),
        ((lowers, rank + share, rank), half),
    )
    sent, tile_range, entry, place = lax.optimization_barrier((sent, tile_range, entry, place))
    steps = exchanged(sent, near)
    steps, tile_range, entry, place = lax.optimization_barrier((steps, tile_range, entry, place))
    values, last = local(
        first_half,
        (place, steps, entry),
        ((lowers, share, rank), jnp.float32),
        ((share, rank), half),
        scalar=True,
    )
    entered = lax.ppermute(last, "row", list(enumerate(across)))
    steps, tile_range, _ = lax.optimization_barrier((steps, tile_range, last))
    gain = product(inverse_diag, tile_range).astype(half)
    values, maps = local(
        second_half,
        (place, steps, values),
        ((lowers, share, rank), jnp.float32),
        ((lowers, rank, rank), half),
        scalar=True,
        aliases={2: 0},
    )
    gain, maps = lax.optimization_barrier((gain, maps))
    (coupled,) = local(enter, (entered, maps, values), ((lowers, share, rank), half))
    coupled = exchanged(coupled, near).reshape(width, rank)
    return pl.pallas_call(
        solve,
        in_specs=[VMEM] * 3,
        out_specs=pl.BlockSpec(memory_space=pl.ANY),
        out_shape=jax.ShapeDtypeStruct(applied.shape, half),
        scratch_shapes=[pltpu.VMEM(applied.shape, half), pltpu.SemaphoreType.DMA((PARTS,))],
        compiler_params=pltpu.CompilerParams(vmem_limit_bytes=16 * 2**20),
    )(gain, coupled, applied)


def solution(mesh):
    return jax.shard_map(
        body,
        mesh=mesh,
        in_specs=(
            P("layer", "row", None),
            P("layer", "row", None),
            P("row", None),
            P("row", None),
            P("row", None),
            P("row", "layer"),
            P(None, "layer"),
        ),
        out_specs=P("row", "layer"),
        check_vma=False,
    )
```

```python
import jax
import jax.numpy as jnp
from jax import lax
from jax.experimental import pallas as pl
from jax.experimental.pallas import tpu as pltpu
from jax.sharding import PartitionSpec as P


def shifted(value, axis, steps):
    count = lax.axis_size(axis)
    leading, last = (max(0, -steps), min(count, count - steps))
    return lax.ppermute(value, axis, [(source, source + steps) for source in range(leading, last)])


def rotated(value, axis, steps):
    count = lax.axis_size(axis)
    return lax.ppermute(value, axis, [(source, (source + steps) % count) for source in range(count)])


def project(basis, vectors):
    return lax.dot_general(
        basis, vectors, (((0,), (0,)), ((), ())), preferred_element_type=jnp.float32
    )


def product(a, b):
    return jnp.dot(a, b, preferred_element_type=jnp.float32)


SMEM = pl.BlockSpec(memory_space=pltpu.SMEM)
VMEM = pl.BlockSpec(memory_space=pltpu.VMEM)
PARTS = 4


def split(value):
    high = value.astype(jnp.bfloat16)
    return high, (value - high.astype(jnp.float32)).astype(jnp.bfloat16)


def wide(value, matrix):
    both = product(jnp.concatenate(split(value)), matrix)
    return both[: value.shape[0]] + both[value.shape[0] :]


def lay(*refs):
    rank = refs[0].shape[1]
    for layer, ref in enumerate(refs[:-1]):
        refs[-1][:, layer * rank : (layer + 1) * rank] = ref[...]


def make_maps(layers, *refs):
    cores = jnp.concatenate([ref[...] for ref in refs[:layers]], axis=0)
    left_ref, others_ref, weights_ref, next_ref, applied_ref, sent_ref = refs[layers:]
    lefts = jnp.concatenate([left_ref[...], others_ref[...]], axis=1)
    shift_t = project(next_ref[...], applied_ref[...]).T.astype(jnp.bfloat16)
    map_t = wide(wide(weights_ref[...], lefts), cores).T.astype(jnp.bfloat16)
    rank = map_t.shape[0]
    share = sent_ref.shape[1] - rank
    for target in range(sent_ref.shape[0]):
        sent_ref[target, :rank] = map_t
        sent_ref[target, rank:] = shift_t[target * share : (target + 1) * share]


def make_range(layers, *refs):
    cores = jnp.concatenate([ref[...] for ref in refs[:layers]], axis=0)
    left_ref, others_ref, range_ref = refs[layers:]
    lefts = jnp.concatenate([left_ref[...], others_ref[...]], axis=1)
    range_ref[...] = (-product(lefts, cores)).astype(jnp.bfloat16)


def chain(steps_ref, state, values_ref, swap):
    count, _, rank = steps_ref.shape
    for member in range(count):
        values_ref[member ^ swap] = state
        state = wide(state, steps_ref[member ^ swap, :rank])
        state = state + steps_ref[member ^ swap, rank:].astype(jnp.float32)
    return state


def first_half(upper_ref, steps_ref, entry_ref, values_ref, last_ref):
    @pl.when(upper_ref[0] == 0)
    def _():
        last_ref[...] = chain(steps_ref, entry_ref[...].T, values_ref, 0).astype(jnp.bfloat16)


def second_half(upper_ref, steps_ref, before_ref, values_ref, maps_ref):
    count, rank, _ = maps_ref.shape

    @pl.when(upper_ref[0] == 0)
    def _():
        maps_ref[...] = jnp.zeros(maps_ref.shape, jnp.bfloat16)

    @pl.when(upper_ref[0] > 0)
    def _():
        chain(steps_ref, jnp.zeros(values_ref.shape[1:], jnp.float32), values_ref, 1)
        rows = lax.broadcasted_iota(jnp.int32, (rank, rank), 0)
        cols = lax.broadcasted_iota(jnp.int32, (rank, rank), 1)
        maps_ref[1] = jnp.where(rows == cols, 1.0, 0.0).astype(jnp.bfloat16)
        state = steps_ref[1, :rank]
        for member in range(1, count):
            maps_ref[member ^ 1] = state
            if member + 1 < count:
                state = product(state, steps_ref[member ^ 1, :rank]).astype(jnp.bfloat16)


def enter(entered_ref, maps_ref, values_ref, coupled_ref):
    entered = entered_ref[...]
    for member in range(coupled_ref.shape[0]):
        moved = product(entered, maps_ref[member])
        coupled_ref[member] = (moved + values_ref[member]).astype(jnp.bfloat16)


def solve(gain_ref, coupled_ref, applied_ref, result_hbm, result, sent):
    rows = gain_ref.shape[0] // PARTS
    coupled = coupled_ref[...].T
    copies = []
    for part in range(PARTS):
        piece = pl.ds(part * rows, rows)
        moved = product(gain_ref[piece], coupled)
        applied = applied_ref[piece].astype(jnp.float32)
        result[piece] = (applied - moved).astype(jnp.bfloat16)
        copies.append(pltpu.make_async_copy(result.at[piece], result_hbm.at[piece], sent.at[part]))
        copies[-1].start()
    for copy in copies:
        copy.wait()


def local(kernel, inputs, *outputs, scalar=False, aliases={}):
    specs = [SMEM] * scalar + [VMEM] * (len(inputs) - scalar)
    return pl.pallas_call(
        kernel,
        in_specs=specs,
        out_specs=[VMEM] * len(outputs),
        out_shape=[jax.ShapeDtypeStruct(*output) for output in outputs],
        input_output_aliases=aliases,
        compiler_params=pltpu.CompilerParams(vmem_limit_bytes=16 * 2**20),
    )(*inputs)


def exchanged(blocks, members):
    return lax.all_to_all(blocks, "row", 0, 0, axis_index_groups=members, tiled=True)


def body(left_factors, right_factors, sketch, row_basis, inverse_diag, right_side, incoming):
    half = jnp.bfloat16
    order, rank = sketch.shape
    width = right_side.shape[1]
    layers, groups = lax.axis_size("layer"), lax.axis_size("row")
    lowers = groups // 2
    here = lax.axis_index("row")
    upper, lower = lax.div(here, lowers), lax.rem(here, lowers)
    share = width // lowers
    across = [lowers + (place ^ 1) for place in range(lowers)]
    near = [list(range(lowers)), across]

    lefts = [left_factors[0]] + [rotated(left_factors[0], "layer", k) for k in range(1, layers)]
    next_rows = shifted(row_basis, "row", -1)
    applied = product(inverse_diag, right_side).astype(half)
    sketch, applied = lax.optimization_barrier((sketch, applied))
    core = project(right_factors[0], sketch).astype(half)
    cores = [core] + [rotated(core, "layer", k) for k in range(1, layers)]

    (others,) = local(lay, lefts[1:], ((order, (layers - 1) * rank), half))
    next_rows, others = lax.optimization_barrier((next_rows, others))
    weights = project(next_rows, inverse_diag)
    entry = lax.dynamic_slice_in_dim(incoming, lower * share, share, 1)
    place = upper.reshape(1)
    others, weights, entry, place = lax.optimization_barrier((others, weights, entry, place))
    (sent,) = local(
        lambda *refs: make_maps(layers, *refs),
        (*cores, lefts[0], others, weights, next_rows, applied),
        ((lowers, rank + share, rank), half),
    )
    sent, others, entry, place = lax.optimization_barrier((sent, others, entry, place))
    steps = exchanged(sent, near)
    steps, others, entry, place = lax.optimization_barrier((steps, others, entry, place))
    values, last = local(
        first_half,
        (place, steps, entry),
        ((lowers, share, rank), jnp.float32),
        ((share, rank), half),
        scalar=True,
    )
    entered = lax.ppermute(last, "row", list(enumerate(across)))
    steps, others, _ = lax.optimization_barrier((steps, others, last))
    (tile_range,) = local(
        lambda *refs: make_range(layers, *refs),
        (*cores, lefts[0], others),
        ((order, rank), half),
    )
    gain = product(inverse_diag, tile_range).astype(half)
    values, maps = local(
        second_half,
        (place, steps, values),
        ((lowers, share, rank), jnp.float32),
        ((lowers, rank, rank), half),
        scalar=True,
        aliases={2: 0},
    )
    gain, maps = lax.optimization_barrier((gain, maps))
    (coupled,) = local(enter, (entered, maps, values), ((lowers, share, rank), half))
    coupled = exchanged(coupled, near).reshape(width, rank)
    return pl.pallas_call(
        solve,
        in_specs=[VMEM] * 3,
        out_specs=pl.BlockSpec(memory_space=pl.ANY),
        out_shape=jax.ShapeDtypeStruct(applied.shape, half),
        scratch_shapes=[pltpu.VMEM(applied.shape, half), pltpu.SemaphoreType.DMA((PARTS,))],
        compiler_params=pltpu.CompilerParams(vmem_limit_bytes=16 * 2**20),
    )(gain, coupled, applied)


def solution(mesh):
    return jax.shard_map(
        body,
        mesh=mesh,
        in_specs=(
            P("layer", "row", None),
            P("layer", "row", None),
            P("row", None),
            P("row", None),
            P("row", None),
            P("row", "layer"),
            P(None, "layer"),
        ),
        out_specs=P("row", "layer"),
        check_vma=False,
    )
```

```python
import jax
import jax.numpy as jnp
from jax import lax
from jax.experimental import pallas as pl
from jax.experimental.pallas import tpu as pltpu
from jax.sharding import PartitionSpec as P


def shifted(value, axis, steps):
    count = lax.axis_size(axis)
    leading, last = (max(0, -steps), min(count, count - steps))
    return lax.ppermute(value, axis, [(source, source + steps) for source in range(leading, last)])


def rotated(value, axis, steps):
    count = lax.axis_size(axis)
    return lax.ppermute(value, axis, [(source, (source + steps) % count) for source in range(count)])


def project(basis, vectors):
    return lax.dot_general(
        basis, vectors, (((0,), (0,)), ((), ())), preferred_element_type=jnp.float32
    )


def product(a, b):
    return jnp.dot(a, b, preferred_element_type=jnp.float32)


SMEM = pl.BlockSpec(memory_space=pltpu.SMEM)
VMEM = pl.BlockSpec(memory_space=pltpu.VMEM)
PARTS = 4


def split(value):
    high = value.astype(jnp.bfloat16)
    return high, (value - high.astype(jnp.float32)).astype(jnp.bfloat16)


def wide(value, matrix):
    both = product(jnp.concatenate(split(value)), matrix)
    return both[: value.shape[0]] + both[value.shape[0] :]


def make_shift(next_ref, applied_ref, shift_ref):
    shift_ref[...] = project(next_ref[...], applied_ref[...]).T.astype(jnp.bfloat16)


def lay(*refs):
    rank = refs[0].shape[1]
    for layer, ref in enumerate(refs[:-1]):
        refs[-1][:, layer * rank : (layer + 1) * rank] = ref[...]


def make_maps(layers, *refs):
    cores = jnp.concatenate([ref[...] for ref in refs[:layers]], axis=0)
    left_ref, others_ref, weights_ref, shift_ref, sent_ref = refs[layers:]
    lefts = jnp.concatenate([left_ref[...], others_ref[...]], axis=1)
    map_t = wide(wide(weights_ref[...], lefts), cores).T.astype(jnp.bfloat16)
    rank = map_t.shape[0]
    share = sent_ref.shape[1] - rank
    for target in range(sent_ref.shape[0]):
        sent_ref[target, :rank] = map_t
        sent_ref[target, rank:] = shift_ref[target * share : (target + 1) * share]


def make_range(layers, *refs):
    cores = jnp.concatenate([ref[...] for ref in refs[:layers]], axis=0)
    left_ref, others_ref, range_ref = refs[layers:]
    lefts = jnp.concatenate([left_ref[...], others_ref[...]], axis=1)
    range_ref[...] = (-product(lefts, cores)).astype(jnp.bfloat16)


def chain(steps_ref, state, values_ref, swap):
    count, _, rank = steps_ref.shape
    for member in range(count):
        values_ref[member ^ swap] = state
        state = wide(state, steps_ref[member ^ swap, :rank])
        state = state + steps_ref[member ^ swap, rank:].astype(jnp.float32)
    return state


def first_half(upper_ref, steps_ref, entry_ref, values_ref, last_ref):
    @pl.when(upper_ref[0] == 0)
    def _():
        last_ref[...] = chain(steps_ref, entry_ref[...].T, values_ref, 0).astype(jnp.bfloat16)


def second_half(upper_ref, steps_ref, before_ref, values_ref, maps_ref):
    count, rank, _ = maps_ref.shape

    @pl.when(upper_ref[0] == 0)
    def _():
        maps_ref[...] = jnp.zeros(maps_ref.shape, jnp.bfloat16)

    @pl.when(upper_ref[0] > 0)
    def _():
        chain(steps_ref, jnp.zeros(values_ref.shape[1:], jnp.float32), values_ref, 1)
        rows = lax.broadcasted_iota(jnp.int32, (rank, rank), 0)
        cols = lax.broadcasted_iota(jnp.int32, (rank, rank), 1)
        maps_ref[1] = jnp.where(rows == cols, 1.0, 0.0).astype(jnp.bfloat16)
        state = steps_ref[1, :rank]
        for member in range(1, count):
            maps_ref[member ^ 1] = state
            if member + 1 < count:
                state = product(state, steps_ref[member ^ 1, :rank]).astype(jnp.bfloat16)


def enter(entered_ref, maps_ref, values_ref, coupled_ref):
    entered = entered_ref[...]
    for member in range(coupled_ref.shape[0]):
        moved = product(entered, maps_ref[member])
        coupled_ref[member] = (moved + values_ref[member]).astype(jnp.bfloat16)


def solve(gain_ref, coupled_ref, applied_ref, result_hbm, result, sent):
    rows = gain_ref.shape[0] // PARTS
    coupled = coupled_ref[...].T
    copies = []
    for part in range(PARTS):
        piece = pl.ds(part * rows, rows)
        moved = product(gain_ref[piece], coupled)
        applied = applied_ref[piece].astype(jnp.float32)
        result[piece] = (applied - moved).astype(jnp.bfloat16)
        copies.append(pltpu.make_async_copy(result.at[piece], result_hbm.at[piece], sent.at[part]))
        copies[-1].start()
    for copy in copies:
        copy.wait()


def local(kernel, inputs, *outputs, scalar=False, aliases={}):
    specs = [SMEM] * scalar + [VMEM] * (len(inputs) - scalar)
    return pl.pallas_call(
        kernel,
        in_specs=specs,
        out_specs=[VMEM] * len(outputs),
        out_shape=[jax.ShapeDtypeStruct(*output) for output in outputs],
        input_output_aliases=aliases,
        compiler_params=pltpu.CompilerParams(vmem_limit_bytes=16 * 2**20),
    )(*inputs)


def exchanged(blocks, members):
    return lax.all_to_all(blocks, "row", 0, 0, axis_index_groups=members, tiled=True)


def body(left_factors, right_factors, sketch, row_basis, inverse_diag, right_side, incoming):
    half = jnp.bfloat16
    order, rank = sketch.shape
    width = right_side.shape[1]
    layers, groups = lax.axis_size("layer"), lax.axis_size("row")
    lowers = groups // 2
    here = lax.axis_index("row")
    upper, lower = lax.div(here, lowers), lax.rem(here, lowers)
    share = width // lowers
    across = [lowers + (place ^ 1) for place in range(lowers)]
    near = [list(range(lowers)), across]

    lefts = [left_factors[0]] + [rotated(left_factors[0], "layer", k) for k in range(1, layers)]
    next_rows = shifted(row_basis, "row", -1)
    applied = product(inverse_diag, right_side).astype(half)
    sketch, applied = lax.optimization_barrier((sketch, applied))
    core = project(right_factors[0], sketch).astype(half)
    cores = [core] + [rotated(core, "layer", k) for k in range(1, layers)]

    (others,) = local(lay, lefts[1:], ((order, (layers - 1) * rank), half))
    next_rows, others = lax.optimization_barrier((next_rows, others))
    (shift_t,) = local(make_shift, (next_rows, applied), ((width, rank), half))
    weights = project(next_rows, inverse_diag)
    entry = lax.dynamic_slice_in_dim(incoming, lower * share, share, 1)
    place = upper.reshape(1)
    others, shift_t, weights, entry, place = lax.optimization_barrier(
        (others, shift_t, weights, entry, place)
    )
    (sent,) = local(
        lambda *refs: make_maps(layers, *refs),
        (*cores, lefts[0], others, weights, shift_t),
        ((lowers, rank + share, rank), half),
    )
    sent, others, entry, place = lax.optimization_barrier((sent, others, entry, place))
    steps = exchanged(sent, near)
    steps, others, entry, place = lax.optimization_barrier((steps, others, entry, place))
    values, last = local(
        first_half,
        (place, steps, entry),
        ((lowers, share, rank), jnp.float32),
        ((share, rank), half),
        scalar=True,
    )
    entered = lax.ppermute(last, "row", list(enumerate(across)))
    steps, others, _ = lax.optimization_barrier((steps, others, last))
    (tile_range,) = local(
        lambda *refs: make_range(layers, *refs),
        (*cores, lefts[0], others),
        ((order, rank), half),
    )
    gain = product(inverse_diag, tile_range).astype(half)
    values, maps = local(
        second_half,
        (place, steps, values),
        ((lowers, share, rank), jnp.float32),
        ((lowers, rank, rank), half),
        scalar=True,
        aliases={2: 0},
    )
    gain, maps = lax.optimization_barrier((gain, maps))
    (coupled,) = local(enter, (entered, maps, values), ((lowers, share, rank), half))
    coupled = exchanged(coupled, near).reshape(width, rank)
    return pl.pallas_call(
        solve,
        in_specs=[VMEM] * 3,
        out_specs=pl.BlockSpec(memory_space=pl.ANY),
        out_shape=jax.ShapeDtypeStruct(applied.shape, half),
        scratch_shapes=[pltpu.VMEM(applied.shape, half), pltpu.SemaphoreType.DMA((PARTS,))],
        compiler_params=pltpu.CompilerParams(vmem_limit_bytes=16 * 2**20),
    )(gain, coupled, applied)


def solution(mesh):
    return jax.shard_map(
        body,
        mesh=mesh,
        in_specs=(
            P("layer", "row", None),
            P("layer", "row", None),
            P("row", None),
            P("row", None),
            P("row", None),
            P("row", "layer"),
            P(None, "layer"),
        ),
        out_specs=P("row", "layer"),
        check_vma=False,
    )
```

```python
import jax
import jax.numpy as jnp
from jax import lax
from jax.experimental import pallas as pl
from jax.experimental.pallas import tpu as pltpu
from jax.sharding import PartitionSpec as P


def shifted(value, axis, steps):
    count = lax.axis_size(axis)
    leading, last = (max(0, -steps), min(count, count - steps))
    return lax.ppermute(value, axis, [(source, source + steps) for source in range(leading, last)])


def rotated(value, axis, steps):
    count = lax.axis_size(axis)
    return lax.ppermute(value, axis, [(source, (source + steps) % count) for source in range(count)])


def project(basis, vectors):
    return lax.dot_general(
        basis, vectors, (((0,), (0,)), ((), ())), preferred_element_type=jnp.float32
    )


def product(a, b):
    return jnp.dot(a, b, preferred_element_type=jnp.float32)


SMEM = pl.BlockSpec(memory_space=pltpu.SMEM)
VMEM = pl.BlockSpec(memory_space=pltpu.VMEM)
PARTS = 4


def split(value):
    high = value.astype(jnp.bfloat16)
    return high, (value - high.astype(jnp.float32)).astype(jnp.bfloat16)


def wide(value, matrix):
    both = product(jnp.concatenate(split(value)), matrix)
    return both[: value.shape[0]] + both[value.shape[0] :]


def lay(*refs):
    rank = refs[0].shape[1]
    for layer, ref in enumerate(refs[:-1]):
        refs[-1][:, layer * rank : (layer + 1) * rank] = ref[...]


def make_maps(layers, *refs):
    cores = jnp.concatenate([ref[...] for ref in refs[:layers]], axis=0)
    left_ref, others_ref, weights_ref, next_ref, applied_ref, range_ref, sent_ref = refs[layers:]
    lefts = jnp.concatenate([left_ref[...], others_ref[...]], axis=1)
    shift_t = project(next_ref[...], applied_ref[...]).T.astype(jnp.bfloat16)
    range_ref[...] = (-product(lefts, cores)).astype(jnp.bfloat16)
    map_t = wide(wide(weights_ref[...], lefts), cores).T.astype(jnp.bfloat16)
    rank = map_t.shape[0]
    share = sent_ref.shape[1] - rank
    for target in range(sent_ref.shape[0]):
        sent_ref[target, :rank] = map_t
        sent_ref[target, rank:] = shift_t[target * share : (target + 1) * share]


def chain(steps_ref, state, values_ref, swap):
    count, _, rank = steps_ref.shape
    for member in range(count):
        values_ref[member ^ swap] = state
        state = wide(state, steps_ref[member ^ swap, :rank])
        state = state + steps_ref[member ^ swap, rank:].astype(jnp.float32)
    return state


def first_half(upper_ref, steps_ref, entry_ref, values_ref, last_ref):
    @pl.when(upper_ref[0] == 0)
    def _():
        last_ref[...] = chain(steps_ref, entry_ref[...].T, values_ref, 0).astype(jnp.bfloat16)


def second_half(upper_ref, steps_ref, before_ref, values_ref, maps_ref):
    count, rank, _ = maps_ref.shape

    @pl.when(upper_ref[0] == 0)
    def _():
        maps_ref[...] = jnp.zeros(maps_ref.shape, jnp.bfloat16)

    @pl.when(upper_ref[0] > 0)
    def _():
        chain(steps_ref, jnp.zeros(values_ref.shape[1:], jnp.float32), values_ref, 1)
        rows = lax.broadcasted_iota(jnp.int32, (rank, rank), 0)
        cols = lax.broadcasted_iota(jnp.int32, (rank, rank), 1)
        maps_ref[1] = jnp.where(rows == cols, 1.0, 0.0).astype(jnp.bfloat16)
        state = steps_ref[1, :rank]
        for member in range(1, count):
            maps_ref[member ^ 1] = state
            if member + 1 < count:
                state = product(state, steps_ref[member ^ 1, :rank]).astype(jnp.bfloat16)


def enter(entered_ref, maps_ref, values_ref, coupled_ref):
    entered = entered_ref[...]
    for member in range(coupled_ref.shape[0]):
        moved = product(entered, maps_ref[member])
        coupled_ref[member] = (moved + values_ref[member]).astype(jnp.bfloat16)


def solve(gain_ref, coupled_ref, applied_ref, result_hbm, result, sent):
    rows = gain_ref.shape[0] // PARTS
    coupled = coupled_ref[...].T
    copies = []
    for part in range(PARTS):
        piece = pl.ds(part * rows, rows)
        moved = product(gain_ref[piece], coupled)
        applied = applied_ref[piece].astype(jnp.float32)
        result[piece] = (applied - moved).astype(jnp.bfloat16)
        copies.append(pltpu.make_async_copy(result.at[piece], result_hbm.at[piece], sent.at[part]))
        copies[-1].start()
    for copy in copies:
        copy.wait()


def local(kernel, inputs, *outputs, scalar=False, aliases={}):
    specs = [SMEM] * scalar + [VMEM] * (len(inputs) - scalar)
    return pl.pallas_call(
        kernel,
        in_specs=specs,
        out_specs=[VMEM] * len(outputs),
        out_shape=[jax.ShapeDtypeStruct(*output) for output in outputs],
        input_output_aliases=aliases,
        compiler_params=pltpu.CompilerParams(vmem_limit_bytes=16 * 2**20),
    )(*inputs)


def exchanged(blocks, members):
    return lax.all_to_all(blocks, "row", 0, 0, axis_index_groups=members, tiled=True)


def body(left_factors, right_factors, sketch, row_basis, inverse_diag, right_side, incoming):
    half = jnp.bfloat16
    order, rank = sketch.shape
    width = right_side.shape[1]
    layers, groups = lax.axis_size("layer"), lax.axis_size("row")
    lowers = groups // 2
    here = lax.axis_index("row")
    upper, lower = lax.div(here, lowers), lax.rem(here, lowers)
    share = width // lowers
    across = [lowers + (place ^ 1) for place in range(lowers)]
    near = [list(range(lowers)), across]

    lefts = [left_factors[0]] + [rotated(left_factors[0], "layer", k) for k in range(1, layers)]
    next_rows = shifted(row_basis, "row", -1)
    applied = product(inverse_diag, right_side).astype(half)
    sketch, applied = lax.optimization_barrier((sketch, applied))
    core = project(right_factors[0], sketch).astype(half)
    cores = [core] + [rotated(core, "layer", k) for k in range(1, layers)]

    (others,) = local(lay, lefts[1:], ((order, (layers - 1) * rank), half))
    next_rows, others = lax.optimization_barrier((next_rows, others))
    weights = project(next_rows, inverse_diag)
    entry = lax.dynamic_slice_in_dim(incoming, lower * share, share, 1)
    place = upper.reshape(1)
    weights, entry, place = lax.optimization_barrier((weights, entry, place))
    tile_range, sent = local(
        lambda *refs: make_maps(layers, *refs),
        (*cores, lefts[0], others, weights, next_rows, applied),
        ((order, rank), half),
        ((lowers, rank + share, rank), half),
    )
    sent, tile_range, entry, place = lax.optimization_barrier((sent, tile_range, entry, place))
    steps = exchanged(sent, near)
    steps, tile_range, entry, place = lax.optimization_barrier((steps, tile_range, entry, place))
    values, last = local(
        first_half,
        (place, steps, entry),
        ((lowers, share, rank), jnp.float32),
        ((share, rank), half),
        scalar=True,
    )
    entered = lax.ppermute(last, "row", list(enumerate(across)))
    steps, tile_range, _ = lax.optimization_barrier((steps, tile_range, last))
    gain = product(inverse_diag, tile_range).astype(half)
    values, maps = local(
        second_half,
        (place, steps, values),
        ((lowers, share, rank), jnp.float32),
        ((lowers, rank, rank), half),
        scalar=True,
        aliases={2: 0},
    )
    gain, maps = lax.optimization_barrier((gain, maps))
    (coupled,) = local(enter, (entered, maps, values), ((lowers, share, rank), half))
    coupled = exchanged(coupled, near).reshape(width, rank)
    return pl.pallas_call(
        solve,
        in_specs=[VMEM] * 3,
        out_specs=pl.BlockSpec(memory_space=pl.ANY),
        out_shape=jax.ShapeDtypeStruct(applied.shape, half),
        scratch_shapes=[pltpu.VMEM(applied.shape, half), pltpu.SemaphoreType.DMA((PARTS,))],
        compiler_params=pltpu.CompilerParams(vmem_limit_bytes=16 * 2**20),
    )(gain, coupled, applied)


def solution(mesh):
    return jax.shard_map(
        body,
        mesh=mesh,
        in_specs=(
            P("layer", "row", None),
            P("layer", "row", None),
            P("row", None),
            P("row", None),
            P("row", None),
            P("row", "layer"),
            P(None, "layer"),
        ),
        out_specs=P("row", "layer"),
        check_vma=False,
    )
```

```python
import jax
import jax.numpy as jnp
from jax import lax
from jax.experimental import pallas as pl
from jax.experimental.pallas import tpu as pltpu
from jax.sharding import PartitionSpec as P


def shifted(value, axis, steps):
    count = lax.axis_size(axis)
    leading, last = (max(0, -steps), min(count, count - steps))
    return lax.ppermute(value, axis, [(source, source + steps) for source in range(leading, last)])


def rotated(value, axis, steps):
    count = lax.axis_size(axis)
    return lax.ppermute(value, axis, [(source, (source + steps) % count) for source in range(count)])


def project(basis, vectors):
    return lax.dot_general(
        basis, vectors, (((0,), (0,)), ((), ())), preferred_element_type=jnp.float32
    )


def product(a, b):
    return jnp.dot(a, b, preferred_element_type=jnp.float32)


SMEM = pl.BlockSpec(memory_space=pltpu.SMEM)
VMEM = pl.BlockSpec(memory_space=pltpu.VMEM)
PARTS = 4


def split(value):
    high = value.astype(jnp.bfloat16)
    return high, (value - high.astype(jnp.float32)).astype(jnp.bfloat16)


def wide(value, matrix, twice=False):
    parts = jnp.concatenate(split(value))
    both = product(jnp.concatenate([parts, parts], axis=1) if twice else parts, matrix)
    return both[: value.shape[0]] + both[value.shape[0] :]


def make_shift(next_ref, applied_ref, shift_ref):
    shift_ref[...] = project(next_ref[...], applied_ref[...]).T.astype(jnp.bfloat16)


def lay(*refs):
    rank = refs[0].shape[1]
    for layer, ref in enumerate(refs[:-1]):
        refs[-1][:, layer * rank : (layer + 1) * rank] = ref[...]


def make_maps(layers, *refs):
    cores = jnp.concatenate([ref[...] for ref in refs[:layers]], axis=0)
    left_ref, others_ref, weights_ref, shift_ref, sent_ref = refs[layers:]
    lefts = jnp.concatenate([left_ref[...], others_ref[...]], axis=1)
    map_t = wide(wide(weights_ref[...], lefts), cores).T.astype(jnp.bfloat16)
    rank = map_t.shape[0]
    share = sent_ref.shape[1] - rank
    for target in range(sent_ref.shape[0]):
        sent_ref[target, :rank] = map_t
        sent_ref[target, rank:] = shift_ref[target * share : (target + 1) * share]


def make_range(layers, *refs):
    cores = jnp.concatenate([ref[...] for ref in refs[:layers]], axis=0)
    left_ref, others_ref, range_ref = refs[layers:]
    lefts = jnp.concatenate([left_ref[...], others_ref[...]], axis=1)
    range_ref[...] = (-product(lefts, cores)).astype(jnp.bfloat16)


def chain(steps_ref, state, values_ref, swap):
    count, _, rank = steps_ref.shape
    for member in range(count):
        values_ref[member ^ swap] = state
        state = wide(state, steps_ref[member ^ swap, :rank])
        state = state + steps_ref[member ^ swap, rank:].astype(jnp.float32)
    return state


def first_half(upper_ref, steps_ref, entry_ref, values_ref, last_ref):
    @pl.when(upper_ref[0] == 0)
    def _():
        count, _, rank = steps_ref.shape
        pairs = [product(steps_ref[k], steps_ref[k + 1, :rank]) for k in range(0, count, 2)]
        state = entry_ref[...].T
        for member, pair in zip(range(0, count, 2), pairs):
            values_ref[member] = state
            shift = steps_ref[member, rank:].astype(jnp.float32)
            values_ref[member + 1] = wide(state, steps_ref[member, :rank]) + shift
            moved = wide(state, jnp.concatenate(split(pair[:rank])), True)
            state = moved + pair[rank:] + steps_ref[member + 1, rank:].astype(jnp.float32)
        last_ref[...] = state.astype(jnp.bfloat16)


def second_half(upper_ref, steps_ref, before_ref, values_ref, maps_ref):
    count, rank, _ = maps_ref.shape

    @pl.when(upper_ref[0] == 0)
    def _():
        maps_ref[...] = jnp.zeros(maps_ref.shape, jnp.bfloat16)

    @pl.when(upper_ref[0] > 0)
    def _():
        chain(steps_ref, jnp.zeros(values_ref.shape[1:], jnp.float32), values_ref, 1)
        rows = lax.broadcasted_iota(jnp.int32, (rank, rank), 0)
        cols = lax.broadcasted_iota(jnp.int32, (rank, rank), 1)
        maps_ref[1] = jnp.where(rows == cols, 1.0, 0.0).astype(jnp.bfloat16)
        state = steps_ref[1, :rank]
        for member in range(1, count):
            maps_ref[member ^ 1] = state
            if member + 1 < count:
                state = product(state, steps_ref[member ^ 1, :rank]).astype(jnp.bfloat16)


def enter(entered_ref, maps_ref, values_ref, coupled_ref):
    entered = entered_ref[...]
    for member in range(coupled_ref.shape[0]):
        moved = product(entered, maps_ref[member])
        coupled_ref[member] = (moved + values_ref[member]).astype(jnp.bfloat16)


def solve(gain_ref, coupled_ref, applied_ref, result_hbm, result, sent):
    rows = gain_ref.shape[0] // PARTS
    coupled = coupled_ref[...].T
    copies = []
    for part in range(PARTS):
        piece = pl.ds(part * rows, rows)
        moved = product(gain_ref[piece], coupled)
        applied = applied_ref[piece].astype(jnp.float32)
        result[piece] = (applied - moved).astype(jnp.bfloat16)
        copies.append(pltpu.make_async_copy(result.at[piece], result_hbm.at[piece], sent.at[part]))
        copies[-1].start()
    for copy in copies:
        copy.wait()


def local(kernel, inputs, *outputs, scalar=False, aliases={}):
    specs = [SMEM] * scalar + [VMEM] * (len(inputs) - scalar)
    return pl.pallas_call(
        kernel,
        in_specs=specs,
        out_specs=[VMEM] * len(outputs),
        out_shape=[jax.ShapeDtypeStruct(*output) for output in outputs],
        input_output_aliases=aliases,
        compiler_params=pltpu.CompilerParams(vmem_limit_bytes=16 * 2**20),
    )(*inputs)


def exchanged(blocks, members):
    return lax.all_to_all(blocks, "row", 0, 0, axis_index_groups=members, tiled=True)


def body(left_factors, right_factors, sketch, row_basis, inverse_diag, right_side, incoming):
    half = jnp.bfloat16
    order, rank = sketch.shape
    width = right_side.shape[1]
    layers, groups = lax.axis_size("layer"), lax.axis_size("row")
    lowers = groups // 2
    here = lax.axis_index("row")
    upper, lower = lax.div(here, lowers), lax.rem(here, lowers)
    share = width // lowers
    across = [lowers + (place ^ 1) for place in range(lowers)]
    near = [list(range(lowers)), across]

    lefts = [left_factors[0]] + [rotated(left_factors[0], "layer", k) for k in range(1, layers)]
    next_rows = shifted(row_basis, "row", -1)
    applied = product(inverse_diag, right_side).astype(half)
    sketch, applied = lax.optimization_barrier((sketch, applied))
    core = project(right_factors[0], sketch).astype(half)
    cores = [core] + [rotated(core, "layer", k) for k in range(1, layers)]

    (others,) = local(lay, lefts[1:], ((order, (layers - 1) * rank), half))
    next_rows, others = lax.optimization_barrier((next_rows, others))
    (shift_t,) = local(make_shift, (next_rows, applied), ((width, rank), half))
    weights = project(next_rows, inverse_diag)
    entry = lax.dynamic_slice_in_dim(incoming, lower * share, share, 1)
    place = upper.reshape(1)
    others, shift_t, weights, entry, place = lax.optimization_barrier(
        (others, shift_t, weights, entry, place)
    )
    (sent,) = local(
        lambda *refs: make_maps(layers, *refs),
        (*cores, lefts[0], others, weights, shift_t),
        ((lowers, rank + share, rank), half),
    )
    sent, others, entry, place = lax.optimization_barrier((sent, others, entry, place))
    steps = exchanged(sent, near)
    steps, others, entry, place = lax.optimization_barrier((steps, others, entry, place))
    values, last = local(
        first_half,
        (place, steps, entry),
        ((lowers, share, rank), jnp.float32),
        ((share, rank), half),
        scalar=True,
    )
    entered = lax.ppermute(last, "row", list(enumerate(across)))
    steps, others, _ = lax.optimization_barrier((steps, others, last))
    (tile_range,) = local(
        lambda *refs: make_range(layers, *refs),
        (*cores, lefts[0], others),
        ((order, rank), half),
    )
    gain = product(inverse_diag, tile_range).astype(half)
    values, maps = local(
        second_half,
        (place, steps, values),
        ((lowers, share, rank), jnp.float32),
        ((lowers, rank, rank), half),
        scalar=True,
        aliases={2: 0},
    )
    gain, maps = lax.optimization_barrier((gain, maps))
    (coupled,) = local(enter, (entered, maps, values), ((lowers, share, rank), half))
    coupled = exchanged(coupled, near).reshape(width, rank)
    return pl.pallas_call(
        solve,
        in_specs=[VMEM] * 3,
        out_specs=pl.BlockSpec(memory_space=pl.ANY),
        out_shape=jax.ShapeDtypeStruct(applied.shape, half),
        scratch_shapes=[pltpu.VMEM(applied.shape, half), pltpu.SemaphoreType.DMA((PARTS,))],
        compiler_params=pltpu.CompilerParams(vmem_limit_bytes=16 * 2**20),
    )(gain, coupled, applied)


def solution(mesh):
    return jax.shard_map(
        body,
        mesh=mesh,
        in_specs=(
            P("layer", "row", None),
            P("layer", "row", None),
            P("row", None),
            P("row", None),
            P("row", None),
            P("row", "layer"),
            P(None, "layer"),
        ),
        out_specs=P("row", "layer"),
        check_vma=False,
    )
```

```python
import jax
import jax.numpy as jnp
from jax import lax
from jax.experimental import pallas as pl
from jax.experimental.pallas import tpu as pltpu
from jax.sharding import PartitionSpec as P


def shifted(value, axis, steps):
    count = lax.axis_size(axis)
    leading, last = (max(0, -steps), min(count, count - steps))
    return lax.ppermute(value, axis, [(source, source + steps) for source in range(leading, last)])


def rotated(value, axis, steps):
    count = lax.axis_size(axis)
    return lax.ppermute(value, axis, [(source, (source + steps) % count) for source in range(count)])


def project(basis, vectors):
    return lax.dot_general(
        basis, vectors, (((0,), (0,)), ((), ())), preferred_element_type=jnp.float32
    )


def product(a, b):
    return jnp.dot(a, b, preferred_element_type=jnp.float32)


SMEM = pl.BlockSpec(memory_space=pltpu.SMEM)
VMEM = pl.BlockSpec(memory_space=pltpu.VMEM)
PARTS = 2


def split(value):
    high = value.astype(jnp.bfloat16)
    return high, (value - high.astype(jnp.float32)).astype(jnp.bfloat16)


def wide(value, matrix):
    both = product(jnp.concatenate(split(value)), matrix)
    return both[: value.shape[0]] + both[value.shape[0] :]


def make_shift(next_ref, applied_ref, shift_ref):
    shift_ref[...] = project(next_ref[...], applied_ref[...]).T.astype(jnp.bfloat16)


def lay(*refs):
    rank = refs[0].shape[1]
    for layer, ref in enumerate(refs[:-1]):
        refs[-1][:, layer * rank : (layer + 1) * rank] = ref[...]


def make_maps(layers, *refs):
    cores = jnp.concatenate([ref[...] for ref in refs[:layers]], axis=0)
    left_ref, others_ref, weights_ref, shift_ref, sent_ref = refs[layers:]
    lefts = jnp.concatenate([left_ref[...], others_ref[...]], axis=1)
    map_t = wide(wide(weights_ref[...], lefts), cores).T.astype(jnp.bfloat16)
    rank = map_t.shape[0]
    share = sent_ref.shape[1] - rank
    for target in range(sent_ref.shape[0]):
        sent_ref[target, :rank] = map_t
        sent_ref[target, rank:] = shift_ref[target * share : (target + 1) * share]


def make_range(layers, *refs):
    cores = jnp.concatenate([ref[...] for ref in refs[:layers]], axis=0)
    left_ref, others_ref, range_ref = refs[layers:]
    lefts = jnp.concatenate([left_ref[...], others_ref[...]], axis=1)
    range_ref[...] = (-product(lefts, cores)).astype(jnp.bfloat16)


def chain(steps_ref, state, values_ref, swap):
    count, _, rank = steps_ref.shape
    for member in range(count):
        values_ref[member ^ swap] = state
        state = wide(state, steps_ref[member ^ swap, :rank])
        state = state + steps_ref[member ^ swap, rank:].astype(jnp.float32)
    return state


def first_half(upper_ref, steps_ref, entry_ref, values_ref, last_ref):
    @pl.when(upper_ref[0] == 0)
    def _():
        last_ref[...] = chain(steps_ref, entry_ref[...].T, values_ref, 0).astype(jnp.bfloat16)


def second_half(upper_ref, steps_ref, before_ref, values_ref, maps_ref):
    count, rank, _ = maps_ref.shape

    @pl.when(upper_ref[0] == 0)
    def _():
        maps_ref[...] = jnp.zeros(maps_ref.shape, jnp.bfloat16)

    @pl.when(upper_ref[0] > 0)
    def _():
        chain(steps_ref, jnp.zeros(values_ref.shape[1:], jnp.float32), values_ref, 1)
        rows = lax.broadcasted_iota(jnp.int32, (rank, rank), 0)
        cols = lax.broadcasted_iota(jnp.int32, (rank, rank), 1)
        maps_ref[1] = jnp.where(rows == cols, 1.0, 0.0).astype(jnp.bfloat16)
        state = steps_ref[1, :rank]
        for member in range(1, count):
            maps_ref[member ^ 1] = state
            if member + 1 < count:
                state = product(state, steps_ref[member ^ 1, :rank]).astype(jnp.bfloat16)


def enter(entered_ref, maps_ref, values_ref, coupled_ref):
    entered = entered_ref[...]
    for member in range(coupled_ref.shape[0]):
        moved = product(entered, maps_ref[member])
        coupled_ref[member] = (moved + values_ref[member]).astype(jnp.bfloat16)


def solve(gain_ref, coupled_ref, applied_ref, result_hbm, result, sent):
    rows = gain_ref.shape[0] // PARTS
    coupled = coupled_ref[...].T
    copies = []
    for part in range(PARTS):
        piece = pl.ds(part * rows, rows)
        moved = product(gain_ref[piece], coupled)
        applied = applied_ref[piece].astype(jnp.float32)
        result[piece] = (applied - moved).astype(jnp.bfloat16)
        copies.append(pltpu.make_async_copy(result.at[piece], result_hbm.at[piece], sent.at[part]))
        copies[-1].start()
    for copy in copies:
        copy.wait()


def local(kernel, inputs, *outputs, scalar=False, aliases={}):
    specs = [SMEM] * scalar + [VMEM] * (len(inputs) - scalar)
    return pl.pallas_call(
        kernel,
        in_specs=specs,
        out_specs=[VMEM] * len(outputs),
        out_shape=[jax.ShapeDtypeStruct(*output) for output in outputs],
        input_output_aliases=aliases,
        compiler_params=pltpu.CompilerParams(vmem_limit_bytes=16 * 2**20),
    )(*inputs)


def exchanged(blocks, members):
    return lax.all_to_all(blocks, "row", 0, 0, axis_index_groups=members, tiled=True)


def body(left_factors, right_factors, sketch, row_basis, inverse_diag, right_side, incoming):
    half = jnp.bfloat16
    order, rank = sketch.shape
    width = right_side.shape[1]
    layers, groups = lax.axis_size("layer"), lax.axis_size("row")
    lowers = groups // 2
    here = lax.axis_index("row")
    upper, lower = lax.div(here, lowers), lax.rem(here, lowers)
    share = width // lowers
    across = [lowers + (place ^ 1) for place in range(lowers)]
    near = [list(range(lowers)), across]

    lefts = [left_factors[0]] + [rotated(left_factors[0], "layer", k) for k in range(1, layers)]
    next_rows = shifted(row_basis, "row", -1)
    applied = product(inverse_diag, right_side).astype(half)
    sketch, applied = lax.optimization_barrier((sketch, applied))
    core = project(right_factors[0], sketch).astype(half)
    cores = [core] + [rotated(core, "layer", k) for k in range(1, layers)]

    (others,) = local(lay, lefts[1:], ((order, (layers - 1) * rank), half))
    next_rows, others = lax.optimization_barrier((next_rows, others))
    (shift_t,) = local(make_shift, (next_rows, applied), ((width, rank), half))
    weights = project(next_rows, inverse_diag)
    entry = lax.dynamic_slice_in_dim(incoming, lower * share, share, 1)
    place = upper.reshape(1)
    others, shift_t, weights, entry, place = lax.optimization_barrier(
        (others, shift_t, weights, entry, place)
    )
    (sent,) = local(
        lambda *refs: make_maps(layers, *refs),
        (*cores, lefts[0], others, weights, shift_t),
        ((lowers, rank + share, rank), half),
    )
    sent, others, entry, place = lax.optimization_barrier((sent, others, entry, place))
    steps = exchanged(sent, near)
    steps, others, entry, place = lax.optimization_barrier((steps, others, entry, place))
    values, last = local(
        first_half,
        (place, steps, entry),
        ((lowers, share, rank), jnp.float32),
        ((share, rank), half),
        scalar=True,
    )
    entered = lax.ppermute(last, "row", list(enumerate(across)))
    steps, others, _ = lax.optimization_barrier((steps, others, last))
    (tile_range,) = local(
        lambda *refs: make_range(layers, *refs),
        (*cores, lefts[0], others),
        ((order, rank), half),
    )
    gain = product(inverse_diag, tile_range).astype(half)
    values, maps = local(
        second_half,
        (place, steps, values),
        ((lowers, share, rank), jnp.float32),
        ((lowers, rank, rank), half),
        scalar=True,
        aliases={2: 0},
    )
    gain, maps = lax.optimization_barrier((gain, maps))
    (coupled,) = local(enter, (entered, maps, values), ((lowers, share, rank), half))
    coupled = exchanged(coupled, near).reshape(width, rank)
    return pl.pallas_call(
        solve,
        in_specs=[VMEM] * 3,
        out_specs=pl.BlockSpec(memory_space=pl.ANY),
        out_shape=jax.ShapeDtypeStruct(applied.shape, half),
        scratch_shapes=[pltpu.VMEM(applied.shape, half), pltpu.SemaphoreType.DMA((PARTS,))],
        compiler_params=pltpu.CompilerParams(vmem_limit_bytes=16 * 2**20),
    )(gain, coupled, applied)


def solution(mesh):
    return jax.shard_map(
        body,
        mesh=mesh,
        in_specs=(
            P("layer", "row", None),
            P("layer", "row", None),
            P("row", None),
            P("row", None),
            P("row", None),
            P("row", "layer"),
            P(None, "layer"),
        ),
        out_specs=P("row", "layer"),
        check_vma=False,
    )
```
